512 devices in a mesh: dom: 64 (over z, y), rep: 8 (over x, core).
Axes of the slice: x: 4, y: 4, z: 16, core: 2. Of those that a mesh axis runs over, the one named last changes fastest.
Arguments:
- feats: bfloat16 [49152, 512], P('dom'), may hold values from -6 to 6
- halo_index: int32 [64, 64, 8], P('dom'), may hold values from 8 to 767
- seed_ids: int32 [262144], P(('dom', 'rep')), may hold values from 0 to 767, as said below
- tiles: bfloat16 [7168, 128, 128], P(('dom', 'rep')), may hold values from -1.25 to 1.25
- tile_dst: int32 [512, 14], P(('dom', 'rep')), may hold values from 0 to 3, as said below
- tile_src: int32 [512, 14], P(('dom', 'rep')), may hold values from 0 to 13
- tile_count: int32 [512], P(('dom', 'rep')), may hold values from 2 to 14, as said below
- w_self: bfloat16 [512, 512], replicated, may hold values from -0.25 to 0.25
- w_neigh: bfloat16 [512, 512], replicated, may hold values from -0.25 to 0.25
- bias: bfloat16 [512], replicated, may hold values from -3 to 3
- cotangent: bfloat16 [262144, 512], P(('dom', 'rep')), may hold values from -6 to 6
Outputs:
- out: bfloat16 [262144, 512], P(('dom', 'rep'))
- input_grad: float32 [49152, 512], P(('dom', 'rep'))
- grad_self: bfloat16 [512, 512], replicated
- grad_neigh: bfloat16 [512, 512], replicated
- grad_bias: float32 [512], replicated
The draws below stay inside these ranges and needn't reach their ends.
Inputs may be any that keep to these rules, and one draw needn't show every extreme that they name: `halo_index`: halo lists never name a hub row, that is a row under 8. `seed_ids`: the 512 ids of one device are distinct. `tile_dst`: the 14 slots of one device name distinct (seed block, source block) pairs. `tile_count`: some device uses all 14 slots in every draw.
All inputs are finite; a program needn't handle non-finite values.
Results may differ from the reference program's by a relative error of at most 0.007.
Values may be sent and summed in bfloat16 or wider, within the bound.
No kernel may reach another device: no remote copies, remote signals or barrier semaphores. Data moves between devices by JAX's collectives and lax.ppermute only.
A program may use at most 64 MiB of HBM per device.

```python
import jax
import jax.numpy as jnp
from jax import lax

H = 512
BLK = 128
SLOTS = 8
HUB_DEV = 8
V_DEV = 768
SEED_DEV = 512
TILES = 14
DEVS = 512
VERTS = 49152
SEEDS = 262144
SRC_BLOCKS = 14
DST_BLOCKS = 4
N_DOM = 64
N_REP = 8


def tile_pairs(key):
    keys = jax.random.split(key, DEVS)
    orders = jax.vmap(lambda single: jax.random.permutation(single, SRC_BLOCKS * DST_BLOCKS)[:TILES])(keys)
    return orders.astype(jnp.int32)


def draw_tile_dst(key, part):
    return tile_pairs(key) // SRC_BLOCKS


def draw_tile_src(key, part):
    return tile_pairs(key) % SRC_BLOCKS


def draw_tile_count(key, part):
    key = jax.random.fold_in(key, 5)
    first, second = jax.random.split(key)
    counts = jax.random.randint(first, (DEVS,), 2, TILES // 2 + 1).astype(jnp.int32)
    fullest = jax.random.randint(second, (), 0, DEVS)
    return counts.at[fullest].set(TILES).astype(jnp.int32)


def draw_seed_ids(key, part):
    key = jax.random.fold_in(key, 7)
    keys = jax.random.split(key, DEVS)
    chosen = jax.vmap(lambda single: jax.random.permutation(single, V_DEV)[:SEED_DEV])(keys)
    return chosen.reshape(DEVS * SEED_DEV).astype(jnp.int32)


def with_ends(result, key, smallest, largest):
    dims = result.shape
    spot = [jax.random.randint(jax.random.fold_in(key, axis), (), 0, dims[axis]) for axis in range(len(dims))]
    result = result.at[tuple(spot)].set(smallest)
    longest = dims.index(max(dims))
    spot[longest] = (spot[longest] + 1) % dims[longest]
    return result.at[tuple(spot)].set(largest)


def level_of(stream_key, shape, shards, least, top_value):
    def one(axis_at, shards_of):
        draws = jax.random.uniform(jax.random.fold_in(jax.random.fold_in(stream_key, 6), axis_at), (shards_of,), jnp.float32, least / len(shards), top_value / len(shards))
        return jnp.repeat(jnp.exp(draws), shape[axis_at] // shards_of).reshape((-1,) + (1,) * (len(shape) - axis_at - 1))

    gain = one(*shards[0])
    for cut in shards[1:]:
        gain = gain * one(*cut)
    return gain


def bell_draw(key, dims, deviation, reach, shards=(), kind=jnp.bfloat16):
    drawn = deviation * jax.random.normal(key, dims, jnp.float32)
    if shards:
        drawn = drawn * level_of(key, dims, shards, -0.22, 0.18)
    return jnp.clip(drawn, -reach, reach).astype(kind)


def setup_inputs(seed: int = 0) -> dict:
    splits = jax.random.split(jax.random.key(seed), 12)
    feats = bell_draw(splits[0], (VERTS, H), 1.0, 6.0, ((0, 64),))
    halo_index = with_ends(jax.random.randint(splits[1], (N_DOM, N_DOM, SLOTS), HUB_DEV, V_DEV), jax.random.fold_in(splits[1], 1), HUB_DEV, V_DEV - 1).astype(jnp.int32)
    seed_ids = draw_seed_ids(jax.random.fold_in(splits[11], 71), 0)
    tiles = bell_draw(splits[3], (DEVS * TILES, BLK, BLK), (BLK ** -0.5), 1.25, ((0, 512),))
    tile_dst = draw_tile_dst(jax.random.fold_in(splits[11], 71), 0)
    tile_src = draw_tile_src(jax.random.fold_in(splits[11], 71), 0)
    tile_count = draw_tile_count(jax.random.fold_in(splits[11], 71), 0)
    w_self = bell_draw(splits[7], (H, H), H ** -0.5, 0.25)
    w_neigh = bell_draw(splits[8], (H, H), H ** -0.5, 0.25)
    bias = bell_draw(splits[9], (H,), 0.5, 3.0)
    cotangent = bell_draw(splits[10], (SEEDS, H), 1.0, 6.0, ((0, 512),))
    return dict(feats=feats, halo_index=halo_index, seed_ids=seed_ids, tiles=tiles, tile_dst=tile_dst, tile_src=tile_src, tile_count=tile_count, w_self=w_self, w_neigh=w_neigh, bias=bias, cotangent=cotangent)


def reference(feats, halo_index, seed_ids, tiles, tile_dst, tile_src, tile_count, w_self, w_neigh, bias, cotangent):
    blocked = feats.reshape(N_DOM, V_DEV, H)
    hub_table = blocked[:, :HUB_DEV].reshape(N_DOM * HUB_DEV, H)
    owners = jnp.arange(N_DOM, dtype=jnp.int32)
    halo_table = blocked[owners[:, None, None], halo_index]
    dev_total = N_DOM * N_REP
    grad_scale = float(SEED_DEV * dev_total) ** -0.5
    src_total = (V_DEV + N_DOM * SLOTS + N_DOM * HUB_DEV) // BLK
    dst_total = SEED_DEV // BLK
    slot_ids = jnp.arange(TILES, dtype=jnp.int32)
    highest = lax.Precision.HIGHEST

    def one_device(carry, inputs):
        row_grad, g_self, g_neigh, g_bias = carry
        index, dev_tiles, dev_dst, dev_src, dev_count, dev_seeds, dev_cot = inputs
        part_id = index // N_REP
        own_rows = blocked[part_id]
        halo_rows = halo_table[:, part_id].reshape(N_DOM * SLOTS, H)
        source = jnp.concatenate([own_rows, halo_rows, hub_table], 0)
        blocks = source.reshape(src_total, BLK, H).astype(jnp.float32)
        live_mask = (slot_ids < dev_count).astype(jnp.float32)
        tiles_wide = dev_tiles.astype(jnp.float32)
        products = jnp.einsum("tij,tjh->tih", tiles_wide, blocks[dev_src], precision=highest)
        dst_onehot = (dev_dst[None, :] == jnp.arange(dst_total, dtype=jnp.int32)[:, None]).astype(jnp.float32) * live_mask[None, :]
        aggregate = jnp.einsum("bt,tih->bih", dst_onehot, products, precision=highest)
        aggregate = aggregate.reshape(SEED_DEV, H).astype(jnp.bfloat16)
        chosen = own_rows[dev_seeds]
        preact = jnp.dot(chosen, w_self, preferred_element_type=jnp.float32)
        preact = preact + jnp.dot(aggregate, w_neigh, preferred_element_type=jnp.float32)
        preact = preact + bias.astype(jnp.float32)
        sigmoid_v = jax.nn.sigmoid(preact)
        output = (preact * sigmoid_v).astype(jnp.bfloat16)
        d_pre = (dev_cot.astype(jnp.float32) * sigmoid_v * (1.0 + preact * (1.0 - sigmoid_v))).astype(jnp.bfloat16)
        g_self = g_self + jnp.dot(chosen.T, d_pre, preferred_element_type=jnp.float32)
        g_neigh = g_neigh + jnp.dot(aggregate.T, d_pre, preferred_element_type=jnp.float32)
        g_bias = g_bias + jnp.sum(d_pre.astype(jnp.float32), 0)
        d_seed = jnp.dot(d_pre, w_self.T, preferred_element_type=jnp.float32)
        d_agg = jnp.dot(d_pre, w_neigh.T, preferred_element_type=jnp.float32).astype(jnp.bfloat16)
        picked = d_agg.reshape(dst_total, BLK, H).astype(jnp.float32)[dev_dst]
        back = jnp.einsum("tij,tih->tjh", tiles_wide, picked, precision=highest)
        src_onehot = (dev_src[None, :] == jnp.arange(src_total, dtype=jnp.int32)[:, None]).astype(jnp.float32) * live_mask[None, :]
        d_source = jnp.einsum("st,tjh->sjh", src_onehot, back, precision=highest).reshape(src_total * BLK, H)
        own_grad = d_source[:V_DEV].at[dev_seeds].add(d_seed)
        halo_grad = d_source[V_DEV:V_DEV + N_DOM * SLOTS].reshape(N_DOM, SLOTS, H)
        hub_grad = d_source[V_DEV + N_DOM * SLOTS:].reshape(N_DOM, HUB_DEV, H)
        row_grad = row_grad.at[part_id].add(own_grad)
        row_grad = row_grad.at[owners[:, None], halo_index[:, part_id]].add(halo_grad)
        row_grad = row_grad.at[:, :HUB_DEV].add(hub_grad)
        return (row_grad, g_self, g_neigh, g_bias), output

    inputs = (jnp.arange(dev_total, dtype=jnp.int32), tiles.reshape(dev_total, TILES, BLK, BLK), tile_dst, tile_src, tile_count, seed_ids.reshape(dev_total, SEED_DEV), cotangent.reshape(dev_total, SEED_DEV, H))
    start = (jnp.zeros((N_DOM, V_DEV, H), jnp.float32), jnp.zeros((H, H), jnp.float32), jnp.zeros((H, H), jnp.float32), jnp.zeros((H,), jnp.float32))
    final, outputs = lax.scan(one_device, start, inputs)
    out = outputs.reshape(dev_total * SEED_DEV, H)
    input_grad = final[0].reshape(N_DOM * V_DEV, H)
    grad_self = (final[1] * grad_scale).astype(jnp.bfloat16)
    grad_neigh = (final[2] * grad_scale).astype(jnp.bfloat16)
    grad_bias = final[3] * grad_scale
    return (out, input_grad, grad_self, grad_neigh, grad_bias)
```

```python
import functools

import jax
import jax.numpy as jnp
from jax import lax
from jax.experimental import pallas as pl
from jax.experimental.pallas import tpu as pltpu
from jax.sharding import PartitionSpec as P

BLK = 128
SLOTS = 8
HUB_DEV = 8
BF16 = jnp.bfloat16
F32 = jnp.float32
VMEM_BYTES = 48 * 1024 * 1024


def dot(a, b, contract_a=1, contract_b=0):
    return lax.dot_general(
        a, b, (((contract_a,), (contract_b,)), ((), ())), preferred_element_type=F32
    )


def iota(shape, dim):
    return lax.broadcasted_iota(jnp.int32, shape, dim)


def vmem(count):
    return [pl.BlockSpec(memory_space=pltpu.VMEM)] * count


def smem(count):
    return [pl.BlockSpec(memory_space=pltpu.SMEM)] * count


def params():
    return pltpu.CompilerParams(vmem_limit_bytes=VMEM_BYTES)


def cost(flops, size):
    return pl.CostEstimate(flops=flops, bytes_accessed=size, transcendentals=0)


def place_tiles(dst_ref, src_ref, count_ref, tiles_ref, adj_ref, first, last):
    adj_ref[...] = jnp.zeros_like(adj_ref)

    def step(slot, carry):
        block = src_ref[0, slot]

        @pl.when(jnp.logical_and(block >= first, block < last))
        def _():
            row = pl.multiple_of(dst_ref[0, slot] * BLK, BLK)
            col = pl.multiple_of((block - first) * BLK, BLK)
            adj_ref[pl.ds(row, BLK), pl.ds(col, BLK)] = tiles_ref[slot]

        return carry

    lax.fori_loop(0, count_ref[0], step, 0)


def send_kernel(rep_ref, lists_ref, feats_ref, send_ref):
    parts, slots = lists_ref.shape
    rows = feats_ref.shape[0]
    rep = rep_ref[0]
    lists = lists_ref[...].astype(F32)
    wanted = jnp.sum(
        jnp.where(iota((parts, slots), 1) == rep, lists, 0.0), axis=1, keepdims=True
    ).astype(jnp.int32)
    place = iota((parts, rows), 1)
    halo = dot((place == wanted).astype(BF16), feats_ref[...]).astype(BF16)
    hub = dot((place == rep).astype(BF16), feats_ref[...]).astype(BF16)
    both = jnp.concatenate([halo, hub], 0)
    shape = (2 * parts, 2 * parts)
    out, into = iota(shape, 0), iota(shape, 1)
    spread = (into == (out % 2) * parts + out // 2).astype(BF16)
    send_ref[...] = dot(spread, both).astype(BF16)


def own_kernel(
    dst_ref, src_ref, count_ref, tiles_ref, feats_ref, seeds_ref, w_self_ref, bias_ref,
    chosen_ref, preact_ref, part_ref, adj_ref,
):
    rows = feats_ref.shape[0]
    seeds = seeds_ref.shape[1]
    place_tiles(dst_ref, src_ref, count_ref, tiles_ref, adj_ref, 0, rows // BLK)
    picks = (iota((rows, seeds), 0) == seeds_ref[...]).astype(BF16)
    chosen = dot(picks, feats_ref[...], 0, 0).astype(BF16)
    chosen_ref[...] = chosen
    preact_ref[...] = dot(chosen, w_self_ref[...]) + bias_ref[...].astype(F32)
    part_ref[...] = dot(adj_ref[...], feats_ref[...])


def forward_kernel(
    own_blocks, dst_ref, src_ref, count_ref, tiles_ref, table_ref, chosen_ref, preact_ref, part_ref,
    w_neigh_ref, cot_ref, out_ref, grad_ref, bias_ref, d_pre_ref, d_agg_ref, adj_ref, source_ref,
):
    reps, both, width = table_ref.shape
    parts = both // 2
    owners = BLK // reps
    blocks = parts * reps // BLK
    place_tiles(
        dst_ref, src_ref, count_ref, tiles_ref, adj_ref, own_blocks, own_blocks + 2 * blocks
    )
    shape = (2 * BLK, 2 * BLK)
    out, into = iota(shape, 0), iota(shape, 1)
    line = out % BLK
    order = (into == (line % reps) * (2 * owners) + (line // reps) * 2 + out // BLK).astype(BF16)
    for block in range(blocks):
        arrived = table_ref[:, 2 * owners * block : 2 * owners * (block + 1), :]
        sorted_rows = dot(order, arrived.reshape(2 * BLK, width)).astype(BF16)
        source_ref[block * BLK : (block + 1) * BLK] = sorted_rows[:BLK]
        source_ref[(blocks + block) * BLK : (blocks + block + 1) * BLK] = sorted_rows[BLK:]
    aggregate = (part_ref[...] + dot(adj_ref[...], source_ref[...])).astype(BF16)
    preact = preact_ref[...] + dot(aggregate, w_neigh_ref[...])
    gate = jax.nn.sigmoid(preact)
    out_ref[...] = (preact * gate).astype(BF16)
    d_pre = (cot_ref[...].astype(F32) * gate * (1.0 + preact * (1.0 - gate))).astype(BF16)
    d_pre_ref[...] = d_pre
    half = chosen_ref.shape[1]
    grad_ref[:half] = dot(chosen_ref[...], d_pre, 0, 0).astype(BF16)
    grad_ref[half:] = dot(aggregate, d_pre, 0, 0).astype(BF16)
    bias_ref[...] = jnp.sum(d_pre.astype(F32), 0, keepdims=True)
    d_agg_ref[...] = dot(d_pre, w_neigh_ref[...], 1, 1).astype(BF16)


def split_rows(wide, rows):
    high = wide.astype(BF16)
    low = (wide - high.astype(F32)).astype(BF16)
    row = iota((rows, wide.shape[1]), 0)
    zero = jnp.zeros((), F32)
    return jnp.where(row == 0, high.astype(F32), jnp.where(row == 1, low.astype(F32), zero)).astype(
        BF16
    )


def backward_kernel(
    dst_ref, src_ref, count_ref, tiles_ref, seeds_ref, d_pre_ref, d_agg_ref, w_self_ref, bias_ref,
    own_ref, send_ref, adj_ref,
):
    reps, lines, width = send_ref.shape
    rows = own_ref.shape[0]
    own_blocks = rows // BLK
    blocks = (adj_ref.shape[1] // BLK - own_blocks) // 2
    parts = blocks * BLK // reps
    owners = BLK // reps
    place_tiles(
        dst_ref, src_ref, count_ref, tiles_ref, adj_ref, 0, own_blocks + 2 * blocks
    )
    d_agg = d_agg_ref[...]
    out, into = iota((BLK, BLK), 0), iota((BLK, BLK), 1)
    order = (into == (out % owners) * reps + out // owners).astype(BF16)
    for kind in range(2):
        for block in range(blocks):
            start = (own_blocks + kind * blocks + block) * BLK
            grad = dot(adj_ref[:, start : start + BLK], d_agg, 0, 0).astype(BF16)
            grad = dot(order, grad).astype(BF16).reshape(reps, owners, width)
            first = kind * parts + block * owners
            send_ref[:, first : first + owners, :] = grad
    bias_rows = split_rows(bias_ref[...], lines - 2 * parts)
    for rep in range(reps):
        send_ref[rep, 2 * parts :, :] = bias_rows
    picks = (iota((rows, d_agg.shape[0]), 0) == seeds_ref[...]).astype(BF16)
    seeded = dot(picks, d_pre_ref[...]).astype(BF16)
    own_ref[...] = dot(seeded, w_self_ref[...], 1, 1) + dot(
        adj_ref[:, :rows], d_agg, 0, 0
    )


def scatter_kernel(rep_ref, lists_ref, back_ref, own_ref, row_ref):
    parts, slots = lists_ref.shape
    rows = own_ref.shape[0]
    rep = rep_ref[0]
    lists = lists_ref[...].astype(F32)
    wanted = jnp.sum(
        jnp.where(iota((parts, slots), 1) == rep, lists, 0.0), axis=1, keepdims=True
    ).astype(jnp.int32)
    place = iota((parts, rows), 1)
    halo_place = (place == wanted).astype(BF16)
    hub_place = (place == rep).astype(BF16)
    picks = jnp.concatenate([halo_place, hub_place], 0)
    row_ref[...] = (own_ref[...] + dot(picks, back_ref[...], 0, 0)).astype(BF16)


def body(
    feats,
    halo_index,
    seed_ids,
    tiles,
    tile_dst,
    tile_src,
    tile_count,
    w_self,
    w_neigh,
    bias,
    cotangent,
):
    parts = lax.axis_size("dom")
    reps = lax.axis_size("rep")
    rows, width = feats.shape
    seeds = cotangent.shape[0]
    rep = lax.axis_index("rep").astype(jnp.int32).reshape(1)
    lists = halo_index[0]
    seed_row = seed_ids.reshape(1, seeds)
    halo_rows = parts * SLOTS
    tile_args = (tile_dst, tile_src, tile_count, tiles)

    def swap(values, axis):
        return lax.all_to_all(values, axis, split_axis=0, concat_axis=0, tiled=True)

    def spread(values, axis, total):
        return swap(jnp.broadcast_to(values[None], (total,) + values.shape), axis)

    send = pl.pallas_call(
        send_kernel,
        out_shape=jax.ShapeDtypeStruct((2 * parts, width), BF16),
        in_specs=smem(1) + vmem(2),
        out_specs=vmem(1)[0],
        compiler_params=params(),
        cost_estimate=cost(4 * parts * rows * width, 2**20),
        name="pick_boundary",
    )(rep, lists, feats)
    arrived = swap(send.reshape(parts, 2, width), "dom")
    table = spread(arrived.reshape(2 * parts, width), "rep", reps)

    chosen, preact, part = pl.pallas_call(
        own_kernel,
        out_shape=(
            jax.ShapeDtypeStruct((seeds, width), BF16),
            jax.ShapeDtypeStruct((seeds, width), F32),
            jax.ShapeDtypeStruct((seeds, width), F32),
        ),
        in_specs=smem(3) + vmem(5),
        out_specs=tuple(vmem(3)),
        scratch_shapes=[pltpu.VMEM((seeds, rows), BF16)],
        compiler_params=params(),
        cost_estimate=cost(2 * seeds * width * (2 * rows + width), 5 * 2**20),
        name="own_rows",
    )(*tile_args, feats, seed_row, w_self, bias.reshape(1, width))

    out, grads, bias_part, d_pre, d_agg = pl.pallas_call(
        functools.partial(forward_kernel, rows // BLK),
        out_shape=(
            jax.ShapeDtypeStruct((seeds, width), BF16),
            jax.ShapeDtypeStruct((2 * width, width), BF16),
            jax.ShapeDtypeStruct((1, width), F32),
            jax.ShapeDtypeStruct((seeds, width), BF16),
            jax.ShapeDtypeStruct((seeds, width), BF16),
        ),
        in_specs=smem(3) + vmem(7),
        out_specs=tuple(vmem(5)),
        scratch_shapes=[
            pltpu.VMEM((seeds, 2 * halo_rows), BF16),
            pltpu.VMEM((2 * halo_rows, width), BF16),
        ],
        compiler_params=params(),
        cost_estimate=cost(2 * seeds * width * (2 * halo_rows + 4 * width), 6 * 2**20),
        name="forward",
    )(*tile_args, table, chosen, preact, part, w_neigh, cotangent)

    weight_parts = swap(grads.reshape(reps, -1, width), "rep")

    own, back_send = pl.pallas_call(
        backward_kernel,
        out_shape=(
            jax.ShapeDtypeStruct((rows, width), F32),
            jax.ShapeDtypeStruct((reps, 2 * parts + 16, width), BF16),
        ),
        in_specs=smem(3) + vmem(6),
        out_specs=tuple(vmem(2)),
        scratch_shapes=[pltpu.VMEM((seeds, rows + 2 * halo_rows), BF16)],
        compiler_params=params(),
        cost_estimate=cost(2 * seeds * width * (3 * rows + 2 * halo_rows), 5 * 2**20),
        name="backward",
    )(*tile_args, seed_row, d_pre, d_agg, w_self, bias_part)

    back_parts = swap(back_send, "rep")

    weight_sum = jnp.sum(weight_parts.astype(F32), 0).astype(BF16)
    weight_rows = weight_sum.reshape(parts, -1, width)
    weight_dom = swap(weight_rows, "dom")

    back_sum = jnp.sum(back_parts.astype(F32), 0)
    bias_sum = back_sum[2 * parts] + back_sum[2 * parts + 1]
    bias_high = bias_sum.astype(BF16)
    bias_low = (bias_sum - bias_high.astype(F32)).astype(BF16)
    back_rows = jnp.stack(
        [
            back_sum[:parts].astype(BF16),
            back_sum[parts : 2 * parts].astype(BF16),
            jnp.broadcast_to(bias_high[None], (parts, width)),
            jnp.broadcast_to(bias_low[None], (parts, width)),
        ],
        1,
    )
    back_dom = swap(back_rows, "dom")

    grad_scale = float(seeds * parts * reps) ** (-0.5)
    weight_done = (jnp.sum(weight_dom.astype(F32), 0) * grad_scale).astype(BF16)
    weight_table = spread(weight_done, "dom", parts).reshape(-1, width)
    weight_all = spread(weight_table, "rep", reps).reshape(2 * width, width)

    grad_bias = jnp.sum(back_dom[:, 2:].astype(F32), (0, 1)) * grad_scale
    back = jnp.swapaxes(back_dom[:, :2], 0, 1).reshape(2 * parts, width)
    row_part = pl.pallas_call(
        scatter_kernel,
        out_shape=jax.ShapeDtypeStruct((rows, width), BF16),
        in_specs=smem(1) + vmem(3),
        out_specs=vmem(1)[0],
        compiler_params=params(),
        cost_estimate=cost(4 * parts * rows * width, 3 * 2**20),
        name="return_rows",
    )(rep, lists, back, own)
    row_parts = swap(row_part.reshape(reps, -1, width), "rep")
    input_grad = jnp.sum(row_parts.astype(F32), 0)
    return (out, input_grad, weight_all[:width], weight_all[width:], grad_bias)


def solution(mesh):
    placed = (
        P("dom", None),
        P("dom", None, None),
        P(("dom", "rep")),
        P(("dom", "rep"), None, None),
        P(("dom", "rep"), None),
        P(("dom", "rep"), None),
        P(("dom", "rep")),
        P(),
        P(),
        P(),
        P(("dom", "rep"), None),
    )
    return jax.shard_map(
        body,
        mesh=mesh,
        in_specs=placed,
        out_specs=(P(("dom", "rep"), None), P(("dom", "rep"), None), P(), P(), P()),
        check_vma=False,
    )
```

```python
import functools

import jax
import jax.numpy as jnp
from jax import lax
from jax.experimental import pallas as pl
from jax.experimental.pallas import tpu as pltpu
from jax.sharding import Mesh
from jax.sharding import PartitionSpec as P

BLK = 128
LANES = 128
SLOTS = 8
X_SIZE = 4
CORES = 2
Y_SIZE = 4
PLANE = Y_SIZE * X_SIZE
BF16 = jnp.bfloat16
F32 = jnp.float32
VMEM_BYTES = 24 * 1024 * 1024


def dot(a, b, contract_a=1, contract_b=0):
    return lax.dot_general(
        a, b, (((contract_a,), (contract_b,)), ((), ())), preferred_element_type=F32
    )


def move(matrix, rows):
    return dot(matrix.astype(BF16), rows).astype(BF16)


def iota(shape, dim):
    return lax.broadcasted_iota(jnp.int32, shape, dim)


def split(wide):
    high = wide.astype(BF16)
    return high, (wide - high.astype(F32)).astype(BF16)


def call(kernel, name, outs, scalars, arrays, scratch=(), flops=0):
    shapes = tuple(jax.ShapeDtypeStruct(shape, dtype) for shape, dtype in outs)
    size = sum(a.size * a.dtype.itemsize for a in (*arrays, *shapes))
    return pl.pallas_call(
        kernel,
        out_shape=shapes,
        in_specs=[pl.BlockSpec(memory_space=pltpu.SMEM)] * len(scalars)
        + [pl.BlockSpec(memory_space=pltpu.VMEM)] * len(arrays),
        out_specs=tuple(pl.BlockSpec(memory_space=pltpu.VMEM) for _ in outs),
        scratch_shapes=list(scratch),
        compiler_params=pltpu.CompilerParams(vmem_limit_bytes=VMEM_BYTES),
        cost_estimate=pl.CostEstimate(flops=flops, bytes_accessed=size, transcendentals=0),
        name=name,
    )(*scalars, *arrays)


def place_tiles(dst_ref, src_ref, count_ref, tiles_ref, adj_ref, first, last):
    adj_ref[...] = jnp.zeros_like(adj_ref)

    def step(slot, carry):
        block = src_ref[0, slot]

        @pl.when(jnp.logical_and(block >= first, block < last))
        def _():
            row = pl.multiple_of(dst_ref[0, slot] * BLK, BLK)
            col = pl.multiple_of((block - first) * BLK, BLK)
            adj_ref[pl.ds(row, BLK), pl.ds(col, BLK)] = tiles_ref[slot]

        return carry

    lax.fori_loop(0, count_ref[0], step, 0)


def boundary_places(rep, lists_ref, rows):
    parts, slots = lists_ref.shape
    lists = lists_ref[...].astype(F32)
    wanted = jnp.sum(
        jnp.where(iota((parts, slots), 1) == rep, lists, 0.0), axis=1, keepdims=True
    ).astype(jnp.int32)
    place = iota((parts, rows), 1)
    return jnp.concatenate(
        [(place == wanted).astype(BF16), (place == rep).astype(BF16)], 0
    )


def by_z(parts):
    shape = (2 * parts, 2 * parts)
    out, into = iota(shape, 0), iota(shape, 1)
    y, kind, z = out % Y_SIZE, out // Y_SIZE % 2, out // (2 * Y_SIZE)
    return into == kind * parts + z * Y_SIZE + y


def send_kernel(rep_ref, lists_ref, feats_ref, send_ref):
    parts = lists_ref.shape[0]
    places = boundary_places(rep_ref[0], lists_ref, feats_ref.shape[0])
    places = move(by_z(parts), places)
    send_ref[...] = move(places, feats_ref[...])


def plane_kernel(arrived_ref, send_ref):
    chunk = send_ref.shape[1]
    depth = chunk // 2
    total = arrived_ref.shape[0]
    shape = (total, total)
    out, into = iota(shape, 0), iota(shape, 1)
    z, kind, y = out % depth, out // depth % 2, out // chunk
    moved = move(into == z * (2 * Y_SIZE) + kind * Y_SIZE + y, arrived_ref[...])
    for y_to in range(Y_SIZE):
        for x_to in range(X_SIZE):
            send_ref[y_to * X_SIZE + x_to] = moved[y_to * chunk : (y_to + 1) * chunk]


def own_kernel(
    core_ref, dst_ref, src_ref, count_ref, tiles_ref, feats_ref, seeds_ref, w_self_ref, bias_ref,
    chosen_t_ref, preact_ref, part_ref, near_ref, near_t_ref, far_ref, far_t_ref,
    own_adj_ref, adj_ref,
):
    rows = feats_ref.shape[0]
    seeds = seeds_ref.shape[1]
    own_blocks = rows // BLK
    table = adj_ref.shape[1]
    place_tiles(dst_ref, src_ref, count_ref, tiles_ref, own_adj_ref, 0, own_blocks)
    place_tiles(
        dst_ref, src_ref, count_ref, tiles_ref, adj_ref, own_blocks, own_blocks + table // BLK
    )
    picks = (iota((rows, seeds), 0) == seeds_ref[...]).astype(BF16)
    feats = feats_ref[...]
    chosen_t_ref[...] = dot(feats, picks, 0, 0).astype(BF16)
    chosen = dot(picks, feats, 0, 0).astype(BF16)
    preact_ref[...] = dot(chosen, w_self_ref[...]) + bias_ref[...].astype(F32)
    part_ref[...] = dot(own_adj_ref[...], feats)
    adj = adj_ref[...]
    half = table // 2
    depth = half // PLANE // 2
    shape = (half, table)
    line, source = iota(shape, 0), iota(shape, 1)
    z, kind = line % depth, line // depth % 2
    x, y = line // (2 * depth) % X_SIZE, line // (2 * depth * X_SIZE)
    start = kind * half + (z * Y_SIZE + y) * SLOTS + x * CORES
    for core, to_ref, to_t_ref in (
        (core_ref[0], near_ref, near_t_ref),
        (1 - core_ref[0], far_ref, far_t_ref),
    ):
        order = (source == start + core).astype(BF16)
        to_ref[...] = dot(adj, order, 1, 1).astype(BF16)
        to_t_ref[...] = dot(order, adj, 1, 1).astype(BF16)


def middle_kernel(
    core_ref, near_ref, far_ref, near_adj_ref, near_adj_t_ref, far_adj_ref, far_adj_t_ref,
    chosen_t_ref, preact_ref, part_ref, w_neigh_ref, cot_ref,
    out_ref, d_pre_ref, d_agg_ref, keep_ref, send_ref,
):
    width = w_neigh_ref.shape[0]
    half = near_ref.shape[0]
    aggregate = (
        part_ref[...]
        + dot(near_adj_ref[...], near_ref[...])
        + dot(far_adj_ref[...], far_ref[...])
    ).astype(BF16)
    preact = preact_ref[...] + dot(aggregate, w_neigh_ref[...])
    gate = jax.nn.sigmoid(preact)
    out_ref[...] = (preact * gate).astype(BF16)
    d_pre = (cot_ref[...].astype(F32) * gate * (1.0 + preact * (1.0 - gate))).astype(BF16)
    d_pre_ref[...] = d_pre
    d_agg = dot(d_pre, w_neigh_ref[...], 1, 1).astype(BF16)
    d_agg_ref[...] = d_agg
    first = dot(chosen_t_ref[...], d_pre).astype(BF16)
    second = dot(aggregate, d_pre, 0, 0).astype(BF16)
    is_first = core_ref[0] == 0
    keep_ref[:width] = jnp.where(is_first, first, second)
    send_ref[:width] = jnp.where(is_first, second, first)
    keep_ref[width : width + half] = dot(near_adj_t_ref[...], d_agg).astype(BF16)
    send_ref[width : width + half] = dot(far_adj_t_ref[...], d_agg).astype(BF16)
    high, low = split(jnp.sum(d_pre.astype(F32), 0, keepdims=True))
    row = iota((keep_ref.shape[0] - width - half, width), 0)
    pair = jnp.where(
        row == 0, high.astype(F32), jnp.where(row == 1, low.astype(F32), 0.0)
    ).astype(BF16)
    keep_ref[width + half :] = pair
    send_ref[width + half :] = pair


def pair_sum_kernel(keep_ref, other_ref, send_ref):
    chunks, lines, width = send_ref.shape
    total = keep_ref[...].astype(F32) + other_ref[...].astype(F32)
    weight, table = width // chunks, (lines - 8 - width // chunks)
    tail = width + chunks * table
    high, low = split(total[tail : tail + 1] + total[tail + 1 : tail + 2])
    row = iota((8, width), 0)
    pair = jnp.where(row == 0, high.astype(F32), jnp.where(row == 1, low.astype(F32), 0.0))
    for chunk in range(chunks):
        send_ref[chunk] = jnp.concatenate(
            [
                total[chunk * weight : (chunk + 1) * weight],
                total[width + chunk * table : width + (chunk + 1) * table],
                pair,
            ],
            0,
        ).astype(BF16)


def plane_sum_kernel(arrived_ref, send_ref):
    chunks, lines, width = arrived_ref.shape
    depth = send_ref.shape[0]
    block = send_ref.shape[1]
    weight = width // chunks
    table = lines - 8 - weight
    groups = width // LANES
    each = weight // depth
    by_y = []
    rest = None
    for y in range(Y_SIZE):
        some = arrived_ref[y * X_SIZE].astype(F32)
        for x in range(1, X_SIZE):
            some = some + arrived_ref[y * X_SIZE + x].astype(F32)
        by_y.append(some[weight : weight + table].astype(BF16))
        rest = some if rest is None else rest + some
    back = jnp.concatenate(by_y, 0)
    shape = (depth * block, Y_SIZE * table)
    out, into = iota(shape, 0), iota(shape, 1)
    y, kind, z = out % Y_SIZE, out // Y_SIZE % 2, out // block
    moved = move(into == y * table + kind * depth + z, back)
    send_ref[:, :, :width] = moved.reshape(depth, block, width)

    weights = rest[:weight].astype(BF16)
    high, low = split(rest[weight + table : weight + table + 1] + rest[weight + table + 1 : weight + table + 2])
    pair_row = iota((16, width), 0)
    pair = jnp.where(
        pair_row == 0, high.astype(F32), jnp.where(pair_row == 1, low.astype(F32), 0.0)
    ).astype(BF16)
    shape = (depth * block, weight)
    out, into = iota(shape, 0), iota(shape, 1)
    line, z = out % block, out // block
    pair_shape = (depth * block, 16)
    pair_line, pair_into = iota(pair_shape, 0) % block, iota(pair_shape, 1)
    weight_block = jnp.zeros((depth * block, LANES), F32)
    bias_block = jnp.zeros((depth * block, LANES), F32)
    for group in range(groups):
        lanes = slice(group * LANES, (group + 1) * LANES)
        here = jnp.logical_and(line // each == group, into == z * each + line % each)
        weight_block += dot(here.astype(BF16), weights[:, lanes])
        here = jnp.logical_and(pair_line // 2 == group, pair_into == pair_line % 2)
        bias_block += dot(here.astype(BF16), pair[:, lanes])
    send_ref[:, :, width : width + LANES] = weight_block.astype(BF16).reshape(depth, block, LANES)
    send_ref[:, :, width + LANES :] = bias_block.astype(BF16).reshape(depth, block, LANES)


def weight_kernel(scale, arrived_ref, send_ref, bias_ref):
    depth, block, _ = arrived_ref.shape
    width = arrived_ref.shape[2] - 2 * LANES
    total = jnp.sum(arrived_ref[:, :, width:].astype(F32), 0) * scale
    done = total[:, :LANES].astype(BF16)
    for z in range(depth):
        send_ref[z] = done
    bias_ref[...] = total[:, LANES:]


def gather_kernel(arrived_ref, send_ref):
    chunks, weight, width = send_ref.shape
    depth, block, _ = arrived_ref.shape
    groups = width // LANES
    each = weight // depth
    arrived = arrived_ref[...].reshape(depth * block, LANES)
    shape = (weight, depth * block)
    out, into = iota(shape, 0), iota(shape, 1)
    z, line = out // each, out % each
    parts = [
        move(into == z * block + group * each + line, arrived) for group in range(groups)
    ]
    whole = jnp.concatenate(parts, 1)
    for chunk in range(chunks):
        send_ref[chunk] = whole


def own_back_kernel(
    dst_ref, src_ref, count_ref, tiles_ref, seeds_ref, d_pre_ref, d_agg_ref, w_self_ref,
    own_ref, adj_ref,
):
    rows = own_ref.shape[0]
    seeds = seeds_ref.shape[1]
    place_tiles(dst_ref, src_ref, count_ref, tiles_ref, adj_ref, 0, rows // BLK)
    picks = (iota((rows, seeds), 0) == seeds_ref[...]).astype(BF16)
    seeded = dot(picks, d_pre_ref[...]).astype(BF16)
    own_ref[...] = dot(seeded, w_self_ref[...], 1, 1) + dot(adj_ref[...], d_agg_ref[...], 0, 0)


def scatter_kernel(rep_ref, core_ref, lists_ref, arrived_ref, own_ref, keep_ref, send_ref):
    parts = lists_ref.shape[0]
    rows, width = own_ref.shape
    places = move(by_z(parts), boundary_places(rep_ref[0], lists_ref, rows))
    back = arrived_ref[:, :, :width].reshape(2 * parts, width)
    total = (own_ref[...] + dot(places, back, 0, 0)).astype(BF16)
    share = rows // (X_SIZE * CORES)
    first = core_ref[0] == 0
    for x in range(X_SIZE):
        low = total[2 * x * share : (2 * x + 1) * share]
        high = total[(2 * x + 1) * share : (2 * x + 2) * share]
        keep_ref[x] = jnp.where(first, low, high)
        send_ref[x] = jnp.where(first, high, low)


def body(
    feats,
    halo_index,
    seed_ids,
    tiles,
    tile_dst,
    tile_src,
    tile_count,
    w_self,
    w_neigh,
    bias,
    cotangent,
):
    depth = lax.axis_size("z")
    parts = depth * Y_SIZE
    reps = X_SIZE * CORES
    rows, width = feats.shape
    seeds = cotangent.shape[0]
    half = parts * SLOTS
    core_id = lax.axis_index("core").astype(jnp.int32)
    x_id = lax.axis_index("x").astype(jnp.int32)
    core = core_id.reshape(1)
    rep = (x_id * CORES + core_id).reshape(1)
    lists = halo_index[0]
    seed_row = seed_ids.reshape(1, seeds)
    tile_scalars = (tile_dst, tile_src, tile_count)
    scale = float(seeds * parts * reps) ** (-0.5)

    def swap(values, axis):
        return lax.all_to_all(values, axis, split_axis=0, concat_axis=0, tiled=True)

    def pair(values):
        return lax.ppermute(values, "core", [(0, 1), (1, 0)])

    (send,) = call(
        send_kernel, "pick_boundary", [((2 * parts, width), BF16)], [rep], [lists, feats],
        flops=4 * parts * rows * width,
    )
    by_depth = swap(send.reshape(depth, 2 * Y_SIZE, width), "z").reshape(2 * parts, width)
    (plane,) = call(
        plane_kernel, "spread_plane", [((PLANE, 2 * depth, width), BF16)], [], [by_depth],
        flops=8 * parts * parts * width,
    )
    near = swap(plane, ("y", "x")).reshape(half, width)
    far = pair(near)

    chosen_t, preact, part, near_adj, near_adj_t, far_adj, far_adj_t = call(
        own_kernel, "own_rows",
        [
            ((width, seeds), BF16),
            ((seeds, width), F32),
            ((seeds, width), F32),
            ((seeds, half), BF16),
            ((half, seeds), BF16),
            ((seeds, half), BF16),
            ((half, seeds), BF16),
        ],
        [core, *tile_scalars],
        [tiles, feats, seed_row, w_self, bias.reshape(1, width)],
        scratch=[pltpu.VMEM((seeds, rows), BF16), pltpu.VMEM((seeds, 2 * half), BF16)],
        flops=2 * seeds * (3 * rows * width + width * width + 8 * half * half),
    )

    out, d_pre, d_agg, keep, pair_send = call(
        middle_kernel, "forward_backward",
        [
            ((seeds, width), BF16),
            ((seeds, width), BF16),
            ((seeds, width), BF16),
            ((width + half + 16, width), BF16),
            ((width + half + 16, width), BF16),
        ],
        [core],
        [
            near, far, near_adj, near_adj_t, far_adj, far_adj_t,
            chosen_t, preact, part, w_neigh, cotangent,
        ],
        flops=2 * seeds * width * (4 * half + 4 * width),
    )

    pair_arrived = pair(pair_send)
    (plane_send,) = call(
        pair_sum_kernel, "sum_pair",
        [((PLANE, width // PLANE + 2 * depth + 8, width), BF16)],
        [], [keep, pair_arrived],
    )
    plane_arrived = swap(plane_send, ("y", "x"))
    (depth_send,) = call(
        plane_sum_kernel, "sum_plane",
        [((depth, 2 * Y_SIZE, width + 2 * LANES), BF16)],
        [], [plane_arrived],
    )
    depth_arrived = swap(depth_send, "z")
    weight_send, bias_rows = call(
        functools.partial(weight_kernel, scale), "sum_weights",
        [((depth, 2 * Y_SIZE, LANES), BF16), ((2 * Y_SIZE, LANES), F32)],
        [], [depth_arrived],
    )
    weight_depth = swap(weight_send, "z")
    (weight_plane,) = call(
        gather_kernel, "gather_weights",
        [((PLANE, width // PLANE, width), BF16)],
        [], [weight_depth],
    )
    weight_near = swap(weight_plane, ("y", "x")).reshape(width, width)
    weight_far = pair(weight_near)
    grad_self = jnp.where(core_id == 0, weight_near, weight_far)
    grad_neigh = jnp.where(core_id == 0, weight_far, weight_near)
    groups = width // LANES
    grad_bias = bias_rows[: 2 * groups].reshape(groups, 2, LANES).sum(1).reshape(width)

    (own,) = call(
        own_back_kernel, "own_rows_back", [((rows, width), F32)],
        [*tile_scalars], [tiles, seed_row, d_pre, d_agg, w_self],
        scratch=[pltpu.VMEM((seeds, rows), BF16)],
        flops=2 * seeds * width * 3 * rows,
    )
    share = rows // reps
    row_keep, row_send = call(
        scatter_kernel, "return_rows",
        [((X_SIZE, share, width), BF16), ((X_SIZE, share, width), BF16)],
        [rep, core], [lists, depth_arrived, own],
        flops=4 * parts * rows * width,
    )
    row_pair = row_keep.astype(F32) + pair(row_send).astype(F32)
    rows_out = row_pair.astype(BF16)
    input_grad = lax.dynamic_index_in_dim(row_pair, x_id, 0, keepdims=False)
    for shift in range(1, X_SIZE):
        chunk = lax.dynamic_index_in_dim(rows_out, (x_id + shift) % X_SIZE, 0, keepdims=False)
        chunk = lax.ppermute(chunk, "x", [(x, (x + shift) % X_SIZE) for x in range(X_SIZE)])
        input_grad = input_grad + chunk.astype(F32)
    return (out, input_grad, grad_self, grad_neigh, grad_bias)


def solution(mesh):
    parts = mesh.shape["dom"]
    physical = Mesh(
        mesh.devices.reshape(parts // Y_SIZE, Y_SIZE, X_SIZE, CORES), ("z", "y", "x", "core")
    )
    dom = ("z", "y")
    every = ("z", "y", "x", "core")
    placed = (
        P(dom, None),
        P(dom, None, None),
        P(every),
        P(every, None, None),
        P(every, None),
        P(every, None),
        P(every),
        P(),
        P(),
        P(),
        P(every, None),
    )
    return jax.shard_map(
        body,
        mesh=physical,
        in_specs=placed,
        out_specs=(P(every, None), P(every, None), P(), P(), P()),
        check_vma=False,
    )
```

```python
import functools

import jax
import jax.numpy as jnp
from jax import lax
from jax.experimental import pallas as pl
from jax.experimental.pallas import tpu as pltpu
from jax.sharding import Mesh
from jax.sharding import PartitionSpec as P

BLK = 128
LANES = 128
SLOTS = 8
X_SIZE = 4
CORES = 2
Y_SIZE = 4
PLANE = Y_SIZE * X_SIZE
BF16 = jnp.bfloat16
F32 = jnp.float32
VMEM_BYTES = 24 * 1024 * 1024


def dot(a, b, contract_a=1, contract_b=0):
    return lax.dot_general(
        a, b, (((contract_a,), (contract_b,)), ((), ())), preferred_element_type=F32
    )


def move(matrix, rows):
    return dot(matrix.astype(BF16), rows).astype(BF16)


def iota(shape, dim):
    return lax.broadcasted_iota(jnp.int32, shape, dim)


def split(wide):
    high = wide.astype(BF16)
    return high, (wide - high.astype(F32)).astype(BF16)


def call(kernel, name, outs, scalars, arrays, scratch=(), flops=0, after=(), space=pltpu.VMEM):
    if after:
        inner, at = kernel, len(scalars) + len(arrays)
        kernel = lambda *refs: inner(*refs[:at], *refs[at + len(after) :])
    shapes = tuple(jax.ShapeDtypeStruct(shape, dtype) for shape, dtype in outs)
    size = sum(a.size * a.dtype.itemsize for a in (*arrays, *shapes))
    return pl.pallas_call(
        kernel,
        out_shape=shapes,
        in_specs=[pl.BlockSpec(memory_space=pltpu.SMEM)] * len(scalars)
        + [pl.BlockSpec(memory_space=space)] * len(arrays)
        + [pl.BlockSpec(memory_space=pl.ANY)] * len(after),
        out_specs=tuple(pl.BlockSpec(memory_space=pltpu.VMEM) for _ in outs),
        scratch_shapes=list(scratch),
        compiler_params=pltpu.CompilerParams(vmem_limit_bytes=VMEM_BYTES),
        cost_estimate=pl.CostEstimate(flops=flops, bytes_accessed=size, transcendentals=0),
        name=name,
    )(*scalars, *arrays, *after)


def place_tiles(dst_ref, src_ref, count_ref, tiles_ref, adj_ref, first, last):
    adj_ref[...] = jnp.zeros_like(adj_ref)

    def step(slot, carry):
        block = src_ref[0, slot]

        @pl.when(jnp.logical_and(block >= first, block < last))
        def _():
            row = pl.multiple_of(dst_ref[0, slot] * BLK, BLK)
            col = pl.multiple_of((block - first) * BLK, BLK)
            adj_ref[pl.ds(row, BLK), pl.ds(col, BLK)] = tiles_ref[slot]

        return carry

    lax.fori_loop(0, count_ref[0], step, 0)


def boundary_places(rep, lists_ref, rows):
    slots, parts = lists_ref.shape
    lists = lists_ref[...].astype(F32)
    wanted = jnp.sum(
        jnp.where(iota((slots, parts), 0) == rep, lists, 0.0), axis=0, keepdims=True
    ).astype(jnp.int32)
    place = iota((rows, parts), 0)
    places = jnp.concatenate([(place == wanted).astype(BF16), (place == rep).astype(BF16)], 1)
    return dot(places, by_z(parts).astype(BF16), 1, 1).astype(BF16)


def by_z(parts):
    shape = (2 * parts, 2 * parts)
    out, into = iota(shape, 0), iota(shape, 1)
    y, kind, z = out % Y_SIZE, out // Y_SIZE % 2, out // (2 * Y_SIZE)
    return into == kind * parts + z * Y_SIZE + y


def send_kernel(rep_ref, lists_hbm, feats_hbm, send_ref, lists_ref, feats_ref, sems):
    lists_copy = pltpu.make_async_copy(lists_hbm, lists_ref, sems.at[0])
    feats_copy = pltpu.make_async_copy(feats_hbm, feats_ref, sems.at[1])
    lists_copy.start()
    feats_copy.start()
    lists_copy.wait()
    places = boundary_places(rep_ref[0], lists_ref, feats_ref.shape[0])
    feats_copy.wait()
    send_ref[...] = dot(places, feats_ref[...], 0, 0).astype(BF16)


def plane_kernel(arrived_ref, send_ref):
    chunk = send_ref.shape[1]
    depth = chunk // 2
    total = arrived_ref.shape[0]
    shape = (total, total)
    out, into = iota(shape, 0), iota(shape, 1)
    z, kind, y = out % depth, out // depth % 2, out // chunk
    moved = move(into == z * (2 * Y_SIZE) + kind * Y_SIZE + y, arrived_ref[...])
    for y_to in range(Y_SIZE):
        for x_to in range(X_SIZE):
            send_ref[y_to * X_SIZE + x_to] = moved[y_to * chunk : (y_to + 1) * chunk]


def own_kernel(
    core_ref, dst_ref, src_ref, count_ref, tiles_ref, feats_ref, seeds_ref, w_self_ref, bias_ref,
    chosen_t_ref, preact_ref, part_ref, near_ref, near_t_ref, far_ref, far_t_ref,
    own_adj_ref, adj_ref,
):
    rows = feats_ref.shape[0]
    seeds = seeds_ref.shape[1]
    own_blocks = rows // BLK
    table = adj_ref.shape[1]
    place_tiles(dst_ref, src_ref, count_ref, tiles_ref, own_adj_ref, 0, own_blocks)
    place_tiles(
        dst_ref, src_ref, count_ref, tiles_ref, adj_ref, own_blocks, own_blocks + table // BLK
    )
    picks = (iota((rows, seeds), 0) == seeds_ref[...]).astype(BF16)
    feats = feats_ref[...]
    chosen_t_ref[...] = dot(feats, picks, 0, 0).astype(BF16)
    chosen = dot(picks, feats, 0, 0).astype(BF16)
    preact_ref[...] = dot(chosen, w_self_ref[...]) + bias_ref[...].astype(F32)
    part_ref[...] = dot(own_adj_ref[...], feats)
    adj = adj_ref[...]
    half = table // 2
    depth = half // PLANE // 2
    shape = (half, table)
    line, source = iota(shape, 0), iota(shape, 1)
    z, kind = line % depth, line // depth % 2
    x, y = line // (2 * depth) % X_SIZE, line // (2 * depth * X_SIZE)
    start = kind * half + (z * Y_SIZE + y) * SLOTS + x * CORES
    for core, to_ref, to_t_ref in (
        (core_ref[0], near_ref, near_t_ref),
        (1 - core_ref[0], far_ref, far_t_ref),
    ):
        order = (source == start + core).astype(BF16)
        to_ref[...] = dot(adj, order, 1, 1).astype(BF16)
        to_t_ref[...] = dot(order, adj, 1, 1).astype(BF16)


def middle_kernel(
    core_ref, near_ref, far_ref, near_adj_ref, near_adj_t_ref, far_adj_ref, far_adj_t_ref,
    chosen_t_ref, preact_ref, part_ref, w_neigh_ref, cot_ref,
    out_ref, d_pre_ref, d_agg_ref, keep_ref, send_ref,
):
    width = w_neigh_ref.shape[0]
    half = near_ref.shape[0]
    aggregate = (
        part_ref[...]
        + dot(near_adj_ref[...], near_ref[...])
        + dot(far_adj_ref[...], far_ref[...])
    ).astype(BF16)
    preact = preact_ref[...] + dot(aggregate, w_neigh_ref[...])
    gate = jax.nn.sigmoid(preact)
    out_ref[...] = (preact * gate).astype(BF16)
    d_pre = (cot_ref[...].astype(F32) * gate * (1.0 + preact * (1.0 - gate))).astype(BF16)
    d_pre_ref[...] = d_pre
    d_agg = dot(d_pre, w_neigh_ref[...], 1, 1).astype(BF16)
    d_agg_ref[...] = d_agg
    first = dot(chosen_t_ref[...], d_pre).astype(BF16)
    second = dot(aggregate, d_pre, 0, 0).astype(BF16)
    is_first = core_ref[0] == 0
    keep_ref[:width] = jnp.where(is_first, first, second)
    send_ref[:width] = jnp.where(is_first, second, first)
    keep_ref[width : width + half] = dot(near_adj_t_ref[...], d_agg).astype(BF16)
    send_ref[width : width + half] = dot(far_adj_t_ref[...], d_agg).astype(BF16)
    high, low = split(jnp.sum(d_pre.astype(F32), 0, keepdims=True))
    row = iota((keep_ref.shape[0] - width - half, width), 0)
    pair = jnp.where(
        row == 0, high.astype(F32), jnp.where(row == 1, low.astype(F32), 0.0)
    ).astype(BF16)
    keep_ref[width + half :] = pair
    send_ref[width + half :] = pair


def pair_sum_kernel(keep_ref, other_ref, send_ref):
    chunks, lines, width = send_ref.shape
    total = keep_ref[...].astype(F32) + other_ref[...].astype(F32)
    weight, table = width // chunks, (lines - 8 - width // chunks)
    tail = width + chunks * table
    high, low = split(total[tail : tail + 1] + total[tail + 1 : tail + 2])
    row = iota((8, width), 0)
    pair = jnp.where(row == 0, high.astype(F32), jnp.where(row == 1, low.astype(F32), 0.0))
    for chunk in range(chunks):
        send_ref[chunk] = jnp.concatenate(
            [
                total[chunk * weight : (chunk + 1) * weight],
                total[width + chunk * table : width + (chunk + 1) * table],
                pair,
            ],
            0,
        ).astype(BF16)


def plane_sum_kernel(arrived_ref, send_ref):
    chunks, lines, width = arrived_ref.shape
    depth = send_ref.shape[0]
    block = send_ref.shape[1]
    weight = width // chunks
    table = lines - 8 - weight
    groups = width // LANES
    each = weight // depth
    by_y = []
    rest = None
    for y in range(Y_SIZE):
        some = arrived_ref[y * X_SIZE].astype(F32)
        for x in range(1, X_SIZE):
            some = some + arrived_ref[y * X_SIZE + x].astype(F32)
        by_y.append(some[weight : weight + table].astype(BF16))
        rest = some if rest is None else rest + some
    back = jnp.concatenate(by_y, 0)
    shape = (depth * block, Y_SIZE * table)
    out, into = iota(shape, 0), iota(shape, 1)
    y, kind, z = out % Y_SIZE, out // Y_SIZE % 2, out // block
    moved = move(into == y * table + kind * depth + z, back)
    send_ref[:, :, :width] = moved.reshape(depth, block, width)

    weights = rest[:weight].astype(BF16)
    high, low = split(rest[weight + table : weight + table + 1] + rest[weight + table + 1 : weight + table + 2])
    pair_row = iota((16, width), 0)
    pair = jnp.where(
        pair_row == 0, high.astype(F32), jnp.where(pair_row == 1, low.astype(F32), 0.0)
    ).astype(BF16)
    shape = (depth * block, weight)
    out, into = iota(shape, 0), iota(shape, 1)
    line, z = out % block, out // block
    pair_shape = (depth * block, 16)
    pair_line, pair_into = iota(pair_shape, 0) % block, iota(pair_shape, 1)
    weight_block = jnp.zeros((depth * block, LANES), F32)
    bias_block = jnp.zeros((depth * block, LANES), F32)
    for group in range(groups):
        lanes = slice(group * LANES, (group + 1) * LANES)
        here = jnp.logical_and(line // each == group, into == z * each + line % each)
        weight_block += dot(here.astype(BF16), weights[:, lanes])
        here = jnp.logical_and(pair_line // 2 == group, pair_into == pair_line % 2)
        bias_block += dot(here.astype(BF16), pair[:, lanes])
    send_ref[:, :, width : width + LANES] = weight_block.astype(BF16).reshape(depth, block, LANES)
    send_ref[:, :, width + LANES :] = bias_block.astype(BF16).reshape(depth, block, LANES)


def weight_kernel(scale, arrived_ref, send_ref, bias_ref):
    depth, block, _ = arrived_ref.shape
    width = arrived_ref.shape[2] - 2 * LANES
    total = jnp.sum(arrived_ref[:, :, width:].astype(F32), 0) * scale
    done = total[:, :LANES].astype(BF16)
    for z in range(depth):
        send_ref[z] = done
    bias_ref[...] = total[:, LANES:]


def gather_kernel(arrived_ref, send_ref):
    chunks, weight, width = send_ref.shape
    depth, block, _ = arrived_ref.shape
    groups = width // LANES
    each = weight // depth
    arrived = arrived_ref[...].reshape(depth * block, LANES)
    shape = (weight, depth * block)
    out, into = iota(shape, 0), iota(shape, 1)
    z, line = out // each, out % each
    parts = [
        move(into == z * block + group * each + line, arrived) for group in range(groups)
    ]
    whole = jnp.concatenate(parts, 1)
    for chunk in range(chunks):
        send_ref[chunk] = whole


def own_back_kernel(
    dst_ref, src_ref, count_ref, tiles_ref, seeds_ref, d_pre_ref, d_agg_ref, w_self_ref,
    own_ref, adj_ref,
):
    rows = own_ref.shape[0]
    seeds = seeds_ref.shape[1]
    place_tiles(dst_ref, src_ref, count_ref, tiles_ref, adj_ref, 0, rows // BLK)
    picks = (iota((rows, seeds), 0) == seeds_ref[...]).astype(BF16)
    seeded = dot(picks, d_pre_ref[...]).astype(BF16)
    own_ref[...] = dot(seeded, w_self_ref[...], 1, 1) + dot(adj_ref[...], d_agg_ref[...], 0, 0)


def scatter_kernel(rep_ref, lists_ref, arrived_ref, own_ref, keep_ref, send_ref, total_ref):
    rows, width = own_ref.shape
    rep = rep_ref[0]
    places = boundary_places(rep, lists_ref, rows)
    back = arrived_ref[:, :, :width].reshape(places.shape[1], width)
    total_ref[...] = (own_ref[...] + dot(places, back)).astype(BF16)
    share = rows // (X_SIZE * CORES)
    for step in range(X_SIZE):
        keep = jnp.bitwise_xor(rep, step * CORES)
        for place, ref in ((keep, keep_ref), (jnp.bitwise_xor(keep, 1), send_ref)):
            ref[step] = total_ref[pl.ds(pl.multiple_of(place * share, 32), share), :]


def copy_kernel(from_ref, to_ref):
    to_ref[...] = from_ref[...]


def body(
    feats,
    halo_index,
    seed_ids,
    tiles,
    tile_dst,
    tile_src,
    tile_count,
    w_self,
    w_neigh,
    bias,
    cotangent,
):
    depth = lax.axis_size("z")
    parts = depth * Y_SIZE
    reps = X_SIZE * CORES
    rows, width = feats.shape
    seeds = cotangent.shape[0]
    half = parts * SLOTS
    core_id = lax.axis_index("core").astype(jnp.int32)
    x_id = lax.axis_index("x").astype(jnp.int32)
    core = core_id.reshape(1)
    rep = (x_id * CORES + core_id).reshape(1)
    lists = halo_index[0].T
    seed_row = seed_ids.reshape(1, seeds)
    tile_scalars = (tile_dst, tile_src, tile_count)
    scale = float(seeds * parts * reps) ** (-0.5)

    def swap(values, axis):
        return lax.all_to_all(values, axis, split_axis=0, concat_axis=0, tiled=True)

    def pair(values):
        return lax.ppermute(values, "core", [(0, 1), (1, 0)])

    (send,) = call(
        send_kernel, "pick_boundary", [((2 * parts, width), BF16)], [rep], [lists, feats],
        scratch=[
            pltpu.VMEM(lists.shape, jnp.int32),
            pltpu.VMEM(feats.shape, BF16),
            pltpu.SemaphoreType.DMA((2,)),
        ],
        space=pl.ANY,
        flops=4 * parts * rows * width,
    )
    by_depth = swap(send.reshape(depth, 2 * Y_SIZE, width), "z").reshape(2 * parts, width)
    chosen_t, preact, part, near_adj, near_adj_t, far_adj, far_adj_t = call(
        own_kernel, "own_rows",
        [
            ((width, seeds), BF16),
            ((seeds, width), F32),
            ((seeds, width), F32),
            ((seeds, half), BF16),
            ((half, seeds), BF16),
            ((seeds, half), BF16),
            ((half, seeds), BF16),
        ],
        [core, *tile_scalars],
        [tiles, feats, seed_row, w_self, bias.reshape(1, width)],
        scratch=[pltpu.VMEM((seeds, rows), BF16), pltpu.VMEM((seeds, 2 * half), BF16)],
        flops=2 * seeds * (3 * rows * width + width * width + 8 * half * half),
    )

    (plane,) = call(
        plane_kernel, "spread_plane", [((PLANE, 2 * depth, width), BF16)], [], [by_depth],
        flops=8 * parts * parts * width, after=[part],
    )
    near = swap(plane, ("y", "x")).reshape(half, width)
    far = pair(near)

    out, d_pre, d_agg, keep, pair_send = call(
        middle_kernel, "forward_backward",
        [
            ((seeds, width), BF16),
            ((seeds, width), BF16),
            ((seeds, width), BF16),
            ((width + half + 16, width), BF16),
            ((width + half + 16, width), BF16),
        ],
        [core],
        [
            near, far, near_adj, near_adj_t, far_adj, far_adj_t,
            chosen_t, preact, part, w_neigh, cotangent,
        ],
        flops=2 * seeds * width * (4 * half + 4 * width),
    )

    pair_arrived = pair(pair_send)
    (own,) = call(
        own_back_kernel, "own_rows_back", [((rows, width), F32)],
        [*tile_scalars], [tiles, seed_row, d_pre, d_agg, w_self],
        scratch=[pltpu.VMEM((seeds, rows), BF16)],
        flops=2 * seeds * width * 3 * rows,
    )
    (plane_send,) = call(
        pair_sum_kernel, "sum_pair",
        [((PLANE, width // PLANE + 2 * depth + 8, width), BF16)],
        [], [keep, pair_arrived], after=[own],
    )
    plane_arrived = swap(plane_send, ("y", "x"))
    (depth_send,) = call(
        plane_sum_kernel, "sum_plane",
        [((depth, 2 * Y_SIZE, width + 2 * LANES), BF16)],
        [], [plane_arrived],
    )
    depth_arrived = swap(depth_send, "z")
    weight_send, bias_rows = call(
        functools.partial(weight_kernel, scale), "sum_weights",
        [((depth, 2 * Y_SIZE, LANES), BF16), ((2 * Y_SIZE, LANES), F32)],
        [], [depth_arrived],
    )
    weight_depth = swap(weight_send, "z")
    share = rows // reps
    row_keep, row_send = call(
        scatter_kernel, "return_rows",
        [((X_SIZE, share, width), BF16), ((X_SIZE, share, width), BF16)],
        [rep], [lists, depth_arrived, own],
        scratch=[pltpu.VMEM((rows, width), BF16)],
        flops=4 * parts * rows * width, after=[weight_send],
    )
    row_pair = row_keep.astype(F32) + pair(row_send).astype(F32)
    rows_out = row_pair.astype(BF16)
    (weight_plane,) = call(
        gather_kernel, "gather_weights",
        [((PLANE, width // PLANE, width), BF16)],
        [], [weight_depth], after=[rows_out], flops=20_000_000_000,
    )
    weight_near = swap(weight_plane, ("y", "x")).reshape(width, width)
    far_half = lax.ppermute(rows_out[2:], "x", [(x, x ^ 2) for x in range(X_SIZE)])
    row_half = row_pair[:2] + far_half.astype(F32)
    beside = lax.ppermute(row_half[1].astype(BF16), "x", [(x, x ^ 1) for x in range(X_SIZE)])
    input_grad = row_half[0] + beside.astype(F32)
    (weight_send,) = call(
        copy_kernel, "hand_on", [((width, width), BF16)], [], [weight_near], after=[input_grad]
    )
    weight_far = pair(weight_send)
    grad_self = jnp.where(core_id == 0, weight_near, weight_far)
    grad_neigh = jnp.where(core_id == 0, weight_far, weight_near)
    groups = width // LANES
    grad_bias = bias_rows[: 2 * groups].reshape(groups, 2, LANES).sum(1).reshape(width)

    return (out, input_grad, grad_self, grad_neigh, grad_bias)


def solution(mesh):
    parts = mesh.shape["dom"]
    physical = Mesh(
        mesh.devices.reshape(parts // Y_SIZE, Y_SIZE, X_SIZE, CORES), ("z", "y", "x", "core")
    )
    dom = ("z", "y")
    every = ("z", "y", "x", "core")
    placed = (
        P(dom, None),
        P(dom, None, None),
        P(every),
        P(every, None, None),
        P(every, None),
        P(every, None),
        P(every),
        P(),
        P(),
        P(),
        P(every, None),
    )
    return jax.shard_map(
        body,
        mesh=physical,
        in_specs=placed,
        out_specs=(P(every, None), P(every, None), P(), P(), P()),
        check_vma=False,
    )
```

```python
import functools
import math

import jax
import jax.numpy as jnp
from jax import lax
from jax.experimental import pallas as pl
from jax.experimental.pallas import tpu as pltpu
from jax.sharding import Mesh
from jax.sharding import PartitionSpec as P

BLK = 128
LANES = 128
SLOTS = 8
X_SIZE = 4
CORES = 2
Y_SIZE = 4
PLANE = Y_SIZE * X_SIZE
BF16 = jnp.bfloat16
F32 = jnp.float32
VMEM_BYTES = 24 * 1024 * 1024
FULL_VMEM_BYTES = 65 * 1000 * 1024


def dot(a, b, contract_a=1, contract_b=0):
    return lax.dot_general(
        a, b, (((contract_a,), (contract_b,)), ((), ())), preferred_element_type=F32
    )


def move(matrix, rows):
    return dot(matrix.astype(BF16), rows).astype(BF16)


def iota(shape, dim):
    return lax.broadcasted_iota(jnp.int32, shape, dim)


def split(wide):
    high = wide.astype(BF16)
    return high, (wide - high.astype(F32)).astype(BF16)


def call(kernel, name, outs, scalars, arrays, scratch=(), flops=0, after=(), hbm=(), hbm_outs=(), limit=VMEM_BYTES):
    if after:
        inner, at = kernel, len(scalars) + len(arrays) + len(hbm)
        kernel = lambda *refs: inner(*refs[:at], *refs[at + len(after) :])
    shapes = tuple(jax.ShapeDtypeStruct(shape, dtype) for shape, dtype in outs)
    shapes += tuple(pltpu.HBM(shape, dtype) for shape, dtype in hbm_outs)
    size = sum(math.prod(a.shape) * a.dtype.itemsize for a in (*arrays, *hbm, *shapes))
    return pl.pallas_call(
        kernel,
        out_shape=shapes,
        in_specs=[pl.BlockSpec(memory_space=pltpu.SMEM)] * len(scalars)
        + [pl.BlockSpec(memory_space=pltpu.VMEM)] * len(arrays)
        + [pl.BlockSpec(memory_space=pltpu.HBM)] * len(hbm)
        + [pl.BlockSpec(memory_space=pl.ANY)] * len(after),
        out_specs=tuple([pl.BlockSpec(memory_space=pltpu.VMEM)] * len(outs))
        + tuple([pl.BlockSpec(memory_space=pltpu.HBM)] * len(hbm_outs)),
        scratch_shapes=list(scratch),
        compiler_params=pltpu.CompilerParams(vmem_limit_bytes=limit),
        cost_estimate=pl.CostEstimate(flops=flops, bytes_accessed=size, transcendentals=0),
        name=name,
    )(*scalars, *arrays, *hbm, *after)


def fetched(arrays):
    return [pltpu.VMEM(a.shape, a.dtype) for a in arrays] + [
        pltpu.SemaphoreType.DMA((len(arrays),))
    ]


def fetch(from_refs, to_refs, sems):
    copies = [
        pltpu.make_async_copy(source, to, sems.at[at])
        for at, (source, to) in enumerate(zip(from_refs, to_refs))
    ]
    for copy in copies:
        copy.start()
    return copies


def place_tiles(dst_ref, src_ref, count_ref, tiles_ref, adj_ref, first, last):
    adj_ref[...] = jnp.zeros_like(adj_ref)

    def step(slot, carry):
        block = src_ref[0, slot]

        @pl.when(jnp.logical_and(block >= first, block < last))
        def _():
            row = pl.multiple_of(dst_ref[0, slot] * BLK, BLK)
            col = pl.multiple_of((block - first) * BLK, BLK)
            adj_ref[pl.ds(row, BLK), pl.ds(col, BLK)] = tiles_ref[slot]

        return carry

    lax.fori_loop(0, count_ref[0], step, 0)


def boundary_places(rep, lists_ref, rows):
    slots, parts = lists_ref.shape
    lists = lists_ref[...].astype(F32)
    wanted = jnp.sum(
        jnp.where(iota((slots, parts), 0) == rep, lists, 0.0), axis=0, keepdims=True
    ).astype(jnp.int32)
    place = iota((rows, parts), 0)
    places = jnp.concatenate([(place == wanted).astype(BF16), (place == rep).astype(BF16)], 1)
    return dot(places, by_z(parts).astype(BF16), 1, 1).astype(BF16)


def by_z(parts):
    shape = (2 * parts, 2 * parts)
    out, into = iota(shape, 0), iota(shape, 1)
    y, kind, z = out % Y_SIZE, out // Y_SIZE % 2, out // (2 * Y_SIZE)
    return into == kind * parts + z * Y_SIZE + y


def send_kernel(rep_ref, lists_hbm, feats_hbm, send_ref, lists_ref, feats_ref, sems):
    lists_copy, feats_copy = fetch((lists_hbm, feats_hbm), (lists_ref, feats_ref), sems)
    lists_copy.wait()
    places = boundary_places(rep_ref[0], lists_ref, feats_ref.shape[0])
    feats_copy.wait()
    send_ref[...] = dot(places, feats_ref[...], 0, 0).astype(BF16)


def plane_kernel(arrived_ref, send_ref):
    chunk = send_ref.shape[1]
    depth = chunk // 2
    total = arrived_ref.shape[0]
    shape = (total, total)
    out, into = iota(shape, 0), iota(shape, 1)
    z, kind, y = out % depth, out // depth % 2, out // chunk
    moved = move(into == z * (2 * Y_SIZE) + kind * Y_SIZE + y, arrived_ref[...])
    for y_to in range(Y_SIZE):
        for x_to in range(X_SIZE):
            send_ref[y_to * X_SIZE + x_to] = moved[y_to * chunk : (y_to + 1) * chunk]


def own_kernel(
    at_ref, dst_ref, src_ref, count_ref, tiles_ref, feats_ref, seeds_ref, w_self_ref, bias_ref,
    lists_ref, mats_ref, sums_ref, places_ref, own_adj_ref, adj_ref,
):
    rows = feats_ref.shape[0]
    seeds = seeds_ref.shape[1]
    own_blocks = rows // BLK
    table = adj_ref.shape[1]
    place_tiles(dst_ref, src_ref, count_ref, tiles_ref, own_adj_ref, 0, own_blocks)
    place_tiles(
        dst_ref, src_ref, count_ref, tiles_ref, adj_ref, own_blocks, own_blocks + table // BLK
    )
    picks = (iota((rows, seeds), 0) == seeds_ref[...]).astype(BF16)
    feats = feats_ref[...]
    mats_ref[2 * seeds : 2 * seeds + feats.shape[1], :seeds] = dot(feats, picks, 0, 0).astype(BF16)
    chosen = dot(picks, feats, 0, 0).astype(BF16)
    sums_ref[:seeds] = dot(chosen, w_self_ref[...]) + bias_ref[...].astype(F32)
    sums_ref[seeds:] = dot(own_adj_ref[...], feats)
    adj = adj_ref[...]
    half = table // 2
    depth = half // PLANE // 2
    at_x, at_core = at_ref[0], at_ref[1]

    shape = (half, table)
    line, source = iota(shape, 0), iota(shape, 1)
    z, kind = line % depth, line // depth % 2
    x, y = line // (2 * depth) % X_SIZE, line // (2 * depth * X_SIZE)
    start = kind * half + (z * Y_SIZE + y) * SLOTS + x * CORES
    for far, core in enumerate((at_core, 1 - at_core)):
        order = (source == start + core).astype(BF16)
        mats_ref[far * seeds : (far + 1) * seeds, :half] = dot(adj, order, 1, 1).astype(BF16)

    parts = half // SLOTS
    share = 2 * parts
    for x_step in range(X_SIZE):
        for core_step in range(CORES):
            shape = (share, table)
            line, source = iota(shape, 0), iota(shape, 1)
            y, kind, z = line % Y_SIZE, line // Y_SIZE % 2, line // (2 * Y_SIZE)
            slot = jnp.bitwise_xor(at_x, x_step) * CORES + jnp.bitwise_xor(at_core, core_step)
            order = source == kind * half + (z * Y_SIZE + y) * SLOTS + slot
            first = 2 * seeds + feats.shape[1] + (x_step * CORES + core_step) * share
            mats_ref[first : first + share, :seeds] = dot(order.astype(BF16), adj, 1, 1).astype(BF16)

    lists = lists_ref[...]
    high, low = (lists // 256).astype(BF16), (lists % 256).astype(BF16)
    shape = (parts, half)
    line = iota(shape, 1)
    of_part = (
        iota(shape, 0) == line % depth * Y_SIZE + line // (2 * depth * X_SIZE)
    ).astype(BF16)
    wanted = (dot(high, of_part) * 256.0 + dot(low, of_part)).astype(jnp.int32)
    line = iota((SLOTS, half), 1)
    slot = line // (2 * depth) % X_SIZE * CORES
    wanted = jnp.where(line // depth % 2 == 1, iota((SLOTS, half), 0), wanted)
    own_rows = places_ref.shape[1]
    place = iota((own_rows, half), 0) + (at_x * CORES + at_core) * own_rows
    for far, core in enumerate((at_core, 1 - at_core)):
        here = iota((SLOTS, half), 0) == slot + core
        row = jnp.sum(jnp.where(here, wanted.astype(F32), 0.0), axis=0, keepdims=True)
        places_ref[far] = (place == row.astype(jnp.int32)).astype(BF16)


def middle_kernel(
    at_ref, near_ref, far_ref, mats_ref, sums_ref, w_neigh_ref, cot_ref,
    out_ref, keep_ref, send_ref, x_keep_ref, x_send_ref, d_both_hbm, d_both_ref, sem,
):
    seeds, width = cot_ref.shape
    half = near_ref.shape[0]
    back = 2 * seeds + width
    aggregate = (
        sums_ref[seeds:]
        + dot(mats_ref[:seeds, :half], near_ref[...])
        + dot(mats_ref[seeds : 2 * seeds, :half], far_ref[...])
    ).astype(BF16)
    preact = sums_ref[:seeds] + dot(aggregate, w_neigh_ref[...])
    gate = jax.nn.sigmoid(preact)
    out_ref[...] = (preact * gate).astype(BF16)
    d_pre = (cot_ref[...].astype(F32) * gate * (1.0 + preact * (1.0 - gate))).astype(BF16)
    d_agg = dot(d_pre, w_neigh_ref[...], 1, 1).astype(BF16)
    d_both_ref[0] = d_pre
    d_both_ref[1] = d_agg
    kept = pltpu.make_async_copy(d_both_ref, d_both_hbm, sem)
    kept.start()
    first = dot(mats_ref[2 * seeds : back, :seeds], d_pre).astype(BF16)
    second = dot(aggregate, d_pre, 0, 0).astype(BF16)
    is_first = at_ref[1] == 0
    keep_ref[:width] = jnp.where(is_first, first, second)
    send_ref[:width] = jnp.where(is_first, second, first)
    high, low = split(jnp.sum(d_pre.astype(F32), 0, keepdims=True))
    pair = two_rows(high, low, keep_ref.shape[0] - width)
    keep_ref[width:] = pair
    send_ref[width:] = pair
    x_keep_ref[...] = dot(mats_ref[back : back + half, :seeds], d_agg)
    x_send_ref[...] = dot(mats_ref[back + half :, :seeds], d_agg).astype(BF16)
    kept.wait()


def two_rows(high, low, rows):
    row = iota((rows, high.shape[1]), 0)
    high, low = high.astype(F32), low.astype(F32)
    return jnp.where(row == 0, high, jnp.where(row == 1, low, 0.0)).astype(BF16)


def halve_kernel(keep_ref, other_ref, next_keep_ref, next_send_ref):
    half = next_keep_ref.shape[0]
    next_keep_ref[...] = keep_ref[:half] + other_ref[:half].astype(F32)
    next_send_ref[...] = (keep_ref[half:] + other_ref[half:].astype(F32)).astype(BF16)


def pair_sum_kernel(keep_ref, other_ref, send_ref):
    chunks, lines, width = send_ref.shape
    total = keep_ref[...].astype(F32) + other_ref[...].astype(F32)
    weight = width // chunks
    high, low = split(total[width : width + 1] + total[width + 1 : width + 2])
    pair = two_rows(high, low, lines - weight).astype(F32)
    for chunk in range(chunks):
        send_ref[chunk] = jnp.concatenate(
            [total[chunk * weight : (chunk + 1) * weight], pair], 0
        ).astype(BF16)


def plane_sum_kernel(arrived_ref, send_ref):
    chunks, lines, width = arrived_ref.shape
    depth, block, _ = send_ref.shape
    weight = width // chunks
    groups = width // LANES
    each = weight // depth
    total = arrived_ref[0].astype(F32)
    for chunk in range(1, chunks):
        total = total + arrived_ref[chunk].astype(F32)
    weights = total[:weight].astype(BF16)
    high, low = split(total[weight : weight + 1] + total[weight + 1 : weight + 2])
    pair = two_rows(high, low, 16)
    shape = (depth * block, weight)
    out, into = iota(shape, 0), iota(shape, 1)
    line, z = out % block, out // block
    pair_shape = (depth * block, 16)
    pair_line, pair_into = iota(pair_shape, 0) % block, iota(pair_shape, 1)
    weight_block = jnp.zeros((depth * block, LANES), F32)
    bias_block = jnp.zeros((depth * block, LANES), F32)
    for group in range(groups):
        lanes = slice(group * LANES, (group + 1) * LANES)
        here = jnp.logical_and(line // each == group, into == z * each + line % each)
        weight_block += dot(here.astype(BF16), weights[:, lanes])
        here = jnp.logical_and(pair_line // 2 == group, pair_into == pair_line % 2)
        bias_block += dot(here.astype(BF16), pair[:, lanes])
    send_ref[:, :, :LANES] = weight_block.astype(BF16).reshape(depth, block, LANES)
    send_ref[:, :, LANES:] = bias_block.astype(BF16).reshape(depth, block, LANES)


def weight_kernel(scale, arrived_ref, done_ref, bias_ref):
    total = jnp.sum(arrived_ref[...].astype(F32), 0) * scale
    done_ref[...] = total[:, :LANES]
    bias_ref[...] = total[:, LANES:]


def pack_kernel(done_ref, keep_ref, other_ref, send_ref):
    depth, block, lanes = send_ref.shape
    width = lanes - LANES
    back = (keep_ref[...] + other_ref[...].astype(F32)).astype(BF16)
    send_ref[:, :, :width] = back.reshape(depth, block, width)
    done = done_ref[...].astype(BF16)
    for z in range(depth):
        send_ref[z, :, width:] = done


def gather_kernel(arrived_ref, send_ref):
    chunks, lines, width = send_ref.shape
    depth, block, _ = arrived_ref.shape
    groups = width // LANES
    weight = width // chunks
    each = weight // depth
    total = depth * block
    arrived = arrived_ref[:, :, width:].reshape(total, LANES)
    shape = (weight, total)
    out, into = iota(shape, 0), iota(shape, 1)
    z, line = out // each, out % each
    whole = jnp.concatenate(
        [move(into == z * block + group * each + line, arrived) for group in range(groups)], 1
    )
    back = arrived_ref[:, :, :width].reshape(total, width)
    shape = (total, total)
    out, into = iota(shape, 0), iota(shape, 1)
    z, kind, y = out % depth, out // depth % 2, out // (2 * depth)
    moved = move(into == z * block + kind * Y_SIZE + y, back)
    for y_to in range(Y_SIZE):
        for x_to in range(X_SIZE):
            chunk = y_to * X_SIZE + x_to
            send_ref[chunk, :weight] = whole
            send_ref[chunk, weight:] = moved[y_to * 2 * depth : (y_to + 1) * 2 * depth]


def own_back_kernel(
    at_ref, dst_ref, src_ref, count_ref, tiles_ref, seeds_ref, d_both_ref, w_self_ref,
    keep_ref, send_ref, adj_ref, own_ref,
):
    rows = own_ref.shape[0]
    seeds = seeds_ref.shape[1]
    place_tiles(dst_ref, src_ref, count_ref, tiles_ref, adj_ref, 0, rows // BLK)
    picks = (iota((rows, seeds), 0) == seeds_ref[...]).astype(BF16)
    seeded = dot(picks, d_both_ref[0]).astype(BF16)
    own_ref[...] = dot(seeded, w_self_ref[...], 1, 1) + dot(adj_ref[...], d_both_ref[1], 0, 0)
    share = rows // (X_SIZE * CORES)
    for step in range(X_SIZE):
        keep = jnp.bitwise_xor(at_ref[0], step) * CORES + at_ref[1]
        send = jnp.bitwise_xor(keep, 1)
        keep_ref[step] = own_ref[pl.ds(pl.multiple_of(keep * share, 32), share), :]
        send_ref[step] = own_ref[pl.ds(pl.multiple_of(send * share, 32), share), :].astype(BF16)


def copy_kernel(from_ref, to_ref):
    to_ref[...] = from_ref[...]


def finish_kernel(
    at_ref, near_ref, far_ref, places_ref, own_ref, rows_ref, first_ref, second_ref,
):
    chunks, lines, width = near_ref.shape
    weight = width // chunks
    near, far = near_ref[:, :weight].reshape(width, width), far_ref[:, :weight].reshape(width, width)
    is_first = at_ref[1] == 0
    first_ref[...] = jnp.where(is_first, near, far)
    second_ref[...] = jnp.where(is_first, far, near)
    total = chunks * (lines - weight)
    rows_ref[...] = (
        own_ref[...]
        + dot(places_ref[0], near_ref[:, weight:].reshape(total, width))
        + dot(places_ref[1], far_ref[:, weight:].reshape(total, width))
    )


def body(
    feats,
    halo_index,
    seed_ids,
    tiles,
    tile_dst,
    tile_src,
    tile_count,
    w_self,
    w_neigh,
    bias,
    cotangent,
):
    depth = lax.axis_size("z")
    parts = depth * Y_SIZE
    reps = X_SIZE * CORES
    rows, width = feats.shape
    seeds = cotangent.shape[0]
    half = parts * SLOTS
    core_id = lax.axis_index("core").astype(jnp.int32)
    x_id = lax.axis_index("x").astype(jnp.int32)
    at = jnp.stack([x_id, core_id])
    rep = (x_id * CORES + core_id).reshape(1)
    lists = halo_index[0].T
    seed_row = seed_ids.reshape(1, seeds)
    tile_scalars = (tile_dst, tile_src, tile_count)
    scale = float(seeds * parts * reps) ** (-0.5)
    weight = width // PLANE
    share = rows // reps
    window = 20_000_000_000

    def swap(values, axis):
        return lax.all_to_all(values, axis, split_axis=0, concat_axis=0, tiled=True)

    def pair(values):
        return lax.ppermute(values, "core", [(0, 1), (1, 0)])

    def cross(values, step):
        return lax.ppermute(values, "x", [(x, x ^ step) for x in range(X_SIZE)])

    (send,) = call(
        send_kernel, "pick_boundary", [((2 * parts, width), BF16)], [rep], [], hbm=[lists, feats],
        scratch=fetched([lists, feats]), flops=4 * parts * rows * width, limit=FULL_VMEM_BYTES,
    )
    by_depth = swap(send.reshape(depth, 2 * Y_SIZE, width), "z").reshape(2 * parts, width)
    mats, sums, places = call(
        own_kernel, "own_rows",
        [
            ((2 * seeds + width + 2 * half, max(seeds, half)), BF16),
            ((2 * seeds, width), F32),
            ((CORES, share, half), BF16),
        ],
        [at, *tile_scalars],
        [tiles, feats, seed_row, w_self, bias.reshape(1, width), lists],
        scratch=[pltpu.VMEM((seeds, rows), BF16), pltpu.VMEM((seeds, 2 * half), BF16)],
        flops=2 * seeds * (3 * rows * width + width * width + 8 * half * half),
    )
    (plane,) = call(
        plane_kernel, "spread_plane", [((PLANE, 2 * depth, width), BF16)], [], [by_depth],
        flops=8 * parts * parts * width, after=[sums],
    )
    near = swap(plane, ("y", "x")).reshape(half, width)
    far = pair(near)

    out, keep, pair_send, x_keep, x_send, d_both = call(
        middle_kernel, "forward_backward",
        [
            ((seeds, width), BF16),
            ((width + 16, width), BF16),
            ((width + 16, width), BF16),
            ((half, width), F32),
            ((half, width), BF16),
        ],
        [at],
        [near, far, mats, sums, w_neigh, cotangent],
        hbm_outs=[((2, seeds, width), BF16)],
        scratch=[pltpu.VMEM((2, seeds, width), BF16), pltpu.SemaphoreType.DMA],
        flops=2 * seeds * width * (4 * half + 4 * width),
    )

    (plane_send,) = call(
        pair_sum_kernel, "sum_pair", [((PLANE, weight + 8, width), BF16)],
        [], [keep, pair(pair_send)],
    )
    plane_arrived = swap(plane_send, ("y", "x"))
    x_keep, x_send = call(
        halve_kernel, "halve_x", [((half // 2, width), F32), ((half // 2, width), BF16)],
        [], [x_keep, cross(x_send, 2)],
    )
    row_keep, row_send = call(
        own_back_kernel, "own_rows_back",
        [((X_SIZE, share, width), F32), ((X_SIZE, share, width), BF16)],
        [at, *tile_scalars], [tiles, seed_row, d_both, w_self],
        scratch=[pltpu.VMEM((seeds, rows), BF16), pltpu.VMEM((rows, width), F32)],
        flops=2 * seeds * width * 3 * rows,
    )
    (depth_send,) = call(
        plane_sum_kernel, "sum_plane", [((depth, 2 * Y_SIZE, 2 * LANES), BF16)],
        [], [plane_arrived], after=[x_send, row_send], flops=window,
    )
    depth_arrived = swap(depth_send, "z")
    core_keep, core_send = call(
        halve_kernel, "halve_core", [((half // 4, width), F32), ((half // 4, width), BF16)],
        [], [x_keep, cross(x_send, 1)],
    )
    weight_done, bias_rows = call(
        functools.partial(weight_kernel, scale), "sum_weights",
        [((2 * Y_SIZE, LANES), F32), ((2 * Y_SIZE, LANES), F32)],
        [], [depth_arrived], after=[core_send], flops=window,
    )

    (depth_send,) = call(
        pack_kernel, "pack_depth", [((depth, 2 * Y_SIZE, width + LANES), BF16)],
        [], [weight_done, core_keep, pair(core_send)],
    )
    depth_arrived = swap(depth_send, "z")
    row_pair = row_keep + pair(row_send).astype(F32)
    rows_out = row_pair[2:].astype(BF16)
    (plane_send,) = call(
        gather_kernel, "gather_depth", [((PLANE, weight + 2 * depth, width), BF16)],
        [], [depth_arrived], after=[rows_out], flops=window,
    )
    near = swap(plane_send, ("y", "x"))
    row_half = row_pair[:2] + cross(rows_out, 2).astype(F32)
    own = row_half[0] + cross(row_half[1].astype(BF16), 1).astype(F32)
    (near_send,) = call(
        copy_kernel, "hand_on", [(near.shape, BF16)], [], [near], after=[own]
    )
    input_grad, grad_self, grad_neigh = call(
        finish_kernel, "finish",
        [((share, width), F32), ((width, width), BF16), ((width, width), BF16)],
        [at], [near, pair(near_send), places, own],
        flops=4 * share * half * width,
    )
    groups = width // LANES
    grad_bias = bias_rows[: 2 * groups].reshape(groups, 2, LANES).sum(1).reshape(width)
    return (out, input_grad, grad_self, grad_neigh, grad_bias)


def solution(mesh):
    parts = mesh.shape["dom"]
    physical = Mesh(
        mesh.devices.reshape(parts // Y_SIZE, Y_SIZE, X_SIZE, CORES), ("z", "y", "x", "core")
    )
    dom = ("z", "y")
    every = ("z", "y", "x", "core")
    placed = (
        P(dom, None),
        P(dom, None, None),
        P(every),
        P(every, None, None),
        P(every, None),
        P(every, None),
        P(every),
        P(),
        P(),
        P(),
        P(every, None),
    )
    return jax.shard_map(
        body,
        mesh=physical,
        in_specs=placed,
        out_specs=(P(every, None), P(every, None), P(), P(), P()),
        check_vma=False,
    )
```

```python
import functools
import math

import jax
import jax.numpy as jnp
from jax import lax
from jax.experimental import pallas as pl
from jax.experimental.pallas import tpu as pltpu
from jax.sharding import Mesh
from jax.sharding import PartitionSpec as P

BLK = 128
LANES = 128
SLOTS = 8
X_SIZE = 4
CORES = 2
Y_SIZE = 4
PLANE = Y_SIZE * X_SIZE
BF16 = jnp.bfloat16
F32 = jnp.float32
VMEM_BYTES = 24 * 1024 * 1024
FULL_VMEM_BYTES = 65 * 1000 * 1024


def dot(a, b, contract_a=1, contract_b=0):
    return lax.dot_general(
        a, b, (((contract_a,), (contract_b,)), ((), ())), preferred_element_type=F32
    )


def move(matrix, rows):
    return dot(matrix.astype(BF16), rows).astype(BF16)


def iota(shape, dim):
    return lax.broadcasted_iota(jnp.int32, shape, dim)


def split(wide):
    high = wide.astype(BF16)
    return high, (wide - high.astype(F32)).astype(BF16)


def call(kernel, name, outs, scalars, arrays, scratch=(), flops=0, after=(), hbm=(), hbm_outs=(), limit=VMEM_BYTES):
    if after:
        inner, at = kernel, len(scalars) + len(arrays) + len(hbm)
        kernel = lambda *refs: inner(*refs[:at], *refs[at + len(after) :])
    shapes = tuple(jax.ShapeDtypeStruct(shape, dtype) for shape, dtype in outs)
    shapes += tuple(pltpu.HBM(shape, dtype) for shape, dtype in hbm_outs)
    size = sum(math.prod(a.shape) * a.dtype.itemsize for a in (*arrays, *hbm, *shapes))
    return pl.pallas_call(
        kernel,
        out_shape=shapes,
        in_specs=[pl.BlockSpec(memory_space=pltpu.SMEM)] * len(scalars)
        + [pl.BlockSpec(memory_space=pltpu.VMEM)] * len(arrays)
        + [pl.BlockSpec(memory_space=pltpu.HBM)] * len(hbm)
        + [pl.BlockSpec(memory_space=pl.ANY)] * len(after),
        out_specs=tuple([pl.BlockSpec(memory_space=pltpu.VMEM)] * len(outs))
        + tuple([pl.BlockSpec(memory_space=pltpu.HBM)] * len(hbm_outs)),
        scratch_shapes=list(scratch),
        compiler_params=pltpu.CompilerParams(vmem_limit_bytes=limit),
        cost_estimate=pl.CostEstimate(flops=flops, bytes_accessed=size, transcendentals=0),
        name=name,
    )(*scalars, *arrays, *hbm, *after)


def fetched(arrays):
    return [pltpu.VMEM(a.shape, a.dtype) for a in arrays] + [
        pltpu.SemaphoreType.DMA((len(arrays),))
    ]


def fetch(from_refs, to_refs, sems):
    copies = [
        pltpu.make_async_copy(source, to, sems.at[at])
        for at, (source, to) in enumerate(zip(from_refs, to_refs))
    ]
    for copy in copies:
        copy.start()
    return copies


def place_tiles(dst_ref, src_ref, count_ref, tiles_ref, adj_ref, first, last):
    adj_ref[...] = jnp.zeros_like(adj_ref)

    def step(slot, carry):
        block = src_ref[0, slot]

        @pl.when(jnp.logical_and(block >= first, block < last))
        def _():
            row = pl.multiple_of(dst_ref[0, slot] * BLK, BLK)
            col = pl.multiple_of((block - first) * BLK, BLK)
            adj_ref[pl.ds(row, BLK), pl.ds(col, BLK)] = tiles_ref[slot]

        return carry

    lax.fori_loop(0, count_ref[0], step, 0)


def boundary_places(rep, lists_ref, rows, order):
    slots, parts = lists_ref.shape
    lists = lists_ref[...].astype(F32)
    wanted = jnp.sum(
        jnp.where(iota((slots, parts), 0) == rep, lists, 0.0), axis=0, keepdims=True
    ).astype(jnp.int32)
    place = iota((rows, parts), 0)
    places = jnp.concatenate([(place == wanted).astype(BF16), (place == rep).astype(BF16)], 1)
    return dot(places, order.astype(BF16), 1, 1).astype(BF16)


def by_z(parts):
    shape = (2 * parts, 2 * parts)
    out, into = iota(shape, 0), iota(shape, 1)
    y, kind, z = out % Y_SIZE, out // Y_SIZE % 2, out // (2 * Y_SIZE)
    return into == kind * parts + z * Y_SIZE + y


def summed_by_z(parts):
    shape = (2 * parts, 2 * parts)
    out, into = iota(shape, 0), iota(shape, 1)
    line, z = out % (2 * Y_SIZE), out // (2 * Y_SIZE)
    halo = jnp.logical_and(line < Y_SIZE, into == z * Y_SIZE + line)
    hub = jnp.logical_and(line == Y_SIZE, into == parts)
    return jnp.logical_or(halo, hub)


def send_kernel(rep_ref, lists_hbm, feats_hbm, send_ref, lists_ref, feats_ref, sems):
    lists_copy, feats_copy = fetch((lists_hbm, feats_hbm), (lists_ref, feats_ref), sems)
    lists_copy.wait()
    parts = lists_ref.shape[1]
    places = boundary_places(rep_ref[0], lists_ref, feats_ref.shape[0], by_z(parts))
    feats_copy.wait()
    send_ref[...] = dot(places, feats_ref[...], 0, 0).astype(BF16)


def plane_kernel(arrived_ref, send_ref):
    chunk = send_ref.shape[1]
    depth = chunk // 2
    total = arrived_ref.shape[0]
    shape = (total, total)
    out, into = iota(shape, 0), iota(shape, 1)
    z, kind, y = out % depth, out // depth % 2, out // chunk
    moved = move(into == z * (2 * Y_SIZE) + kind * Y_SIZE + y, arrived_ref[...])
    for y_to in range(Y_SIZE):
        for x_to in range(X_SIZE):
            send_ref[y_to * X_SIZE + x_to] = moved[y_to * chunk : (y_to + 1) * chunk]


def own_kernel(
    core_ref, dst_ref, src_ref, count_ref, tiles_ref, feats_ref, seeds_ref, w_self_ref, bias_ref,
    mats_ref, sums_ref, own_adj_ref, adj_ref,
):
    rows = feats_ref.shape[0]
    seeds = seeds_ref.shape[1]
    own_blocks = rows // BLK
    table = adj_ref.shape[1]
    place_tiles(dst_ref, src_ref, count_ref, tiles_ref, own_adj_ref, 0, own_blocks)
    place_tiles(
        dst_ref, src_ref, count_ref, tiles_ref, adj_ref, own_blocks, own_blocks + table // BLK
    )
    picks = (iota((rows, seeds), 0) == seeds_ref[...]).astype(BF16)
    feats = feats_ref[...]
    mats_ref[2 * seeds + adj_ref.shape[1] :, :seeds] = dot(feats, picks, 0, 0).astype(BF16)
    chosen = dot(picks, feats, 0, 0).astype(BF16)
    sums_ref[:seeds] = dot(chosen, w_self_ref[...]) + bias_ref[...].astype(F32)
    sums_ref[seeds:] = dot(own_adj_ref[...], feats)
    adj = adj_ref[...]
    half = table // 2
    depth = half // PLANE // 2
    shape = (half, table)
    line, source = iota(shape, 0), iota(shape, 1)
    z, kind = line % depth, line // depth % 2
    x, y = line // (2 * depth) % X_SIZE, line // (2 * depth * X_SIZE)
    start = kind * half + (z * Y_SIZE + y) * SLOTS + x * CORES
    for far, core in enumerate((core_ref[0], 1 - core_ref[0])):
        order = (source == start + core).astype(BF16)
        mats_ref[far * seeds : (far + 1) * seeds, :half] = dot(adj, order, 1, 1).astype(BF16)
        first = 2 * seeds + far * half
        mats_ref[first : first + half, :seeds] = dot(order, adj, 1, 1).astype(BF16)


def middle_kernel(
    core_ref, near_ref, far_ref, mats_ref, sums_ref, w_neigh_ref, cot_ref,
    out_ref, d_pre_ref, d_agg_ref, keep_ref, send_ref,
):
    width = w_neigh_ref.shape[0]
    half = near_ref.shape[0]
    seeds = cot_ref.shape[0]
    near_back, far_back, chosen_t = (2 * seeds + step * half for step in range(3))
    aggregate = (
        sums_ref[seeds:]
        + dot(mats_ref[:seeds, :half], near_ref[...])
        + dot(mats_ref[seeds : 2 * seeds, :half], far_ref[...])
    ).astype(BF16)
    preact = sums_ref[:seeds] + dot(aggregate, w_neigh_ref[...])
    gate = jax.nn.sigmoid(preact)
    out_ref[...] = (preact * gate).astype(BF16)
    d_pre = (cot_ref[...].astype(F32) * gate * (1.0 + preact * (1.0 - gate))).astype(BF16)
    d_pre_ref[...] = d_pre
    d_agg = dot(d_pre, w_neigh_ref[...], 1, 1).astype(BF16)
    d_agg_ref[...] = d_agg
    first = dot(mats_ref[chosen_t:, :seeds], d_pre).astype(BF16)
    second = dot(aggregate, d_pre, 0, 0).astype(BF16)
    is_first = core_ref[0] == 0
    keep_ref[:width] = jnp.where(is_first, first, second)
    send_ref[:width] = jnp.where(is_first, second, first)
    keep_ref[width : width + half] = dot(mats_ref[near_back:far_back, :seeds], d_agg).astype(BF16)
    send_ref[width : width + half] = dot(mats_ref[far_back:chosen_t, :seeds], d_agg).astype(BF16)
    high, low = split(jnp.sum(d_pre.astype(F32), 0, keepdims=True))
    row = iota((keep_ref.shape[0] - width - half, width), 0)
    pair = jnp.where(
        row == 0, high.astype(F32), jnp.where(row == 1, low.astype(F32), 0.0)
    ).astype(BF16)
    keep_ref[width + half :] = pair
    send_ref[width + half :] = pair


def pair_sum_kernel(keep_ref, other_ref, send_ref):
    chunks, lines, width = send_ref.shape
    total = keep_ref[...].astype(F32) + other_ref[...].astype(F32)
    weight, table = width // chunks, (lines - 8 - width // chunks)
    tail = width + chunks * table
    high, low = split(total[tail : tail + 1] + total[tail + 1 : tail + 2])
    row = iota((8, width), 0)
    pair = jnp.where(row == 0, high.astype(F32), jnp.where(row == 1, low.astype(F32), 0.0))
    for chunk in range(chunks):
        send_ref[chunk] = jnp.concatenate(
            [
                total[chunk * weight : (chunk + 1) * weight],
                total[width + chunk * table : width + (chunk + 1) * table],
                pair,
            ],
            0,
        ).astype(BF16)


def plane_sum_kernel(arrived_ref, send_ref):
    chunks, lines, width = arrived_ref.shape
    depth, block, _ = send_ref.shape
    weight = width // chunks
    each = weight // depth
    tail = weight + 2 * depth
    rows = []
    rest = None
    for y in range(Y_SIZE):
        some = arrived_ref[y * X_SIZE].astype(F32)
        for x in range(1, X_SIZE):
            some = some + arrived_ref[y * X_SIZE + x].astype(F32)
        rows.append(some[weight : weight + depth])
        rest = some if rest is None else rest + some
    bias = jnp.zeros((depth, width), F32) + jnp.sum(rest[tail:], 0, keepdims=True)
    rows += [rest[weight + depth : tail], rest[:weight], bias]
    rows = jnp.concatenate(rows, 0).astype(BF16)
    shape = (depth * block, rows.shape[0])
    out, into = iota(shape, 0), iota(shape, 1)
    line, z = out % block, out // block
    first = (Y_SIZE + 1) * depth
    of_weight = jnp.logical_and(line > Y_SIZE, line <= Y_SIZE + each)
    wanted = jnp.where(
        of_weight,
        first + z * each + line - Y_SIZE - 1,
        jnp.where(line <= Y_SIZE, line * depth, first + weight) + z,
    )
    send_ref[...] = move(into == wanted, rows).reshape(depth, block, width)


def weight_kernel(scale, arrived_ref, send_ref, bias_ref):
    depth, block, width = arrived_ref.shape
    total = jnp.sum(arrived_ref[...].astype(F32), 0) * scale
    each = block - Y_SIZE - 2
    row = iota((block, LANES), 0)
    done = jnp.zeros((block, LANES), F32)
    for group in range(width // LANES):
        for line in range(each):
            some = total[Y_SIZE + 1 + line : Y_SIZE + 2 + line, group * LANES : (group + 1) * LANES]
            done = jnp.where(row == group * each + line, some, done)
    done = done.astype(BF16)
    for z in range(depth):
        send_ref[z] = done
    bias_ref[...] = total[block - 1 :]


def gather_kernel(arrived_ref, send_ref):
    chunks, weight, width = send_ref.shape
    depth, block, _ = arrived_ref.shape
    groups = width // LANES
    each = weight // depth
    arrived = arrived_ref[...].reshape(depth * block, LANES)
    shape = (weight, depth * block)
    out, into = iota(shape, 0), iota(shape, 1)
    z, line = out // each, out % each
    parts = [
        move(into == z * block + group * each + line, arrived) for group in range(groups)
    ]
    whole = jnp.concatenate(parts, 1)
    for chunk in range(chunks):
        send_ref[chunk] = whole


def own_back_kernel(
    dst_ref, src_ref, count_ref, tiles_ref, seeds_ref, d_pre_ref, d_agg_ref, w_self_ref,
    own_ref, adj_ref,
):
    rows = own_ref.shape[0]
    seeds = seeds_ref.shape[1]
    place_tiles(dst_ref, src_ref, count_ref, tiles_ref, adj_ref, 0, rows // BLK)
    picks = (iota((rows, seeds), 0) == seeds_ref[...]).astype(BF16)
    seeded = dot(picks, d_pre_ref[...]).astype(BF16)
    own_ref[...] = dot(seeded, w_self_ref[...], 1, 1) + dot(adj_ref[...], d_agg_ref[...], 0, 0)


def scatter_kernel(rep_ref, lists_ref, arrived_ref, own_ref, keep_ref, send_ref, total_ref):
    rows, width = own_ref.shape
    rep = rep_ref[0]
    places = boundary_places(rep, lists_ref, rows, summed_by_z(lists_ref.shape[1]))
    back = arrived_ref[...].reshape(places.shape[1], width)
    total_ref[...] = (own_ref[...] + dot(places, back)).astype(BF16)
    share = rows // (X_SIZE * CORES)
    for step in range(X_SIZE):
        keep = jnp.bitwise_xor(rep, step * CORES)
        for place, ref in ((keep, keep_ref), (jnp.bitwise_xor(keep, 1), send_ref)):
            ref[step] = total_ref[pl.ds(pl.multiple_of(place * share, 32), share), :]


def copy_kernel(from_ref, to_ref):
    to_ref[...] = from_ref[...]


def body(
    feats,
    halo_index,
    seed_ids,
    tiles,
    tile_dst,
    tile_src,
    tile_count,
    w_self,
    w_neigh,
    bias,
    cotangent,
):
    depth = lax.axis_size("z")
    parts = depth * Y_SIZE
    reps = X_SIZE * CORES
    rows, width = feats.shape
    seeds = cotangent.shape[0]
    half = parts * SLOTS
    core_id = lax.axis_index("core").astype(jnp.int32)
    x_id = lax.axis_index("x").astype(jnp.int32)
    core = core_id.reshape(1)
    rep = (x_id * CORES + core_id).reshape(1)
    lists = halo_index[0].T
    seed_row = seed_ids.reshape(1, seeds)
    tile_scalars = (tile_dst, tile_src, tile_count)
    scale = float(seeds * parts * reps) ** (-0.5)

    def swap(values, axis):
        return lax.all_to_all(values, axis, split_axis=0, concat_axis=0, tiled=True)

    def pair(values):
        return lax.ppermute(values, "core", [(0, 1), (1, 0)])

    (send,) = call(
        send_kernel, "pick_boundary", [((2 * parts, width), BF16)], [rep], [], hbm=[lists, feats],
        scratch=fetched([lists, feats]), flops=4 * parts * rows * width, limit=FULL_VMEM_BYTES,
    )
    by_depth = swap(send.reshape(depth, 2 * Y_SIZE, width), "z").reshape(2 * parts, width)
    mats, sums = call(
        own_kernel, "own_rows",
        [
            ((2 * (seeds + half) + width, max(seeds, half)), BF16),
            ((2 * seeds, width), F32),
        ],
        [core, *tile_scalars],
        [tiles, feats, seed_row, w_self, bias.reshape(1, width)],
        scratch=[pltpu.VMEM((seeds, rows), BF16), pltpu.VMEM((seeds, 2 * half), BF16)],
        flops=2 * seeds * (3 * rows * width + width * width + 8 * half * half),
    )

    (plane,) = call(
        plane_kernel, "spread_plane", [((PLANE, 2 * depth, width), BF16)], [], [by_depth],
        flops=8 * parts * parts * width, after=[sums],
    )
    near = swap(plane, ("y", "x")).reshape(half, width)
    far = pair(near)

    out, d_pre, d_agg, keep, pair_send = call(
        middle_kernel, "forward_backward",
        [
            ((seeds, width), BF16),
            ((seeds, width), BF16),
            ((seeds, width), BF16),
            ((width + half + 16, width), BF16),
            ((width + half + 16, width), BF16),
        ],
        [core],
        [
            near, far, mats, sums, w_neigh, cotangent,
        ],
        flops=2 * seeds * width * (4 * half + 4 * width),
    )

    pair_arrived = pair(pair_send)
    (own,) = call(
        own_back_kernel, "own_rows_back", [((rows, width), F32)],
        [*tile_scalars], [tiles, seed_row, d_pre, d_agg, w_self],
        scratch=[pltpu.VMEM((seeds, rows), BF16)],
        flops=2 * seeds * width * 3 * rows,
    )
    (plane_send,) = call(
        pair_sum_kernel, "sum_pair",
        [((PLANE, width // PLANE + 2 * depth + 8, width), BF16)],
        [], [keep, pair_arrived], after=[own],
    )
    plane_arrived = swap(plane_send, ("y", "x"))
    (depth_send,) = call(
        plane_sum_kernel, "sum_plane",
        [((depth, 2 * Y_SIZE, width), BF16)],
        [], [plane_arrived],
    )
    depth_arrived = swap(depth_send, "z")
    weight_send, bias_row = call(
        functools.partial(weight_kernel, scale), "sum_weights",
        [((depth, 2 * Y_SIZE, LANES), BF16), ((1, width), F32)],
        [], [depth_arrived],
    )
    weight_depth = swap(weight_send, "z")
    share = rows // reps
    row_keep, row_send = call(
        scatter_kernel, "return_rows",
        [((X_SIZE, share, width), BF16), ((X_SIZE, share, width), BF16)],
        [rep], [lists, depth_arrived, own],
        scratch=[pltpu.VMEM((rows, width), BF16)],
        flops=4 * parts * rows * width, after=[weight_send],
    )
    row_pair = row_keep.astype(F32) + pair(row_send).astype(F32)
    rows_out = row_pair.astype(BF16)
    (weight_plane,) = call(
        gather_kernel, "gather_weights",
        [((PLANE, width // PLANE, width), BF16)],
        [], [weight_depth], flops=20_000_000_000,
    )
    weight_near = swap(weight_plane, ("y", "x")).reshape(width, width)
    input_grad = row_pair[0]
    for step in range(1, X_SIZE):
        beside = lax.ppermute(rows_out[step], "x", [(x, x ^ step) for x in range(X_SIZE)])
        input_grad = input_grad + beside.astype(F32)
    (weight_send,) = call(
        copy_kernel, "hand_on", [((width, width), BF16)], [], [weight_near], after=[input_grad]
    )
    weight_far = pair(weight_send)
    grad_self = jnp.where(core_id == 0, weight_near, weight_far)
    grad_neigh = jnp.where(core_id == 0, weight_far, weight_near)
    grad_bias = bias_row.reshape(width)
    return (out, input_grad, grad_self, grad_neigh, grad_bias)


def solution(mesh):
    parts = mesh.shape["dom"]
    physical = Mesh(
        mesh.devices.reshape(parts // Y_SIZE, Y_SIZE, X_SIZE, CORES), ("z", "y", "x", "core")
    )
    dom = ("z", "y")
    every = ("z", "y", "x", "core")
    placed = (
        P(dom, None),
        P(dom, None, None),
        P(every),
        P(every, None, None),
        P(every, None),
        P(every, None),
        P(every),
        P(),
        P(),
        P(),
        P(every, None),
    )
    return jax.shard_map(
        body,
        mesh=physical,
        in_specs=placed,
        out_specs=(P(every, None), P(every, None), P(), P(), P()),
        check_vma=False,
    )
```

```python
import functools
import math

import jax
import jax.numpy as jnp
from jax import lax
from jax.experimental import pallas as pl
from jax.experimental.pallas import tpu as pltpu
from jax.sharding import Mesh
from jax.sharding import PartitionSpec as P

BLK = 128
LANES = 128
SLOTS = 8
X_SIZE = 4
CORES = 2
Y_SIZE = 4
PLANE = Y_SIZE * X_SIZE
BF16 = jnp.bfloat16
F32 = jnp.float32
VMEM_BYTES = 24 * 1024 * 1024
FULL_VMEM_BYTES = 65 * 1000 * 1024


def dot(a, b, contract_a=1, contract_b=0):
    return lax.dot_general(
        a, b, (((contract_a,), (contract_b,)), ((), ())), preferred_element_type=F32
    )


def move(matrix, rows):
    return dot(matrix.astype(BF16), rows).astype(BF16)


def iota(shape, dim):
    return lax.broadcasted_iota(jnp.int32, shape, dim)


def split(wide):
    high = wide.astype(BF16)
    return high, (wide - high.astype(F32)).astype(BF16)


def call(kernel, name, outs, scalars, arrays, scratch=(), flops=0, after=(), hbm=(), hbm_outs=(), limit=VMEM_BYTES):
    if after:
        inner, at = kernel, len(scalars) + len(arrays) + len(hbm)
        kernel = lambda *refs: inner(*refs[:at], *refs[at + len(after) :])
    shapes = tuple(jax.ShapeDtypeStruct(shape, dtype) for shape, dtype in outs)
    shapes += tuple(pltpu.HBM(shape, dtype) for shape, dtype in hbm_outs)
    size = sum(math.prod(a.shape) * a.dtype.itemsize for a in (*arrays, *hbm, *shapes))
    return pl.pallas_call(
        kernel,
        out_shape=shapes,
        in_specs=[pl.BlockSpec(memory_space=pltpu.SMEM)] * len(scalars)
        + [pl.BlockSpec(memory_space=pltpu.VMEM)] * len(arrays)
        + [pl.BlockSpec(memory_space=pltpu.HBM)] * len(hbm)
        + [pl.BlockSpec(memory_space=pl.ANY)] * len(after),
        out_specs=tuple([pl.BlockSpec(memory_space=pltpu.VMEM)] * len(outs))
        + tuple([pl.BlockSpec(memory_space=pltpu.HBM)] * len(hbm_outs)),
        scratch_shapes=list(scratch),
        compiler_params=pltpu.CompilerParams(vmem_limit_bytes=limit),
        cost_estimate=pl.CostEstimate(flops=flops, bytes_accessed=size, transcendentals=0),
        name=name,
    )(*scalars, *arrays, *hbm, *after)


def fetched(arrays):
    return [pltpu.VMEM(a.shape, a.dtype) for a in arrays] + [
        pltpu.SemaphoreType.DMA((len(arrays),))
    ]


def fetch(from_refs, to_refs, sems):
    copies = [
        pltpu.make_async_copy(source, to, sems.at[at])
        for at, (source, to) in enumerate(zip(from_refs, to_refs))
    ]
    for copy in copies:
        copy.start()
    return copies


def place_tiles(dst_ref, src_ref, count_ref, tiles_ref, adj_ref, first, last):
    adj_ref[...] = jnp.zeros_like(adj_ref)

    def step(slot, carry):
        block = src_ref[0, slot]

        @pl.when(jnp.logical_and(block >= first, block < last))
        def _():
            row = pl.multiple_of(dst_ref[0, slot] * BLK, BLK)
            col = pl.multiple_of((block - first) * BLK, BLK)
            adj_ref[pl.ds(row, BLK), pl.ds(col, BLK)] = tiles_ref[slot]

        return carry

    lax.fori_loop(0, count_ref[0], step, 0)


def boundary_places(rep, lists_ref, rows, order):
    slots, parts = lists_ref.shape
    lists = lists_ref[...].astype(F32)
    wanted = jnp.sum(
        jnp.where(iota((slots, parts), 0) == rep, lists, 0.0), axis=0, keepdims=True
    ).astype(jnp.int32)
    place = iota((rows, parts), 0)
    places = jnp.concatenate([(place == wanted).astype(BF16), (place == rep).astype(BF16)], 1)
    return dot(places, order.astype(BF16), 1, 1).astype(BF16)


def by_z(parts):
    shape = (2 * parts, 2 * parts)
    out, into = iota(shape, 0), iota(shape, 1)
    y, kind, z = out % Y_SIZE, out // Y_SIZE % 2, out // (2 * Y_SIZE)
    return into == kind * parts + z * Y_SIZE + y


def summed_by_z(parts):
    shape = (2 * parts, 2 * parts)
    out, into = iota(shape, 0), iota(shape, 1)
    line, z = out % (2 * Y_SIZE), out // (2 * Y_SIZE)
    halo = jnp.logical_and(line < Y_SIZE, into == z * Y_SIZE + line)
    hub = jnp.logical_and(line == Y_SIZE, into == parts)
    return jnp.logical_or(halo, hub)


def send_kernel(rep_ref, lists_hbm, feats_hbm, send_ref, lists_ref, feats_ref, sems):
    lists_copy, feats_copy = fetch((lists_hbm, feats_hbm), (lists_ref, feats_ref), sems)
    lists_copy.wait()
    parts = lists_ref.shape[1]
    places = boundary_places(rep_ref[0], lists_ref, feats_ref.shape[0], by_z(parts))
    feats_copy.wait()
    send_ref[...] = dot(places, feats_ref[...], 0, 0).astype(BF16)


def plane_kernel(arrived_ref, send_ref):
    chunk = send_ref.shape[1]
    depth = chunk // 2
    total = arrived_ref.shape[0]
    shape = (total, total)
    out, into = iota(shape, 0), iota(shape, 1)
    z, kind, y = out % depth, out // depth % 2, out // chunk
    moved = move(into == z * (2 * Y_SIZE) + kind * Y_SIZE + y, arrived_ref[...])
    for y_to in range(Y_SIZE):
        for x_to in range(X_SIZE):
            send_ref[y_to * X_SIZE + x_to] = moved[y_to * chunk : (y_to + 1) * chunk]


def own_kernel(
    core_ref, dst_ref, src_ref, count_ref, tiles_ref, feats_ref, seeds_ref, w_self_ref, bias_ref,
    mats_ref, sums_ref, own_adj_ref, adj_ref,
):
    rows = feats_ref.shape[0]
    seeds = seeds_ref.shape[1]
    own_blocks = rows // BLK
    table = adj_ref.shape[1]
    place_tiles(dst_ref, src_ref, count_ref, tiles_ref, own_adj_ref, 0, own_blocks)
    place_tiles(
        dst_ref, src_ref, count_ref, tiles_ref, adj_ref, own_blocks, own_blocks + table // BLK
    )
    picks = (iota((rows, seeds), 0) == seeds_ref[...]).astype(BF16)
    feats = feats_ref[...]
    mats_ref[2 * seeds + adj_ref.shape[1] :, :seeds] = dot(feats, picks, 0, 0).astype(BF16)
    chosen = dot(picks, feats, 0, 0).astype(BF16)
    sums_ref[:seeds] = dot(chosen, w_self_ref[...]) + bias_ref[...].astype(F32)
    sums_ref[seeds:] = dot(own_adj_ref[...], feats)
    adj = adj_ref[...]
    half = table // 2
    depth = half // PLANE // 2
    shape = (half, table)
    line, source = iota(shape, 0), iota(shape, 1)
    z, kind = line % depth, line // depth % 2
    x, y = line // (2 * depth) % X_SIZE, line // (2 * depth * X_SIZE)
    start = kind * half + (z * Y_SIZE + y) * SLOTS + x * CORES
    for far, core in enumerate((core_ref[0], 1 - core_ref[0])):
        order = (source == start + core).astype(BF16)
        mats_ref[far * seeds : (far + 1) * seeds, :half] = dot(adj, order, 1, 1).astype(BF16)
        first = 2 * seeds + far * half
        mats_ref[first : first + half, :seeds] = dot(order, adj, 1, 1).astype(BF16)


def middle_kernel(
    core_ref, near_ref, far_ref, mats_ref, sums_ref, w_neigh_ref, cot_ref,
    out_ref, d_pre_ref, d_agg_ref, keep_ref, send_ref,
):
    width = w_neigh_ref.shape[0]
    half = near_ref.shape[0]
    seeds = cot_ref.shape[0]
    near_back, far_back, chosen_t = (2 * seeds + step * half for step in range(3))
    aggregate = (
        sums_ref[seeds:]
        + dot(mats_ref[:seeds, :half], near_ref[...])
        + dot(mats_ref[seeds : 2 * seeds, :half], far_ref[...])
    ).astype(BF16)
    preact = sums_ref[:seeds] + dot(aggregate, w_neigh_ref[...])
    gate = jax.nn.sigmoid(preact)
    out_ref[...] = (preact * gate).astype(BF16)
    d_pre = (cot_ref[...].astype(F32) * gate * (1.0 + preact * (1.0 - gate))).astype(BF16)
    d_pre_ref[...] = d_pre
    d_agg = dot(d_pre, w_neigh_ref[...], 1, 1).astype(BF16)
    d_agg_ref[...] = d_agg
    first = dot(mats_ref[chosen_t:, :seeds], d_pre).astype(BF16)
    second = dot(aggregate, d_pre, 0, 0).astype(BF16)
    is_first = core_ref[0] == 0
    keep_ref[:width] = jnp.where(is_first, first, second)
    send_ref[:width] = jnp.where(is_first, second, first)
    keep_ref[width : width + half] = dot(mats_ref[near_back:far_back, :seeds], d_agg).astype(BF16)
    send_ref[width : width + half] = dot(mats_ref[far_back:chosen_t, :seeds], d_agg).astype(BF16)
    high, low = split(jnp.sum(d_pre.astype(F32), 0, keepdims=True))
    row = iota((keep_ref.shape[0] - width - half, width), 0)
    pair = jnp.where(
        row == 0, high.astype(F32), jnp.where(row == 1, low.astype(F32), 0.0)
    ).astype(BF16)
    keep_ref[width + half :] = pair
    send_ref[width + half :] = pair


def pair_sum_kernel(keep_ref, other_ref, send_ref):
    chunks, lines, width = send_ref.shape
    total = keep_ref[...].astype(F32) + other_ref[...].astype(F32)
    weight, table = width // chunks, (lines - 8 - width // chunks)
    tail = width + chunks * table
    high, low = split(total[tail : tail + 1] + total[tail + 1 : tail + 2])
    row = iota((8, width), 0)
    pair = jnp.where(row == 0, high.astype(F32), jnp.where(row == 1, low.astype(F32), 0.0))
    for chunk in range(chunks):
        send_ref[chunk] = jnp.concatenate(
            [
                total[chunk * weight : (chunk + 1) * weight],
                total[width + chunk * table : width + (chunk + 1) * table],
                pair,
            ],
            0,
        ).astype(BF16)


def plane_sum_kernel(arrived_ref, send_ref):
    chunks, lines, width = arrived_ref.shape
    depth, block, _ = send_ref.shape
    weight = width // chunks
    each = weight // depth
    tail = weight + 2 * depth
    rows = []
    rest = None
    for y in range(Y_SIZE):
        some = arrived_ref[y * X_SIZE].astype(F32)
        for x in range(1, X_SIZE):
            some = some + arrived_ref[y * X_SIZE + x].astype(F32)
        rows.append(some[weight : weight + depth])
        rest = some if rest is None else rest + some
    bias = jnp.zeros((depth, width), F32) + jnp.sum(rest[tail:], 0, keepdims=True)
    rows += [rest[weight + depth : tail], rest[:weight], bias]
    rows = jnp.concatenate(rows, 0).astype(BF16)
    shape = (depth * block, rows.shape[0])
    out, into = iota(shape, 0), iota(shape, 1)
    line, z = out % block, out // block
    first = (Y_SIZE + 1) * depth
    of_weight = jnp.logical_and(line > Y_SIZE, line <= Y_SIZE + each)
    wanted = jnp.where(
        of_weight,
        first + z * each + line - Y_SIZE - 1,
        jnp.where(line <= Y_SIZE, line * depth, first + weight) + z,
    )
    send_ref[...] = move(into == wanted, rows).reshape(depth, block, width)


def weight_kernel(scale, arrived_ref, send_ref, bias_ref):
    depth, block, width = arrived_ref.shape
    total = jnp.sum(arrived_ref[...].astype(F32), 0) * scale
    each = block - Y_SIZE - 2
    row = iota((block, LANES), 0)
    done = jnp.zeros((block, LANES), F32)
    for group in range(width // LANES):
        for line in range(each):
            some = total[Y_SIZE + 1 + line : Y_SIZE + 2 + line, group * LANES : (group + 1) * LANES]
            done = jnp.where(row == group * each + line, some, done)
    done = done.astype(BF16)
    for z in range(depth):
        send_ref[z] = done
    bias_ref[...] = total[block - 1 :]


def gather_kernel(arrived_ref, whole_ref):
    weight, width = whole_ref.shape
    depth, block, _ = arrived_ref.shape
    groups = width // LANES
    each = weight // depth
    arrived = arrived_ref[...].reshape(depth * block, LANES)
    shape = (weight, depth * block)
    out, into = iota(shape, 0), iota(shape, 1)
    z, line = out // each, out % each
    for group in range(groups):
        rows = move(into == z * block + group * each + line, arrived)
        whole_ref[:, group * LANES : (group + 1) * LANES] = rows


def spread_kernel(whole_ref, send_ref):
    for chunk in range(send_ref.shape[0]):
        send_ref[chunk] = whole_ref[...]


def own_back_kernel(
    dst_ref, src_ref, count_ref, tiles_ref, seeds_ref, d_pre_ref, d_agg_ref, w_self_ref,
    own_ref, adj_ref,
):
    rows = own_ref.shape[0]
    seeds = seeds_ref.shape[1]
    place_tiles(dst_ref, src_ref, count_ref, tiles_ref, adj_ref, 0, rows // BLK)
    picks = (iota((rows, seeds), 0) == seeds_ref[...]).astype(BF16)
    seeded = dot(picks, d_pre_ref[...]).astype(BF16)
    own_ref[...] = dot(seeded, w_self_ref[...], 1, 1) + dot(adj_ref[...], d_agg_ref[...], 0, 0)


def scatter_kernel(rep_ref, lists_ref, arrived_ref, own_ref, keep_ref, *send_refs_and_total):
    *send_refs, total_ref = send_refs_and_total
    rows, width = own_ref.shape
    rep = rep_ref[0]
    places = boundary_places(rep, lists_ref, rows, summed_by_z(lists_ref.shape[1]))
    back = arrived_ref[...].reshape(places.shape[1], width)
    total_ref[...] = own_ref[...] + dot(places, back)
    share = rows // (X_SIZE * CORES)
    for step, ref in enumerate([keep_ref, *send_refs]):
        for core in range(CORES):
            place = jnp.bitwise_xor(rep, step * CORES + core)
            some = total_ref[pl.ds(pl.multiple_of(place * share, 32), share), :]
            ref[core * share : (core + 1) * share] = some.astype(ref.dtype)


def row_sum_kernel(keep_ref, *refs):
    *arrived_refs, own_ref, send_ref = refs
    share = own_ref.shape[0]
    total = keep_ref[...]
    for ref in arrived_refs:
        total = total + ref[...].astype(F32)
    own_ref[...] = total[:share]
    send_ref[...] = total[share:].astype(BF16)


def join_kernel(weights_ref, rows_ref, send_ref):
    width = weights_ref.shape[0]
    send_ref[:width] = weights_ref[...]
    send_ref[width:] = rows_ref[...]


def finish_kernel(core_ref, near_ref, own_ref, far_ref, first_ref, second_ref, rows_ref):
    width = near_ref.shape[0]
    near, far = near_ref[...], far_ref[:width]
    is_first = core_ref[0] == 0
    first_ref[...] = jnp.where(is_first, near, far)
    second_ref[...] = jnp.where(is_first, far, near)
    rows_ref[...] = own_ref[...] + far_ref[width:].astype(F32)


def body(
    feats,
    halo_index,
    seed_ids,
    tiles,
    tile_dst,
    tile_src,
    tile_count,
    w_self,
    w_neigh,
    bias,
    cotangent,
):
    depth = lax.axis_size("z")
    parts = depth * Y_SIZE
    reps = X_SIZE * CORES
    rows, width = feats.shape
    seeds = cotangent.shape[0]
    half = parts * SLOTS
    core_id = lax.axis_index("core").astype(jnp.int32)
    x_id = lax.axis_index("x").astype(jnp.int32)
    core = core_id.reshape(1)
    rep = (x_id * CORES + core_id).reshape(1)
    lists = halo_index[0].T
    seed_row = seed_ids.reshape(1, seeds)
    tile_scalars = (tile_dst, tile_src, tile_count)
    scale = float(seeds * parts * reps) ** (-0.5)

    def swap(values, axis):
        return lax.all_to_all(values, axis, split_axis=0, concat_axis=0, tiled=True)

    def pair(values):
        return lax.ppermute(values, "core", [(0, 1), (1, 0)])

    (send,) = call(
        send_kernel, "pick_boundary", [((2 * parts, width), BF16)], [rep], [], hbm=[lists, feats],
        scratch=fetched([lists, feats]), flops=4 * parts * rows * width, limit=FULL_VMEM_BYTES,
    )
    by_depth = swap(send.reshape(depth, 2 * Y_SIZE, width), "z").reshape(2 * parts, width)
    mats, sums = call(
        own_kernel, "own_rows",
        [
            ((2 * (seeds + half) + width, max(seeds, half)), BF16),
            ((2 * seeds, width), F32),
        ],
        [core, *tile_scalars],
        [tiles, feats, seed_row, w_self, bias.reshape(1, width)],
        scratch=[pltpu.VMEM((seeds, rows), BF16), pltpu.VMEM((seeds, 2 * half), BF16)],
        flops=2 * seeds * (3 * rows * width + width * width + 8 * half * half),
    )

    (plane,) = call(
        plane_kernel, "spread_plane", [((PLANE, 2 * depth, width), BF16)], [], [by_depth],
        flops=8 * parts * parts * width, after=[sums],
    )
    near = swap(plane, ("y", "x")).reshape(half, width)
    far = pair(near)

    out, d_pre, d_agg, keep, pair_send = call(
        middle_kernel, "forward_backward",
        [
            ((seeds, width), BF16),
            ((seeds, width), BF16),
            ((seeds, width), BF16),
            ((width + half + 16, width), BF16),
            ((width + half + 16, width), BF16),
        ],
        [core],
        [
            near, far, mats, sums, w_neigh, cotangent,
        ],
        flops=2 * seeds * width * (4 * half + 4 * width),
    )

    pair_arrived = pair(pair_send)
    (own,) = call(
        own_back_kernel, "own_rows_back", [((rows, width), F32)],
        [*tile_scalars], [tiles, seed_row, d_pre, d_agg, w_self],
        scratch=[pltpu.VMEM((seeds, rows), BF16)],
        flops=2 * seeds * width * 3 * rows,
    )
    (plane_send,) = call(
        pair_sum_kernel, "sum_pair",
        [((PLANE, width // PLANE + 2 * depth + 8, width), BF16)],
        [], [keep, pair_arrived], after=[own],
    )
    plane_arrived = swap(plane_send, ("y", "x"))
    (depth_send,) = call(
        plane_sum_kernel, "sum_plane",
        [((depth, 2 * Y_SIZE, width), BF16)],
        [], [plane_arrived],
    )
    depth_arrived = swap(depth_send, "z")
    weight_send, bias_row = call(
        functools.partial(weight_kernel, scale), "sum_weights",
        [((depth, 2 * Y_SIZE, LANES), BF16), ((1, width), F32)],
        [], [depth_arrived],
    )
    weight_depth = swap(weight_send, "z")
    share = rows // reps
    row_keep, *row_sends = call(
        scatter_kernel, "return_rows",
        [((CORES * share, width), F32)] + [((CORES * share, width), BF16)] * (X_SIZE - 1),
        [rep], [lists, depth_arrived, own],
        scratch=[pltpu.VMEM((rows, width), F32)],
        flops=4 * parts * rows * width, after=[weight_send],
    )
    row_arrived = [
        lax.ppermute(some, "x", [(x, x ^ step) for x in range(X_SIZE)])
        for step, some in enumerate(row_sends, 1)
    ]
    (weight_rows,) = call(
        gather_kernel, "gather_weights", [((width // PLANE, width), BF16)],
        [], [weight_depth], flops=20_000_000_000,
    )
    row_own, row_send = call(
        row_sum_kernel, "sum_rows", [((share, width), F32), ((share, width), BF16)],
        [], [row_keep, *row_arrived],
    )
    (weight_plane,) = call(
        spread_kernel, "spread_weights", [((PLANE, width // PLANE, width), BF16)],
        [], [weight_rows], after=[row_send],
    )
    weight_near = swap(weight_plane, ("y", "x")).reshape(width, width)
    (last_send,) = call(
        join_kernel, "join", [((width + share, width), BF16)], [], [weight_near, row_send]
    )
    grad_self, grad_neigh, input_grad = call(
        finish_kernel, "finish",
        [((width, width), BF16), ((width, width), BF16), ((share, width), F32)],
        [core], [weight_near, row_own, pair(last_send)],
    )
    grad_bias = bias_row.reshape(width)
    return (out, input_grad, grad_self, grad_neigh, grad_bias)


def solution(mesh):
    parts = mesh.shape["dom"]
    physical = Mesh(
        mesh.devices.reshape(parts // Y_SIZE, Y_SIZE, X_SIZE, CORES), ("z", "y", "x", "core")
    )
    dom = ("z", "y")
    every = ("z", "y", "x", "core")
    placed = (
        P(dom, None),
        P(dom, None, None),
        P(every),
        P(every, None, None),
        P(every, None),
        P(every, None),
        P(every),
        P(),
        P(),
        P(),
        P(every, None),
    )
    return jax.shard_map(
        body,
        mesh=physical,
        in_specs=placed,
        out_specs=(P(every, None), P(every, None), P(), P(), P()),
        check_vma=False,
    )
```

```python
import functools
import math

import jax
import jax.numpy as jnp
from jax import lax
from jax.experimental import pallas as pl
from jax.experimental.pallas import tpu as pltpu
from jax.sharding import Mesh
from jax.sharding import PartitionSpec as P

BLK = 128
LANES = 128
SLOTS = 8
X_SIZE = 4
CORES = 2
Y_SIZE = 4
PLANE = Y_SIZE * X_SIZE
BF16 = jnp.bfloat16
F32 = jnp.float32
VMEM_BYTES = 24 * 1024 * 1024
FULL_VMEM_BYTES = 65 * 1000 * 1024


def dot(a, b, contract_a=1, contract_b=0):
    return lax.dot_general(
        a, b, (((contract_a,), (contract_b,)), ((), ())), preferred_element_type=F32
    )


def move(matrix, rows):
    return dot(matrix.astype(BF16), rows).astype(BF16)


def iota(shape, dim):
    return lax.broadcasted_iota(jnp.int32, shape, dim)


def split(wide):
    high = wide.astype(BF16)
    return high, (wide - high.astype(F32)).astype(BF16)


def call(kernel, name, outs, scalars, arrays, scratch=(), flops=0, after=(), hbm=(), hbm_outs=(), limit=VMEM_BYTES):
    if after:
        inner, at = kernel, len(scalars) + len(arrays) + len(hbm)
        kernel = lambda *refs: inner(*refs[:at], *refs[at + len(after) :])
    shapes = tuple(jax.ShapeDtypeStruct(shape, dtype) for shape, dtype in outs)
    shapes += tuple(pltpu.HBM(shape, dtype) for shape, dtype in hbm_outs)
    size = sum(math.prod(a.shape) * a.dtype.itemsize for a in (*arrays, *hbm, *shapes))
    return pl.pallas_call(
        kernel,
        out_shape=shapes,
        in_specs=[pl.BlockSpec(memory_space=pltpu.SMEM)] * len(scalars)
        + [pl.BlockSpec(memory_space=pltpu.VMEM)] * len(arrays)
        + [pl.BlockSpec(memory_space=pltpu.HBM)] * len(hbm)
        + [pl.BlockSpec(memory_space=pl.ANY)] * len(after),
        out_specs=tuple([pl.BlockSpec(memory_space=pltpu.VMEM)] * len(outs))
        + tuple([pl.BlockSpec(memory_space=pltpu.HBM)] * len(hbm_outs)),
        scratch_shapes=list(scratch),
        compiler_params=pltpu.CompilerParams(vmem_limit_bytes=limit),
        cost_estimate=pl.CostEstimate(flops=flops, bytes_accessed=size, transcendentals=0),
        name=name,
    )(*scalars, *arrays, *hbm, *after)


def fetched(arrays):
    return [pltpu.VMEM(a.shape, a.dtype) for a in arrays] + [
        pltpu.SemaphoreType.DMA((len(arrays),))
    ]


def fetch(from_refs, to_refs, sems):
    copies = [
        pltpu.make_async_copy(source, to, sems.at[at])
        for at, (source, to) in enumerate(zip(from_refs, to_refs))
    ]
    for copy in copies:
        copy.start()
    return copies


def place_tiles(dst_ref, src_ref, count_ref, tiles_ref, adj_ref, first, last):
    adj_ref[...] = jnp.zeros_like(adj_ref)

    def step(slot, carry):
        block = src_ref[0, slot]

        @pl.when(jnp.logical_and(block >= first, block < last))
        def _():
            row = pl.multiple_of(dst_ref[0, slot] * BLK, BLK)
            col = pl.multiple_of((block - first) * BLK, BLK)
            adj_ref[pl.ds(row, BLK), pl.ds(col, BLK)] = tiles_ref[slot]

        return carry

    lax.fori_loop(0, count_ref[0], step, 0)


def boundary_places(rep, lists_ref, rows, order):
    slots, parts = lists_ref.shape
    lists = lists_ref[...].astype(F32)
    wanted = jnp.sum(
        jnp.where(iota((slots, parts), 0) == rep, lists, 0.0), axis=0, keepdims=True
    ).astype(jnp.int32)
    place = iota((rows, parts), 0)
    places = jnp.concatenate([(place == wanted).astype(BF16), (place == rep).astype(BF16)], 1)
    return dot(places, order.astype(BF16), 1, 1).astype(BF16)


def by_z(parts):
    shape = (2 * parts, 2 * parts)
    out, into = iota(shape, 0), iota(shape, 1)
    y, kind, z = out % Y_SIZE, out // Y_SIZE % 2, out // (2 * Y_SIZE)
    return into == kind * parts + z * Y_SIZE + y


def summed_by_z(parts):
    shape = (2 * parts, 2 * parts)
    out, into = iota(shape, 0), iota(shape, 1)
    line, z = out % (2 * Y_SIZE), out // (2 * Y_SIZE)
    halo = jnp.logical_and(line < Y_SIZE, into == z * Y_SIZE + line)
    hub = jnp.logical_and(line == Y_SIZE, into == parts)
    return jnp.logical_or(halo, hub)


def send_kernel(rep_ref, lists_hbm, feats_hbm, send_ref, lists_ref, feats_ref, sems):
    lists_copy, feats_copy = fetch((lists_hbm, feats_hbm), (lists_ref, feats_ref), sems)
    lists_copy.wait()
    parts = lists_ref.shape[1]
    places = boundary_places(rep_ref[0], lists_ref, feats_ref.shape[0], by_z(parts))
    feats_copy.wait()
    send_ref[...] = dot(places, feats_ref[...], 0, 0).astype(BF16)


def plane_kernel(arrived_ref, send_ref):
    chunk = send_ref.shape[1]
    depth = chunk // 2
    total = arrived_ref.shape[0]
    shape = (total, total)
    out, into = iota(shape, 0), iota(shape, 1)
    z, kind, y = out % depth, out // depth % 2, out // chunk
    moved = move(into == z * (2 * Y_SIZE) + kind * Y_SIZE + y, arrived_ref[...])
    for y_to in range(Y_SIZE):
        for x_to in range(X_SIZE):
            send_ref[y_to * X_SIZE + x_to] = moved[y_to * chunk : (y_to + 1) * chunk]


def own_kernel(
    core_ref, dst_ref, src_ref, count_ref, tiles_ref, feats_ref, seeds_ref, w_self_ref, bias_ref,
    mats_ref, sums_ref, own_adj_ref, adj_ref,
):
    rows = feats_ref.shape[0]
    seeds = seeds_ref.shape[1]
    own_blocks = rows // BLK
    table = adj_ref.shape[1]
    place_tiles(dst_ref, src_ref, count_ref, tiles_ref, own_adj_ref, 0, own_blocks)
    place_tiles(
        dst_ref, src_ref, count_ref, tiles_ref, adj_ref, own_blocks, own_blocks + table // BLK
    )
    picks = (iota((rows, seeds), 0) == seeds_ref[...]).astype(BF16)
    feats = feats_ref[...]
    mats_ref[2 * seeds + adj_ref.shape[1] :, :seeds] = dot(feats, picks, 0, 0).astype(BF16)
    chosen = dot(picks, feats, 0, 0).astype(BF16)
    sums_ref[:seeds] = dot(chosen, w_self_ref[...]) + bias_ref[...].astype(F32)
    sums_ref[seeds:] = dot(own_adj_ref[...], feats)
    adj = adj_ref[...]
    half = table // 2
    depth = half // PLANE // 2
    shape = (half, table)
    line, source = iota(shape, 0), iota(shape, 1)
    z, kind = line % depth, line // depth % 2
    x, y = line // (2 * depth) % X_SIZE, line // (2 * depth * X_SIZE)
    start = kind * half + (z * Y_SIZE + y) * SLOTS + x * CORES
    for far, core in enumerate((core_ref[0], 1 - core_ref[0])):
        order = (source == start + core).astype(BF16)
        mats_ref[far * seeds : (far + 1) * seeds, :half] = dot(adj, order, 1, 1).astype(BF16)
        first = 2 * seeds + far * half
        mats_ref[first : first + half, :seeds] = dot(order, adj, 1, 1).astype(BF16)


def middle_kernel(
    core_ref, near_ref, far_ref, mats_ref, sums_ref, w_neigh_ref, cot_ref,
    out_ref, d_pre_ref, d_agg_ref, keep_ref, send_ref,
):
    width = w_neigh_ref.shape[0]
    half = near_ref.shape[0]
    seeds = cot_ref.shape[0]
    near_back, far_back, chosen_t = (2 * seeds + step * half for step in range(3))
    aggregate = (
        sums_ref[seeds:]
        + dot(mats_ref[:seeds, :half], near_ref[...])
        + dot(mats_ref[seeds : 2 * seeds, :half], far_ref[...])
    ).astype(BF16)
    preact = sums_ref[:seeds] + dot(aggregate, w_neigh_ref[...])
    gate = jax.nn.sigmoid(preact)
    out_ref[...] = (preact * gate).astype(BF16)
    d_pre = (cot_ref[...].astype(F32) * gate * (1.0 + preact * (1.0 - gate))).astype(BF16)
    d_pre_ref[...] = d_pre
    d_agg = dot(d_pre, w_neigh_ref[...], 1, 1).astype(BF16)
    d_agg_ref[...] = d_agg
    first = dot(mats_ref[chosen_t:, :seeds], d_pre).astype(BF16)
    second = dot(aggregate, d_pre, 0, 0).astype(BF16)
    is_first = core_ref[0] == 0
    keep_ref[:width] = jnp.where(is_first, first, second)
    send_ref[:width] = jnp.where(is_first, second, first)
    keep_ref[width : width + half] = dot(mats_ref[near_back:far_back, :seeds], d_agg).astype(BF16)
    send_ref[width : width + half] = dot(mats_ref[far_back:chosen_t, :seeds], d_agg).astype(BF16)
    high, low = split(jnp.sum(d_pre.astype(F32), 0, keepdims=True))
    row = iota((keep_ref.shape[0] - width - half, width), 0)
    pair = jnp.where(
        row == 0, high.astype(F32), jnp.where(row == 1, low.astype(F32), 0.0)
    ).astype(BF16)
    keep_ref[width + half :] = pair
    send_ref[width + half :] = pair


def pair_sum_kernel(keep_ref, other_ref, send_ref):
    chunks, lines, width = send_ref.shape
    total = keep_ref[...].astype(F32) + other_ref[...].astype(F32)
    weight, table = width // chunks, (lines - 8 - width // chunks)
    tail = width + chunks * table
    high, low = split(total[tail : tail + 1] + total[tail + 1 : tail + 2])
    row = iota((8, width), 0)
    pair = jnp.where(row == 0, high.astype(F32), jnp.where(row == 1, low.astype(F32), 0.0))
    for chunk in range(chunks):
        send_ref[chunk] = jnp.concatenate(
            [
                total[chunk * weight : (chunk + 1) * weight],
                total[width + chunk * table : width + (chunk + 1) * table],
                pair,
            ],
            0,
        ).astype(BF16)


def plane_sum_kernel(arrived_ref, send_ref):
    chunks, lines, width = arrived_ref.shape
    depth, block, _ = send_ref.shape
    weight = width // chunks
    each = weight // depth
    tail = weight + 2 * depth
    rows = []
    rest = None
    for y in range(Y_SIZE):
        some = arrived_ref[y * X_SIZE].astype(F32)
        for x in range(1, X_SIZE):
            some = some + arrived_ref[y * X_SIZE + x].astype(F32)
        rows.append(some[weight : weight + depth])
        rest = some if rest is None else rest + some
    bias = jnp.zeros((depth, width), F32) + jnp.sum(rest[tail:], 0, keepdims=True)
    rows += [rest[weight + depth : tail], rest[:weight], bias]
    rows = jnp.concatenate(rows, 0).astype(BF16)
    shape = (depth * block, rows.shape[0])
    out, into = iota(shape, 0), iota(shape, 1)
    line, z = out % block, out // block
    first = (Y_SIZE + 1) * depth
    of_weight = jnp.logical_and(line > Y_SIZE, line <= Y_SIZE + each)
    wanted = jnp.where(
        of_weight,
        first + z * each + line - Y_SIZE - 1,
        jnp.where(line <= Y_SIZE, line * depth, first + weight) + z,
    )
    send_ref[...] = move(into == wanted, rows).reshape(depth, block, width)


def weight_kernel(scale, arrived_ref, send_ref, bias_ref):
    depth, block, width = arrived_ref.shape
    total = jnp.sum(arrived_ref[...].astype(F32), 0) * scale
    each = block - Y_SIZE - 2
    row = iota((block, LANES), 0)
    done = jnp.zeros((block, LANES), F32)
    for group in range(width // LANES):
        for line in range(each):
            some = total[Y_SIZE + 1 + line : Y_SIZE + 2 + line, group * LANES : (group + 1) * LANES]
            done = jnp.where(row == group * each + line, some, done)
    done = done.astype(BF16)
    for z in range(depth):
        send_ref[z] = done
    bias_ref[...] = total[block - 1 :]


def gather_kernel(arrived_ref, whole_ref):
    weight, width = whole_ref.shape
    depth, block, _ = arrived_ref.shape
    groups = width // LANES
    each = weight // depth
    arrived = arrived_ref[...].reshape(depth * block, LANES)
    shape = (weight, depth * block)
    out, into = iota(shape, 0), iota(shape, 1)
    z, line = out // each, out % each
    for group in range(groups):
        rows = move(into == z * block + group * each + line, arrived)
        whole_ref[:, group * LANES : (group + 1) * LANES] = rows


def spread_kernel(whole_ref, send_ref):
    for chunk in range(send_ref.shape[0]):
        send_ref[chunk] = whole_ref[...]


def own_back_kernel(
    dst_ref, src_ref, count_ref, tiles_ref, seeds_ref, d_pre_ref, d_agg_ref, w_self_ref,
    own_ref, adj_ref,
):
    rows = own_ref.shape[0]
    seeds = seeds_ref.shape[1]
    place_tiles(dst_ref, src_ref, count_ref, tiles_ref, adj_ref, 0, rows // BLK)
    picks = (iota((rows, seeds), 0) == seeds_ref[...]).astype(BF16)
    seeded = dot(picks, d_pre_ref[...]).astype(BF16)
    own_ref[...] = dot(seeded, w_self_ref[...], 1, 1) + dot(adj_ref[...], d_agg_ref[...], 0, 0)


def scatter_kernel(rep_ref, lists_ref, arrived_ref, own_ref, keep_ref, *send_refs_and_total):
    *send_refs, total_ref = send_refs_and_total
    rows, width = own_ref.shape
    rep = rep_ref[0]
    places = boundary_places(rep, lists_ref, rows, summed_by_z(lists_ref.shape[1]))
    back = arrived_ref[...].reshape(places.shape[1], width)
    total_ref[...] = own_ref[...] + dot(places, back)
    share = rows // (X_SIZE * CORES)
    for step, ref in enumerate([keep_ref, *send_refs]):
        for core in range(CORES):
            place = jnp.bitwise_xor(rep, step * CORES + core)
            some = total_ref[pl.ds(pl.multiple_of(place * share, 32), share), :]
            ref[core * share : (core + 1) * share] = some.astype(ref.dtype)


def row_sum_kernel(keep_ref, *refs):
    *arrived_refs, own_ref, send_ref = refs
    share = own_ref.shape[0]
    total = keep_ref[...]
    for ref in arrived_refs:
        total = total + ref[...].astype(F32)
    own_ref[...] = total[:share]
    send_ref[...] = total[share:].astype(BF16)


def join_kernel(weights_ref, rows_ref, send_ref):
    width = weights_ref.shape[0]
    send_ref[:width] = weights_ref[...]
    send_ref[width:] = rows_ref[...]


def finish_kernel(core_ref, near_ref, own_ref, far_ref, first_ref, second_ref, rows_ref):
    width = near_ref.shape[0]
    near, far = near_ref[...], far_ref[:width]
    is_first = core_ref[0] == 0
    first_ref[...] = jnp.where(is_first, near, far)
    second_ref[...] = jnp.where(is_first, far, near)
    rows_ref[...] = own_ref[...] + far_ref[width:].astype(F32)


def body(
    feats,
    halo_index,
    seed_ids,
    tiles,
    tile_dst,
    tile_src,
    tile_count,
    w_self,
    w_neigh,
    bias,
    cotangent,
):
    depth = lax.axis_size("z")
    parts = depth * Y_SIZE
    reps = X_SIZE * CORES
    rows, width = feats.shape
    seeds = cotangent.shape[0]
    half = parts * SLOTS
    core_id = lax.axis_index("core").astype(jnp.int32)
    x_id = lax.axis_index("x").astype(jnp.int32)
    core = core_id.reshape(1)
    rep = (x_id * CORES + core_id).reshape(1)
    lists = halo_index[0].T
    seed_row = seed_ids.reshape(1, seeds)
    tile_scalars = (tile_dst, tile_src, tile_count)
    scale = float(seeds * parts * reps) ** (-0.5)

    window = 20_000_000_000

    def swap(values, axis):
        return lax.all_to_all(values, axis, split_axis=0, concat_axis=0, tiled=True)

    def pair(values):
        return lax.ppermute(values, "core", [(0, 1), (1, 0)])

    (send,) = call(
        send_kernel, "pick_boundary", [((2 * parts, width), BF16)], [rep], [], hbm=[lists, feats],
        scratch=fetched([lists, feats]), flops=4 * parts * rows * width, limit=FULL_VMEM_BYTES,
    )
    by_depth = swap(send.reshape(depth, 2 * Y_SIZE, width), "z").reshape(2 * parts, width)
    mats, sums = call(
        own_kernel, "own_rows",
        [
            ((2 * (seeds + half) + width, max(seeds, half)), BF16),
            ((2 * seeds, width), F32),
        ],
        [core, *tile_scalars],
        [tiles, feats, seed_row, w_self, bias.reshape(1, width)],
        scratch=[pltpu.VMEM((seeds, rows), BF16), pltpu.VMEM((seeds, 2 * half), BF16)],
        flops=2 * seeds * (3 * rows * width + width * width + 8 * half * half),
    )

    (plane,) = call(
        plane_kernel, "spread_plane", [((PLANE, 2 * depth, width), BF16)], [], [by_depth],
        flops=8 * parts * parts * width, after=[sums],
    )
    near = swap(plane, ("y", "x")).reshape(half, width)
    far = pair(near)

    out, d_pre, d_agg, keep, pair_send = call(
        middle_kernel, "forward_backward",
        [
            ((seeds, width), BF16),
            ((seeds, width), BF16),
            ((seeds, width), BF16),
            ((width + half + 16, width), BF16),
            ((width + half + 16, width), BF16),
        ],
        [core],
        [
            near, far, mats, sums, w_neigh, cotangent,
        ],
        flops=2 * seeds * width * (4 * half + 4 * width),
    )

    pair_arrived = pair(pair_send)
    (own,) = call(
        own_back_kernel, "own_rows_back", [((rows, width), F32)],
        [*tile_scalars], [tiles, seed_row, d_pre, d_agg, w_self],
        scratch=[pltpu.VMEM((seeds, rows), BF16)],
        flops=2 * seeds * width * 3 * rows,
    )
    (plane_send,) = call(
        pair_sum_kernel, "sum_pair",
        [((PLANE, width // PLANE + 2 * depth + 8, width), BF16)],
        [], [keep, pair_arrived], after=[own],
    )
    plane_arrived = swap(plane_send, ("y", "x"))
    (depth_send,) = call(
        plane_sum_kernel, "sum_plane",
        [((depth, 2 * Y_SIZE, width), BF16)],
        [], [plane_arrived],
    )
    depth_arrived = swap(depth_send, "z")
    weight_send, bias_row = call(
        functools.partial(weight_kernel, scale), "sum_weights",
        [((depth, 2 * Y_SIZE, LANES), BF16), ((1, width), F32)],
        [], [depth_arrived],
    )
    weight_depth = swap(weight_send, "z")
    share = rows // reps
    row_keep, *row_sends = call(
        scatter_kernel, "return_rows",
        [((CORES * share, width), F32)] + [((CORES * share, width), BF16)] * (X_SIZE - 1),
        [rep], [lists, depth_arrived, own],
        scratch=[pltpu.VMEM((rows, width), F32)],
        flops=4 * parts * rows * width, after=[weight_send],
    )
    row_arrived = [
        lax.ppermute(row_sends[step - 1], "x", [(x, x ^ step) for x in range(X_SIZE)])
        for step in (2, 1, 3)
    ]
    (weight_rows,) = call(
        gather_kernel, "gather_weights", [((width // PLANE, width), BF16)],
        [], [weight_depth], flops=window, after=[row_keep],
    )
    row_own, row_send = call(
        row_sum_kernel, "sum_rows", [((share, width), F32), ((share, width), BF16)],
        [], [row_keep, *row_arrived], flops=window,
    )
    (weight_plane,) = call(
        spread_kernel, "spread_weights", [((PLANE, width // PLANE, width), BF16)],
        [], [weight_rows],
    )
    weight_near = swap(weight_plane, ("y", "x")).reshape(width, width)
    (last_send,) = call(
        join_kernel, "join", [((width + share, width), BF16)], [], [weight_near, row_send]
    )
    grad_self, grad_neigh, input_grad = call(
        finish_kernel, "finish",
        [((width, width), BF16), ((width, width), BF16), ((share, width), F32)],
        [core], [weight_near, row_own, pair(last_send)],
    )
    grad_bias = bias_row.reshape(width)
    return (out, input_grad, grad_self, grad_neigh, grad_bias)


def solution(mesh):
    parts = mesh.shape["dom"]
    physical = Mesh(
        mesh.devices.reshape(parts // Y_SIZE, Y_SIZE, X_SIZE, CORES), ("z", "y", "x", "core")
    )
    dom = ("z", "y")
    every = ("z", "y", "x", "core")
    placed = (
        P(dom, None),
        P(dom, None, None),
        P(every),
        P(every, None, None),
        P(every, None),
        P(every, None),
        P(every),
        P(),
        P(),
        P(),
        P(every, None),
    )
    return jax.shard_map(
        body,
        mesh=physical,
        in_specs=placed,
        out_specs=(P(every, None), P(every, None), P(), P(), P()),
        check_vma=False,
    )
```

```python
import functools
import math

import jax
import jax.numpy as jnp
from jax import lax
from jax.experimental import pallas as pl
from jax.experimental.pallas import tpu as pltpu
from jax.sharding import Mesh
from jax.sharding import PartitionSpec as P

BLK = 128
LANES = 128
SLOTS = 8
X_SIZE = 4
CORES = 2
Y_SIZE = 4
PLANE = Y_SIZE * X_SIZE
BF16 = jnp.bfloat16
F32 = jnp.float32
VMEM_BYTES = 24 * 1024 * 1024
FULL_VMEM_BYTES = 65 * 1000 * 1024


def dot(a, b, contract_a=1, contract_b=0):
    return lax.dot_general(
        a, b, (((contract_a,), (contract_b,)), ((), ())), preferred_element_type=F32
    )


def move(matrix, rows):
    return dot(matrix.astype(BF16), rows).astype(BF16)


def iota(shape, dim):
    return lax.broadcasted_iota(jnp.int32, shape, dim)


def call(kernel, name, outs, scalars, arrays, scratch=(), flops=0, after=(), hbm=(), hbm_outs=(), limit=VMEM_BYTES):
    if after:
        inner, at = kernel, len(scalars) + len(arrays) + len(hbm)
        kernel = lambda *refs: inner(*refs[:at], *refs[at + len(after) :])
    shapes = tuple(jax.ShapeDtypeStruct(shape, dtype) for shape, dtype in outs)
    shapes += tuple(pltpu.HBM(shape, dtype) for shape, dtype in hbm_outs)
    size = sum(math.prod(a.shape) * a.dtype.itemsize for a in (*arrays, *hbm, *shapes))
    return pl.pallas_call(
        kernel,
        out_shape=shapes,
        in_specs=[pl.BlockSpec(memory_space=pltpu.SMEM)] * len(scalars)
        + [pl.BlockSpec(memory_space=pltpu.VMEM)] * len(arrays)
        + [pl.BlockSpec(memory_space=pltpu.HBM)] * len(hbm)
        + [pl.BlockSpec(memory_space=pl.ANY)] * len(after),
        out_specs=tuple([pl.BlockSpec(memory_space=pltpu.VMEM)] * len(outs))
        + tuple([pl.BlockSpec(memory_space=pltpu.HBM)] * len(hbm_outs)),
        scratch_shapes=list(scratch),
        compiler_params=pltpu.CompilerParams(vmem_limit_bytes=limit),
        cost_estimate=pl.CostEstimate(flops=flops, bytes_accessed=size, transcendentals=0),
        name=name,
    )(*scalars, *arrays, *hbm, *after)


def fetched(arrays):
    return [pltpu.VMEM(a.shape, a.dtype) for a in arrays] + [
        pltpu.SemaphoreType.DMA((len(arrays),))
    ]


def fetch(from_refs, to_refs, sems):
    copies = [
        pltpu.make_async_copy(source, to, sems.at[at])
        for at, (source, to) in enumerate(zip(from_refs, to_refs))
    ]
    for copy in copies:
        copy.start()
    return copies


def place_tiles(dst_ref, src_ref, count_ref, tiles_ref, adj_ref, first, last):
    adj_ref[...] = jnp.zeros_like(adj_ref)

    def step(slot, carry):
        block = src_ref[0, slot]

        @pl.when(jnp.logical_and(block >= first, block < last))
        def _():
            row = pl.multiple_of(dst_ref[0, slot] * BLK, BLK)
            col = pl.multiple_of((block - first) * BLK, BLK)
            adj_ref[pl.ds(row, BLK), pl.ds(col, BLK)] = tiles_ref[slot]

        return carry

    lax.fori_loop(0, count_ref[0], step, 0)


def boundary_places(rep, lists_ref, rows, order):
    slots, parts = lists_ref.shape
    lists = lists_ref[...].astype(F32)
    wanted = jnp.sum(
        jnp.where(iota((slots, parts), 0) == rep, lists, 0.0), axis=0, keepdims=True
    ).astype(jnp.int32)
    place = iota((rows, parts), 0)
    places = jnp.concatenate([(place == wanted).astype(BF16), (place == rep).astype(BF16)], 1)
    return dot(places, order.astype(BF16), 1, 1).astype(BF16)


def summed_by_z(parts):
    shape = (2 * parts, 2 * parts)
    out, into = iota(shape, 0), iota(shape, 1)
    line, z = out % (2 * Y_SIZE), out // (2 * Y_SIZE)
    halo = jnp.logical_and(line < Y_SIZE, into == z * Y_SIZE + line)
    hub = jnp.logical_and(line == Y_SIZE, into == parts)
    return jnp.logical_or(halo, hub)


def send_kernel(rep_ref, lists_hbm, feats_hbm, send_ref, lists_ref, feats_ref, sems):
    lists_copy, feats_copy = fetch((lists_hbm, feats_hbm), (lists_ref, feats_ref), sems)
    slots, parts = lists_ref.shape
    rep = rep_ref[0]
    shape = (2 * parts, parts)
    line = iota(shape, 0)
    part = line // (2 * Y_SIZE) * Y_SIZE + line % Y_SIZE
    of_part = (part == iota(shape, 1)).astype(BF16)
    lists_copy.wait()
    lists = lists_ref[...]
    high, low = (lists // 256).astype(BF16), (lists % 256).astype(BF16)
    wanted = dot(of_part, high, 1, 1) * 256.0 + dot(of_part, low, 1, 1)
    shape = (2 * parts, slots)
    is_hub = iota(shape, 0) // Y_SIZE % 2 == 1
    wanted = jnp.where(is_hub, rep.astype(F32), wanted)
    wanted = jnp.sum(jnp.where(iota(shape, 1) == rep, wanted, 0.0), axis=1, keepdims=True)
    places = iota((2 * parts, feats_ref.shape[0]), 1) == wanted.astype(jnp.int32)
    places = places.astype(BF16)
    feats_copy.wait()
    send_ref[...] = dot(places, feats_ref[...]).astype(BF16)


def plane_kernel(arrived_ref, send_ref):
    chunk = send_ref.shape[1]
    depth = chunk // 2
    total = arrived_ref.shape[0]
    shape = (total, total)
    out, into = iota(shape, 0), iota(shape, 1)
    z, kind, y = out % depth, out // depth % 2, out // chunk
    moved = move(into == z * (2 * Y_SIZE) + kind * Y_SIZE + y, arrived_ref[...])
    for y_to in range(Y_SIZE):
        for x_to in range(X_SIZE):
            send_ref[y_to * X_SIZE + x_to] = moved[y_to * chunk : (y_to + 1) * chunk]


def own_kernel(
    core_ref, dst_ref, src_ref, count_ref, tiles_ref, feats_ref, seeds_ref, w_self_ref, bias_ref,
    mats_ref, sums_ref, own_adj_ref, adj_ref,
):
    rows = feats_ref.shape[0]
    seeds = seeds_ref.shape[1]
    own_blocks = rows // BLK
    table = adj_ref.shape[1]
    place_tiles(dst_ref, src_ref, count_ref, tiles_ref, own_adj_ref, 0, own_blocks)
    place_tiles(
        dst_ref, src_ref, count_ref, tiles_ref, adj_ref, own_blocks, own_blocks + table // BLK
    )
    picks = (iota((rows, seeds), 0) == seeds_ref[...]).astype(BF16)
    feats = feats_ref[...]
    mats_ref[2 * seeds + adj_ref.shape[1] :, :seeds] = dot(feats, picks, 0, 0).astype(BF16)
    chosen = dot(picks, feats, 0, 0).astype(BF16)
    sums_ref[:seeds] = dot(chosen, w_self_ref[...]) + bias_ref[...].astype(F32)
    sums_ref[seeds:] = dot(own_adj_ref[...], feats)
    adj = adj_ref[...]
    half = table // 2
    depth = half // PLANE // 2
    shape = (half, table)
    line, source = iota(shape, 0), iota(shape, 1)
    z, kind = line % depth, line // depth % 2
    x, y = line // (2 * depth) % X_SIZE, line // (2 * depth * X_SIZE)
    start = kind * half + (z * Y_SIZE + y) * SLOTS + x * CORES
    for far, core in enumerate((core_ref[0], 1 - core_ref[0])):
        order = (source == start + core).astype(BF16)
        mats_ref[far * seeds : (far + 1) * seeds, :half] = dot(adj, order, 1, 1).astype(BF16)
        first = 2 * seeds + far * half
        mats_ref[first : first + half, :seeds] = dot(order, adj, 1, 1).astype(BF16)


def middle_kernel(
    core_ref, near_ref, far_ref, mats_ref, sums_ref, w_neigh_ref, cot_ref,
    out_ref, d_pre_ref, d_agg_ref, keep_ref, send_ref,
):
    width = w_neigh_ref.shape[0]
    half = near_ref.shape[0]
    seeds = cot_ref.shape[0]
    near_back, far_back, chosen_t = (2 * seeds + step * half for step in range(3))
    aggregate = (
        sums_ref[seeds:]
        + dot(mats_ref[:seeds, :half], near_ref[...])
        + dot(mats_ref[seeds : 2 * seeds, :half], far_ref[...])
    ).astype(BF16)
    preact = sums_ref[:seeds] + dot(aggregate, w_neigh_ref[...])
    gate = jax.nn.sigmoid(preact)
    out_ref[...] = (preact * gate).astype(BF16)
    d_pre = (cot_ref[...].astype(F32) * gate * (1.0 + preact * (1.0 - gate))).astype(BF16)
    d_pre_ref[...] = d_pre
    d_agg = dot(d_pre, w_neigh_ref[...], 1, 1).astype(BF16)
    d_agg_ref[...] = d_agg
    first = dot(mats_ref[chosen_t:, :seeds], d_pre).astype(BF16)
    second = dot(aggregate, d_pre, 0, 0).astype(BF16)
    is_first = core_ref[0] == 0
    keep_ref[:width] = jnp.where(is_first, first, second)
    send_ref[:width] = jnp.where(is_first, second, first)
    keep_ref[width : width + half] = dot(mats_ref[near_back:far_back, :seeds], d_agg).astype(BF16)
    send_ref[width : width + half] = dot(mats_ref[far_back:chosen_t, :seeds], d_agg).astype(BF16)
    bias = two_rows(jnp.sum(d_pre.astype(F32), 0, keepdims=True), keep_ref.shape[0] - width - half)
    keep_ref[width + half :] = bias
    send_ref[width + half :] = bias


def two_rows(wide, rows):
    high = wide.astype(BF16).astype(F32)
    row = iota((rows, wide.shape[1]), 0)
    return jnp.where(row == 0, high, jnp.where(row == 1, wide - high, 0.0)).astype(BF16)


def pair_sum_kernel(keep_ref, other_ref, send_ref, bias_ref):
    chunks, lines, width = send_ref.shape
    total = keep_ref[...].astype(F32) + other_ref[...].astype(F32)
    weight = width // chunks
    table = lines - weight
    bias_ref[...] = jnp.sum(total[width + chunks * table :], 0, keepdims=True)
    total = total.astype(BF16)
    for chunk in range(chunks):
        send_ref[chunk, :weight] = total[chunk * weight : (chunk + 1) * weight]
        send_ref[chunk, weight:] = total[width + chunk * table : width + (chunk + 1) * table]


def plane_sum_kernel(arrived_ref, bias_ref, send_ref):
    chunks, lines, width = arrived_ref.shape
    depth, block, _ = send_ref.shape
    weight = width // chunks
    each = weight // depth
    tail = weight + 2 * depth
    rows = []
    rest = None
    for y in range(Y_SIZE):
        some = arrived_ref[y * X_SIZE].astype(F32)
        for x in range(1, X_SIZE):
            some = some + arrived_ref[y * X_SIZE + x].astype(F32)
        rows.append(some[weight : weight + depth])
        rest = some if rest is None else rest + some
    bias = jnp.zeros((depth, width), F32) + bias_ref[...]
    rows += [rest[weight + depth : tail], rest[:weight], bias]
    rows = jnp.concatenate(rows, 0).astype(BF16)
    shape = (depth * block, rows.shape[0])
    out, into = iota(shape, 0), iota(shape, 1)
    line, z = out % block, out // block
    first = (Y_SIZE + 1) * depth
    of_weight = jnp.logical_and(line > Y_SIZE, line <= Y_SIZE + each)
    wanted = jnp.where(
        of_weight,
        first + z * each + line - Y_SIZE - 1,
        jnp.where(line <= Y_SIZE, line * depth, first + weight) + z,
    )
    send_ref[...] = move(into == wanted, rows).reshape(depth, block, width)


def weight_kernel(scale, arrived_ref, send_ref, bias_ref):
    depth, block, width = arrived_ref.shape
    total = jnp.sum(arrived_ref[...].astype(F32), 0) * scale
    each = block - Y_SIZE - 2
    row = iota((block, LANES), 0)
    done = jnp.zeros((block, LANES), F32)
    for group in range(width // LANES):
        for line in range(each):
            some = total[Y_SIZE + 1 + line : Y_SIZE + 2 + line, group * LANES : (group + 1) * LANES]
            done = jnp.where(row == group * each + line, some, done)
    done = done.astype(BF16)
    for z in range(depth):
        send_ref[z] = done
    bias_ref[...] = total[block - 1 :]


def gather_kernel(arrived_ref, whole_ref):
    weight, width = whole_ref.shape
    depth, block, _ = arrived_ref.shape
    groups = width // LANES
    each = weight // depth
    arrived = arrived_ref[...].reshape(depth * block, LANES)
    shape = (weight, depth * block)
    out, into = iota(shape, 0), iota(shape, 1)
    z, line = out // each, out % each
    for group in range(groups):
        rows = move(into == z * block + group * each + line, arrived)
        whole_ref[:, group * LANES : (group + 1) * LANES] = rows


def spread_kernel(whole_ref, send_ref):
    for chunk in range(send_ref.shape[0]):
        send_ref[chunk] = whole_ref[...]


def own_back_kernel(
    dst_ref, src_ref, count_ref, tiles_ref, seeds_ref, d_pre_ref, d_agg_ref, w_self_ref,
    own_ref, adj_ref,
):
    rows = own_ref.shape[0]
    seeds = seeds_ref.shape[1]
    place_tiles(dst_ref, src_ref, count_ref, tiles_ref, adj_ref, 0, rows // BLK)
    picks = (iota((rows, seeds), 0) == seeds_ref[...]).astype(BF16)
    seeded = dot(picks, d_pre_ref[...]).astype(BF16)
    own_ref[...] = dot(seeded, w_self_ref[...], 1, 1) + dot(adj_ref[...], d_agg_ref[...], 0, 0)


def scatter_kernel(
    rep_ref, lists_ref, arrived_ref, own_ref, bias_ref, keep_ref, *send_refs_and_total
):
    *send_refs, total_ref = send_refs_and_total
    rows, width = own_ref.shape
    rep = rep_ref[0]
    places = boundary_places(rep, lists_ref, rows, summed_by_z(lists_ref.shape[1]))
    back = arrived_ref[...].reshape(places.shape[1], width)
    total_ref[...] = own_ref[...] + dot(places, back)
    share = rows // (X_SIZE * CORES)
    for step, ref in enumerate([keep_ref, *send_refs]):
        for core in range(CORES):
            place = jnp.bitwise_xor(rep, step * CORES + core)
            some = total_ref[pl.ds(pl.multiple_of(place * share, 32), share), :]
            ref[core * share : (core + 1) * share] = some.astype(ref.dtype)
    bias = two_rows(bias_ref[...], send_refs[0].shape[0] - CORES * share)
    for ref in send_refs:
        ref[CORES * share :] = bias


def row_sum_kernel(keep_ref, bias_ref, *refs):
    *arrived_refs, own_ref, send_ref, bias_sum_ref, bias_send_ref = refs
    share = own_ref.shape[0]
    total, bias = keep_ref[...], bias_ref[...]
    for ref in arrived_refs:
        arrived = ref[...].astype(F32)
        total = total + arrived[: CORES * share]
        bias = bias + jnp.sum(arrived[CORES * share :], 0, keepdims=True)
    own_ref[...] = total[:share]
    send_ref[...] = total[share:].astype(BF16)
    bias_sum_ref[...] = bias
    bias_send_ref[...] = two_rows(bias, bias_send_ref.shape[0])


def join_kernel(weights_ref, rows_ref, send_ref):
    width = weights_ref.shape[0]
    send_ref[:width] = weights_ref[...]
    send_ref[width:] = rows_ref[...]


def finish_kernel(core_ref, near_ref, own_ref, bias_sum_ref, far_ref, *refs):
    *bias_refs, first_ref, second_ref, rows_ref, bias_ref = refs
    width = near_ref.shape[0]
    near, far = near_ref[...], far_ref[:width]
    is_first = core_ref[0] == 0
    first_ref[...] = jnp.where(is_first, near, far)
    second_ref[...] = jnp.where(is_first, far, near)
    rows_ref[...] = own_ref[...] + far_ref[width:].astype(F32)
    bias = bias_sum_ref[...]
    for ref in bias_refs:
        bias = bias + jnp.sum(ref[...].astype(F32), 0, keepdims=True)
    bias_ref[...] = bias


def body(
    feats,
    halo_index,
    seed_ids,
    tiles,
    tile_dst,
    tile_src,
    tile_count,
    w_self,
    w_neigh,
    bias,
    cotangent,
):
    depth = lax.axis_size("z")
    parts = depth * Y_SIZE
    reps = X_SIZE * CORES
    rows, width = feats.shape
    seeds = cotangent.shape[0]
    half = parts * SLOTS
    core_id = lax.axis_index("core").astype(jnp.int32)
    x_id = lax.axis_index("x").astype(jnp.int32)
    core = core_id.reshape(1)
    rep = (x_id * CORES + core_id).reshape(1)
    lists = halo_index[0].T
    seed_row = seed_ids.reshape(1, seeds)
    tile_scalars = (tile_dst, tile_src, tile_count)
    scale = float(seeds * parts * reps) ** (-0.5)

    window = 20_000_000_000

    def swap(values, axis):
        return lax.all_to_all(values, axis, split_axis=0, concat_axis=0, tiled=True)

    def pair(values):
        return lax.ppermute(values, "core", [(0, 1), (1, 0)])

    (send,) = call(
        send_kernel, "pick_boundary", [((2 * parts, width), BF16)], [rep], [], hbm=[lists, feats],
        scratch=fetched([lists, feats]), flops=4 * parts * rows * width, limit=FULL_VMEM_BYTES,
    )
    by_depth = swap(send.reshape(depth, 2 * Y_SIZE, width), "z").reshape(2 * parts, width)
    mats, sums = call(
        own_kernel, "own_rows",
        [
            ((2 * (seeds + half) + width, max(seeds, half)), BF16),
            ((2 * seeds, width), F32),
        ],
        [core, *tile_scalars],
        [tiles, feats, seed_row, w_self, bias.reshape(1, width)],
        scratch=[pltpu.VMEM((seeds, rows), BF16), pltpu.VMEM((seeds, 2 * half), BF16)],
        flops=2 * seeds * (3 * rows * width + width * width + 8 * half * half),
    )

    (plane,) = call(
        plane_kernel, "spread_plane", [((PLANE, 2 * depth, width), BF16)], [], [by_depth],
        flops=8 * parts * parts * width, after=[sums],
    )
    near = swap(plane, ("y", "x")).reshape(half, width)
    far = pair(near)

    out, d_pre, d_agg, keep, pair_send = call(
        middle_kernel, "forward_backward",
        [
            ((seeds, width), BF16),
            ((seeds, width), BF16),
            ((seeds, width), BF16),
            ((width + half + 16, width), BF16),
            ((width + half + 16, width), BF16),
        ],
        [core],
        [
            near, far, mats, sums, w_neigh, cotangent,
        ],
        flops=2 * seeds * width * (4 * half + 4 * width),
    )

    pair_arrived = pair(pair_send)
    (own,) = call(
        own_back_kernel, "own_rows_back", [((rows, width), F32)],
        [*tile_scalars], [tiles, seed_row, d_pre, d_agg, w_self],
        scratch=[pltpu.VMEM((seeds, rows), BF16)],
        flops=2 * seeds * width * 3 * rows,
    )
    plane_send, pair_bias = call(
        pair_sum_kernel, "sum_pair",
        [((PLANE, width // PLANE + 2 * depth, width), BF16), ((1, width), F32)],
        [], [keep, pair_arrived], after=[own],
    )
    plane_arrived = swap(plane_send, ("y", "x"))
    (depth_send,) = call(
        plane_sum_kernel, "sum_plane",
        [((depth, 2 * Y_SIZE, width), BF16)],
        [], [plane_arrived, pair_bias],
    )
    depth_arrived = swap(depth_send, "z")
    weight_send, depth_bias = call(
        functools.partial(weight_kernel, scale), "sum_weights",
        [((depth, 2 * Y_SIZE, LANES), BF16), ((1, width), F32)],
        [], [depth_arrived],
    )
    weight_depth = swap(weight_send, "z")
    share = rows // reps
    row_keep, *row_sends = call(
        scatter_kernel, "return_rows",
        [((CORES * share, width), F32)] + [((CORES * share + 16, width), BF16)] * (X_SIZE - 1),
        [rep], [lists, depth_arrived, own, depth_bias],
        scratch=[pltpu.VMEM((rows, width), F32)],
        flops=4 * parts * rows * width, after=[weight_send],
    )
    row_arrived = [
        lax.ppermute(row_sends[step - 1], "x", [(x, x ^ step) for x in range(X_SIZE)])
        for step in (2, 1, 3)
    ]
    (weight_rows,) = call(
        gather_kernel, "gather_weights", [((width // PLANE, width), BF16)],
        [], [weight_depth], flops=window, after=[row_keep],
    )
    row_own, row_send, x_bias, bias_send = call(
        row_sum_kernel, "sum_rows",
        [((share, width), F32), ((share, width), BF16), ((1, width), F32), ((16, width), BF16)],
        [], [row_keep, depth_bias, *row_arrived], flops=window,
    )
    bias_arrived = [
        lax.ppermute(bias_send, "y", [(y, y ^ step) for y in range(Y_SIZE)])
        for step in range(1, Y_SIZE)
    ]
    (weight_plane,) = call(
        spread_kernel, "spread_weights", [((PLANE, width // PLANE, width), BF16)],
        [], [weight_rows],
    )
    weight_near = swap(weight_plane, ("y", "x")).reshape(width, width)
    (last_send,) = call(
        join_kernel, "join", [((width + share, width), BF16)], [], [weight_near, row_send],
        after=bias_arrived,
    )
    grad_self, grad_neigh, input_grad, grad_bias = call(
        finish_kernel, "finish",
        [
            ((width, width), BF16),
            ((width, width), BF16),
            ((share, width), F32),
            ((1, width), F32),
        ],
        [core], [weight_near, row_own, x_bias, pair(last_send), *bias_arrived],
    )
    return (out, input_grad, grad_self, grad_neigh, grad_bias.reshape(width))


def solution(mesh):
    parts = mesh.shape["dom"]
    physical = Mesh(
        mesh.devices.reshape(parts // Y_SIZE, Y_SIZE, X_SIZE, CORES), ("z", "y", "x", "core")
    )
    dom = ("z", "y")
    every = ("z", "y", "x", "core")
    placed = (
        P(dom, None),
        P(dom, None, None),
        P(every),
        P(every, None, None),
        P(every, None),
        P(every, None),
        P(every),
        P(),
        P(),
        P(),
        P(every, None),
    )
    return jax.shard_map(
        body,
        mesh=physical,
        in_specs=placed,
        out_specs=(P(every, None), P(every, None), P(), P(), P()),
        check_vma=False,
    )
```

```python
import functools
import math

import jax
import jax.numpy as jnp
from jax import lax
from jax.experimental import pallas as pl
from jax.experimental.pallas import tpu as pltpu
from jax.sharding import Mesh
from jax.sharding import PartitionSpec as P

BLK = 128
LANES = 128
SLOTS = 8
X_SIZE = 4
CORES = 2
Y_SIZE = 4
PLANE = Y_SIZE * X_SIZE
BF16 = jnp.bfloat16
F32 = jnp.float32
ROUND_FLOPS = 0
SUM_FLOPS = 20_000_000_000
VMEM_BYTES = 24 * 1024 * 1024
FULL_VMEM_BYTES = 65 * 1000 * 1024


def dot(a, b, contract_a=1, contract_b=0):
    return lax.dot_general(
        a, b, (((contract_a,), (contract_b,)), ((), ())), preferred_element_type=F32
    )


def move(matrix, rows):
    return dot(matrix.astype(BF16), rows).astype(BF16)


def iota(shape, dim):
    return lax.broadcasted_iota(jnp.int32, shape, dim)


def split(wide):
    high = wide.astype(BF16)
    return high, (wide - high.astype(F32)).astype(BF16)


def call(kernel, name, outs, scalars, arrays, scratch=(), flops=0, after=(), hbm=(), hbm_outs=(), limit=VMEM_BYTES):
    if after:
        inner, at = kernel, len(scalars) + len(arrays) + len(hbm)
        kernel = lambda *refs: inner(*refs[:at], *refs[at + len(after) :])
    shapes = tuple(jax.ShapeDtypeStruct(shape, dtype) for shape, dtype in outs)
    shapes += tuple(pltpu.HBM(shape, dtype) for shape, dtype in hbm_outs)
    size = sum(math.prod(a.shape) * a.dtype.itemsize for a in (*arrays, *hbm, *shapes))
    return pl.pallas_call(
        kernel,
        out_shape=shapes,
        in_specs=[pl.BlockSpec(memory_space=pltpu.SMEM)] * len(scalars)
        + [pl.BlockSpec(memory_space=pltpu.VMEM)] * len(arrays)
        + [pl.BlockSpec(memory_space=pltpu.HBM)] * len(hbm)
        + [pl.BlockSpec(memory_space=pl.ANY)] * len(after),
        out_specs=tuple([pl.BlockSpec(memory_space=pltpu.VMEM)] * len(outs))
        + tuple([pl.BlockSpec(memory_space=pltpu.HBM)] * len(hbm_outs)),
        scratch_shapes=list(scratch),
        compiler_params=pltpu.CompilerParams(vmem_limit_bytes=limit),
        cost_estimate=pl.CostEstimate(flops=flops, bytes_accessed=size, transcendentals=0),
        name=name,
    )(*scalars, *arrays, *hbm, *after)


def fetched(arrays):
    return [pltpu.VMEM(a.shape, a.dtype) for a in arrays] + [
        pltpu.SemaphoreType.DMA((len(arrays),))
    ]


def fetch(from_refs, to_refs, sems):
    copies = [
        pltpu.make_async_copy(source, to, sems.at[at])
        for at, (source, to) in enumerate(zip(from_refs, to_refs))
    ]
    for copy in copies:
        copy.start()
    return copies


def place_tiles(dst_ref, src_ref, count_ref, tiles_ref, adj_ref, first, last):
    adj_ref[...] = jnp.zeros_like(adj_ref)

    def step(slot, carry):
        block = src_ref[0, slot]

        @pl.when(jnp.logical_and(block >= first, block < last))
        def _():
            row = pl.multiple_of(dst_ref[0, slot] * BLK, BLK)
            col = pl.multiple_of((block - first) * BLK, BLK)
            adj_ref[pl.ds(row, BLK), pl.ds(col, BLK)] = tiles_ref[slot]

        return carry

    lax.fori_loop(0, count_ref[0], step, 0)


def boundary_places(rep, lists_ref, rows, order):
    slots, parts = lists_ref.shape
    lists = lists_ref[...].astype(F32)
    wanted = jnp.sum(
        jnp.where(iota((slots, parts), 0) == rep, lists, 0.0), axis=0, keepdims=True
    ).astype(jnp.int32)
    place = iota((rows, parts), 0)
    places = jnp.concatenate([(place == wanted).astype(BF16), (place == rep).astype(BF16)], 1)
    return dot(places, order.astype(BF16), 1, 1).astype(BF16)


def by_z(parts):
    shape = (2 * parts, 2 * parts)
    out, into = iota(shape, 0), iota(shape, 1)
    y, kind, z = out % Y_SIZE, out // Y_SIZE % 2, out // (2 * Y_SIZE)
    return into == kind * parts + z * Y_SIZE + y


def summed_by_z(parts):
    shape = (2 * parts, 2 * parts)
    out, into = iota(shape, 0), iota(shape, 1)
    line, z = out % (2 * Y_SIZE), out // (2 * Y_SIZE)
    halo = jnp.logical_and(line < Y_SIZE, into == z * Y_SIZE + line)
    hub = jnp.logical_and(line == Y_SIZE, into == parts)
    return jnp.logical_or(halo, hub)


def send_kernel(rep_ref, lists_hbm, feats_hbm, send_ref, lists_ref, feats_ref, sems):
    lists_copy, feats_copy = fetch((lists_hbm, feats_hbm), (lists_ref, feats_ref), sems)
    lists_copy.wait()
    parts = lists_ref.shape[1]
    places = boundary_places(rep_ref[0], lists_ref, feats_ref.shape[0], by_z(parts))
    feats_copy.wait()
    send_ref[...] = dot(places, feats_ref[...], 0, 0).astype(BF16)


def plane_kernel(arrived_ref, send_ref):
    chunk = send_ref.shape[1]
    depth = chunk // 2
    total = arrived_ref.shape[0]
    shape = (total, total)
    out, into = iota(shape, 0), iota(shape, 1)
    z, kind, y = out % depth, out // depth % 2, out // chunk
    moved = move(into == z * (2 * Y_SIZE) + kind * Y_SIZE + y, arrived_ref[...])
    for y_to in range(Y_SIZE):
        for x_to in range(X_SIZE):
            send_ref[y_to * X_SIZE + x_to] = moved[y_to * chunk : (y_to + 1) * chunk]


def own_kernel(
    core_ref, dst_ref, src_ref, count_ref, tiles_ref, feats_ref, seeds_ref, w_self_ref, bias_ref,
    mats_ref, sums_ref, own_adj_ref, adj_ref,
):
    rows = feats_ref.shape[0]
    seeds = seeds_ref.shape[1]
    own_blocks = rows // BLK
    table = adj_ref.shape[1]
    place_tiles(dst_ref, src_ref, count_ref, tiles_ref, own_adj_ref, 0, own_blocks)
    place_tiles(
        dst_ref, src_ref, count_ref, tiles_ref, adj_ref, own_blocks, own_blocks + table // BLK
    )
    picks = (iota((rows, seeds), 0) == seeds_ref[...]).astype(BF16)
    feats = feats_ref[...]
    mats_ref[2 * seeds + adj_ref.shape[1] :, :seeds] = dot(feats, picks, 0, 0).astype(BF16)
    chosen = dot(picks, feats, 0, 0).astype(BF16)
    sums_ref[:seeds] = dot(chosen, w_self_ref[...]) + bias_ref[...].astype(F32)
    sums_ref[seeds:] = dot(own_adj_ref[...], feats)
    adj = adj_ref[...]
    half = table // 2
    depth = half // PLANE // 2
    shape = (half, table)
    line, source = iota(shape, 0), iota(shape, 1)
    z, kind = line % depth, line // depth % 2
    x, y = line // (2 * depth) % X_SIZE, line // (2 * depth * X_SIZE)
    start = kind * half + (z * Y_SIZE + y) * SLOTS + x * CORES
    for far, core in enumerate((core_ref[0], 1 - core_ref[0])):
        order = (source == start + core).astype(BF16)
        mats_ref[far * seeds : (far + 1) * seeds, :half] = dot(adj, order, 1, 1).astype(BF16)
        first = 2 * seeds + far * half
        mats_ref[first : first + half, :seeds] = dot(order, adj, 1, 1).astype(BF16)


def middle_kernel(
    core_ref, near_ref, far_ref, mats_ref, sums_ref, w_neigh_ref, cot_ref,
    out_ref, d_pre_ref, d_agg_ref, keep_ref, send_ref,
):
    width = w_neigh_ref.shape[0]
    half = near_ref.shape[0]
    seeds = cot_ref.shape[0]
    near_back, far_back, chosen_t = (2 * seeds + step * half for step in range(3))
    aggregate = (
        sums_ref[seeds:]
        + dot(mats_ref[:seeds, :half], near_ref[...])
        + dot(mats_ref[seeds : 2 * seeds, :half], far_ref[...])
    ).astype(BF16)
    preact = sums_ref[:seeds] + dot(aggregate, w_neigh_ref[...])
    gate = jax.nn.sigmoid(preact)
    out_ref[...] = (preact * gate).astype(BF16)
    d_pre = (cot_ref[...].astype(F32) * gate * (1.0 + preact * (1.0 - gate))).astype(BF16)
    d_pre_ref[...] = d_pre
    d_agg = dot(d_pre, w_neigh_ref[...], 1, 1).astype(BF16)
    d_agg_ref[...] = d_agg
    first = dot(mats_ref[chosen_t:, :seeds], d_pre).astype(BF16)
    second = dot(aggregate, d_pre, 0, 0).astype(BF16)
    is_first = core_ref[0] == 0
    keep_ref[:width] = jnp.where(is_first, first, second)
    send_ref[:width] = jnp.where(is_first, second, first)
    keep_ref[width : width + half] = dot(mats_ref[near_back:far_back, :seeds], d_agg).astype(BF16)
    send_ref[width : width + half] = dot(mats_ref[far_back:chosen_t, :seeds], d_agg).astype(BF16)
    high, low = split(jnp.sum(d_pre.astype(F32), 0, keepdims=True))
    row = iota((keep_ref.shape[0] - width - half, width), 0)
    pair = jnp.where(
        row == 0, high.astype(F32), jnp.where(row == 1, low.astype(F32), 0.0)
    ).astype(BF16)
    keep_ref[width + half :] = pair
    send_ref[width + half :] = pair


def pair_sum_kernel(keep_ref, other_ref, send_ref):
    chunks, lines, width = send_ref.shape
    total = keep_ref[...].astype(F32) + other_ref[...].astype(F32)
    weight, table = width // chunks, (lines - 8 - width // chunks)
    tail = width + chunks * table
    high, low = split(total[tail : tail + 1] + total[tail + 1 : tail + 2])
    row = iota((8, width), 0)
    pair = jnp.where(row == 0, high.astype(F32), jnp.where(row == 1, low.astype(F32), 0.0))
    for chunk in range(chunks):
        send_ref[chunk] = jnp.concatenate(
            [
                total[chunk * weight : (chunk + 1) * weight],
                total[width + chunk * table : width + (chunk + 1) * table],
                pair,
            ],
            0,
        ).astype(BF16)


def plane_sum_kernel(arrived_ref, send_ref, round_ref, whole_ref):
    chunks, lines, width = arrived_ref.shape
    depth, block, _ = send_ref.shape
    weight = width // chunks
    tail = weight + 2 * depth
    rows = []
    rest = None
    for y in range(Y_SIZE):
        some = arrived_ref[y * X_SIZE].astype(F32)
        for x in range(1, X_SIZE):
            some = some + arrived_ref[y * X_SIZE + x].astype(F32)
        rows.append(some[weight : weight + depth])
        rest = some if rest is None else rest + some
    rows = jnp.concatenate(rows + [rest[weight + depth : tail]], 0).astype(BF16)
    shape = (depth * block, rows.shape[0])
    out, into = iota(shape, 0), iota(shape, 1)
    line, z = out % block, out // block
    wanted = jnp.where(line <= Y_SIZE, line * depth + z, -1)
    send_ref[...] = move(into == wanted, rows).reshape(depth, block, width)
    whole_ref[:weight] = rest[:weight]
    bias = jnp.sum(rest[tail:], 0, keepdims=True)
    row = iota((whole_ref.shape[0] - weight, width), 0)
    whole_ref[weight:] = jnp.where(row == 0, bias, 0.0)
    round_ref[...] = whole_ref[...].astype(BF16)


def sum_four(own_ref, beside_ref, far_ref, farther_ref):
    pair = own_ref[...].astype(F32) + beside_ref[...].astype(F32)
    return pair + (far_ref[...].astype(F32) + farther_ref[...].astype(F32))


def round_kernel(own_ref, beside_ref, far_ref, farther_ref, send_ref):
    send_ref[...] = sum_four(own_ref, beside_ref, far_ref, farther_ref).astype(BF16)


def weight_kernel(scale, own_ref, beside_ref, far_ref, farther_ref, whole_ref, bias_ref):
    weight = whole_ref.shape[0]
    total = sum_four(own_ref, beside_ref, far_ref, farther_ref) * scale
    whole_ref[...] = total[:weight].astype(BF16)
    bias_ref[...] = jnp.sum(total[weight:], 0, keepdims=True)


def spread_kernel(whole_ref, send_ref):
    for chunk in range(send_ref.shape[0]):
        send_ref[chunk] = whole_ref[...]


def own_back_kernel(
    dst_ref, src_ref, count_ref, tiles_ref, seeds_ref, d_pre_ref, d_agg_ref, w_self_ref,
    own_ref, adj_ref,
):
    rows = own_ref.shape[0]
    seeds = seeds_ref.shape[1]
    place_tiles(dst_ref, src_ref, count_ref, tiles_ref, adj_ref, 0, rows // BLK)
    picks = (iota((rows, seeds), 0) == seeds_ref[...]).astype(BF16)
    seeded = dot(picks, d_pre_ref[...]).astype(BF16)
    own_ref[...] = dot(seeded, w_self_ref[...], 1, 1) + dot(adj_ref[...], d_agg_ref[...], 0, 0)


def scatter_kernel(rep_ref, lists_ref, arrived_ref, own_ref, keep_ref, *send_refs_and_total):
    *send_refs, total_ref = send_refs_and_total
    rows, width = own_ref.shape
    rep = rep_ref[0]
    places = boundary_places(rep, lists_ref, rows, summed_by_z(lists_ref.shape[1]))
    back = arrived_ref[...].reshape(places.shape[1], width)
    total_ref[...] = own_ref[...] + dot(places, back)
    share = rows // (X_SIZE * CORES)
    for step, ref in enumerate([keep_ref, *send_refs]):
        for core in range(CORES):
            place = jnp.bitwise_xor(rep, step * CORES + core)
            some = total_ref[pl.ds(pl.multiple_of(place * share, 32), share), :]
            ref[core * share : (core + 1) * share] = some.astype(ref.dtype)


def row_sum_kernel(keep_ref, *refs):
    *arrived_refs, own_ref, send_ref = refs
    share = own_ref.shape[0]
    total = keep_ref[...]
    for ref in arrived_refs:
        total = total + ref[...].astype(F32)
    own_ref[...] = total[:share]
    send_ref[...] = total[share:].astype(BF16)


def join_kernel(weights_ref, rows_ref, send_ref):
    width = weights_ref.shape[0]
    send_ref[:width] = weights_ref[...]
    send_ref[width:] = rows_ref[...]


def finish_kernel(core_ref, near_ref, own_ref, far_ref, first_ref, second_ref, rows_ref):
    width = near_ref.shape[0]
    near, far = near_ref[...], far_ref[:width]
    is_first = core_ref[0] == 0
    first_ref[...] = jnp.where(is_first, near, far)
    second_ref[...] = jnp.where(is_first, far, near)
    rows_ref[...] = own_ref[...] + far_ref[width:].astype(F32)


def body(
    feats,
    halo_index,
    seed_ids,
    tiles,
    tile_dst,
    tile_src,
    tile_count,
    w_self,
    w_neigh,
    bias,
    cotangent,
):
    depth = lax.axis_size("z")
    parts = depth * Y_SIZE
    reps = X_SIZE * CORES
    rows, width = feats.shape
    seeds = cotangent.shape[0]
    half = parts * SLOTS
    core_id = lax.axis_index("core").astype(jnp.int32)
    x_id = lax.axis_index("x").astype(jnp.int32)
    core = core_id.reshape(1)
    rep = (x_id * CORES + core_id).reshape(1)
    lists = halo_index[0].T
    seed_row = seed_ids.reshape(1, seeds)
    tile_scalars = (tile_dst, tile_src, tile_count)
    scale = float(seeds * parts * reps) ** (-0.5)

    window = 20_000_000_000

    def swap(values, axis):
        return lax.all_to_all(values, axis, split_axis=0, concat_axis=0, tiled=True)

    def pair(values):
        return lax.ppermute(values, "core", [(0, 1), (1, 0)])

    (send,) = call(
        send_kernel, "pick_boundary", [((2 * parts, width), BF16)], [rep], [], hbm=[lists, feats],
        scratch=fetched([lists, feats]), flops=4 * parts * rows * width, limit=FULL_VMEM_BYTES,
    )
    by_depth = swap(send.reshape(depth, 2 * Y_SIZE, width), "z").reshape(2 * parts, width)
    mats, sums = call(
        own_kernel, "own_rows",
        [
            ((2 * (seeds + half) + width, max(seeds, half)), BF16),
            ((2 * seeds, width), F32),
        ],
        [core, *tile_scalars],
        [tiles, feats, seed_row, w_self, bias.reshape(1, width)],
        scratch=[pltpu.VMEM((seeds, rows), BF16), pltpu.VMEM((seeds, 2 * half), BF16)],
        flops=2 * seeds * (3 * rows * width + width * width + 8 * half * half),
    )

    (plane,) = call(
        plane_kernel, "spread_plane", [((PLANE, 2 * depth, width), BF16)], [], [by_depth],
        flops=8 * parts * parts * width, after=[sums],
    )
    near = swap(plane, ("y", "x")).reshape(half, width)
    far = pair(near)

    out, d_pre, d_agg, keep, pair_send = call(
        middle_kernel, "forward_backward",
        [
            ((seeds, width), BF16),
            ((seeds, width), BF16),
            ((seeds, width), BF16),
            ((width + half + 16, width), BF16),
            ((width + half + 16, width), BF16),
        ],
        [core],
        [
            near, far, mats, sums, w_neigh, cotangent,
        ],
        flops=2 * seeds * width * (4 * half + 4 * width),
    )

    pair_arrived = pair(pair_send)
    (own,) = call(
        own_back_kernel, "own_rows_back", [((rows, width), F32)],
        [*tile_scalars], [tiles, seed_row, d_pre, d_agg, w_self],
        scratch=[pltpu.VMEM((seeds, rows), BF16)],
        flops=2 * seeds * width * 3 * rows,
    )
    (plane_send,) = call(
        pair_sum_kernel, "sum_pair",
        [((PLANE, width // PLANE + 2 * depth + 8, width), BF16)],
        [], [keep, pair_arrived], after=[own],
    )
    plane_arrived = swap(plane_send, ("y", "x"))
    weight = width // PLANE
    depth_send, round_send = call(
        plane_sum_kernel, "sum_plane",
        [((depth, 2 * Y_SIZE, width), BF16), ((weight + 16, width), BF16)],
        [], [plane_arrived],
        scratch=[pltpu.VMEM((weight + 16, width), F32)],
    )
    depth_arrived = swap(depth_send, "z")

    def four(values, stride):
        steps = [stride * step for step in range(1, 4)] if stride < depth else [0, 0, 0]
        moved = {
            step: lax.ppermute(values, "z", [(z, z ^ step) for z in range(depth)])
            for step in sorted(steps, key=lambda step: -min(step, depth - step))
            if step
        }
        return [values] + [moved[step] if step else jnp.zeros_like(values) for step in steps]

    (round_send,) = call(
        round_kernel, "sum_round", [((weight + 16, width), BF16)], [], four(round_send, 1),
        flops=ROUND_FLOPS,
    )
    weight_rows, bias_row = call(
        functools.partial(weight_kernel, scale), "sum_weights",
        [((weight, width), BF16), ((1, width), F32)], [], four(round_send, 4),
        flops=SUM_FLOPS,
    )
    share = rows // reps
    row_keep, *row_sends = call(
        scatter_kernel, "return_rows",
        [((CORES * share, width), F32)] + [((CORES * share, width), BF16)] * (X_SIZE - 1),
        [rep], [lists, depth_arrived, own],
        scratch=[pltpu.VMEM((rows, width), F32)],
        flops=4 * parts * rows * width,
    )
    row_arrived = [
        lax.ppermute(row_sends[step - 1], "x", [(x, x ^ step) for x in range(X_SIZE)])
        for step in (2, 1, 3)
    ]
    row_own, row_send = call(
        row_sum_kernel, "sum_rows", [((share, width), F32), ((share, width), BF16)],
        [], [row_keep, *row_arrived], flops=window,
    )
    (weight_plane,) = call(
        spread_kernel, "spread_weights", [((PLANE, width // PLANE, width), BF16)],
        [], [weight_rows], after=[row_keep],
    )
    weight_near = swap(weight_plane, ("y", "x")).reshape(width, width)
    (last_send,) = call(
        join_kernel, "join", [((width + share, width), BF16)], [], [weight_near, row_send]
    )
    grad_self, grad_neigh, input_grad = call(
        finish_kernel, "finish",
        [((width, width), BF16), ((width, width), BF16), ((share, width), F32)],
        [core], [weight_near, row_own, pair(last_send)],
    )
    grad_bias = bias_row.reshape(width)
    return (out, input_grad, grad_self, grad_neigh, grad_bias)


def solution(mesh):
    parts = mesh.shape["dom"]
    physical = Mesh(
        mesh.devices.reshape(parts // Y_SIZE, Y_SIZE, X_SIZE, CORES), ("z", "y", "x", "core")
    )
    dom = ("z", "y")
    every = ("z", "y", "x", "core")
    placed = (
        P(dom, None),
        P(dom, None, None),
        P(every),
        P(every, None, None),
        P(every, None),
        P(every, None),
        P(every),
        P(),
        P(),
        P(),
        P(every, None),
    )
    return jax.shard_map(
        body,
        mesh=physical,
        in_specs=placed,
        out_specs=(P(every, None), P(every, None), P(), P(), P()),
        check_vma=False,
    )
```

```python
import functools
import math

import jax
import jax.numpy as jnp
from jax import lax
from jax.experimental import pallas as pl
from jax.experimental.pallas import tpu as pltpu
from jax.sharding import Mesh
from jax.sharding import PartitionSpec as P

BLK = 128
LANES = 128
SLOTS = 8
X_SIZE = 4
CORES = 2
Y_SIZE = 4
PLANE = Y_SIZE * X_SIZE
BF16 = jnp.bfloat16
F32 = jnp.float32
VMEM_BYTES = 24 * 1024 * 1024
FULL_VMEM_BYTES = 65 * 1000 * 1024


def dot(a, b, contract_a=1, contract_b=0):
    return lax.dot_general(
        a, b, (((contract_a,), (contract_b,)), ((), ())), preferred_element_type=F32
    )


def move(matrix, rows):
    return dot(matrix.astype(BF16), rows).astype(BF16)


def iota(shape, dim):
    return lax.broadcasted_iota(jnp.int32, shape, dim)


def two_rows(wide, rows):
    high = wide.astype(BF16).astype(F32)
    row = iota((rows, wide.shape[1]), 0)
    return jnp.where(row == 0, high, jnp.where(row == 1, wide - high, 0.0)).astype(BF16)


def call(kernel, name, outs, scalars, arrays, scratch=(), flops=0, after=(), hbm=(), hbm_outs=(), limit=VMEM_BYTES):
    if after:
        inner, at = kernel, len(scalars) + len(arrays) + len(hbm)
        kernel = lambda *refs: inner(*refs[:at], *refs[at + len(after) :])
    shapes = tuple(jax.ShapeDtypeStruct(shape, dtype) for shape, dtype in outs)
    shapes += tuple(pltpu.HBM(shape, dtype) for shape, dtype in hbm_outs)
    size = sum(math.prod(a.shape) * a.dtype.itemsize for a in (*arrays, *hbm, *shapes))
    return pl.pallas_call(
        kernel,
        out_shape=shapes,
        in_specs=[pl.BlockSpec(memory_space=pltpu.SMEM)] * len(scalars)
        + [pl.BlockSpec(memory_space=pltpu.VMEM)] * len(arrays)
        + [pl.BlockSpec(memory_space=pltpu.HBM)] * len(hbm)
        + [pl.BlockSpec(memory_space=pl.ANY)] * len(after),
        out_specs=tuple([pl.BlockSpec(memory_space=pltpu.VMEM)] * len(outs))
        + tuple([pl.BlockSpec(memory_space=pltpu.HBM)] * len(hbm_outs)),
        scratch_shapes=list(scratch),
        compiler_params=pltpu.CompilerParams(vmem_limit_bytes=limit),
        cost_estimate=pl.CostEstimate(flops=flops, bytes_accessed=size, transcendentals=0),
        name=name,
    )(*scalars, *arrays, *hbm, *after)


def fetched(arrays):
    return [pltpu.VMEM(a.shape, a.dtype) for a in arrays] + [
        pltpu.SemaphoreType.DMA((len(arrays),))
    ]


def fetch(from_refs, to_refs, sems):
    copies = [
        pltpu.make_async_copy(source, to, sems.at[at])
        for at, (source, to) in enumerate(zip(from_refs, to_refs))
    ]
    for copy in copies:
        copy.start()
    return copies


def place_tiles(dst_ref, src_ref, count_ref, tiles_ref, adj_ref, first, last):
    adj_ref[...] = jnp.zeros_like(adj_ref)

    def step(slot, carry):
        block = src_ref[0, slot]

        @pl.when(jnp.logical_and(block >= first, block < last))
        def _():
            row = pl.multiple_of(dst_ref[0, slot] * BLK, BLK)
            col = pl.multiple_of((block - first) * BLK, BLK)
            adj_ref[pl.ds(row, BLK), pl.ds(col, BLK)] = tiles_ref[slot]

        return carry

    lax.fori_loop(0, count_ref[0], step, 0)


def boundary_places(rep, lists_ref, rows, order):
    slots, parts = lists_ref.shape
    lists = lists_ref[...].astype(F32)
    wanted = jnp.sum(
        jnp.where(iota((slots, parts), 0) == rep, lists, 0.0), axis=0, keepdims=True
    ).astype(jnp.int32)
    place = iota((rows, parts), 0)
    places = jnp.concatenate([(place == wanted).astype(BF16), (place == rep).astype(BF16)], 1)
    return dot(places, order.astype(BF16), 1, 1).astype(BF16)


def summed_by_z(parts):
    shape = (2 * parts, 2 * parts)
    out, into = iota(shape, 0), iota(shape, 1)
    line, z = out % (2 * Y_SIZE), out // (2 * Y_SIZE)
    halo = jnp.logical_and(line < Y_SIZE, into == z * Y_SIZE + line)
    hub = jnp.logical_and(line == Y_SIZE, into == parts)
    return jnp.logical_or(halo, hub)


def send_kernel(rep_ref, lists_hbm, feats_hbm, send_ref, lists_ref, feats_ref, sems):
    lists_copy, feats_copy = fetch((lists_hbm, feats_hbm), (lists_ref, feats_ref), sems)
    slots, parts = lists_ref.shape
    depth = parts // Y_SIZE
    rep = rep_ref[0]
    shape = (2 * parts, parts)
    out, into = iota(shape, 0), iota(shape, 1)
    row, z = out % (2 * Y_SIZE), out // (2 * Y_SIZE)
    of_part = (into == z * Y_SIZE + row % Y_SIZE).astype(BF16)
    lists_copy.wait()
    lists = lists_ref[...]
    high, low = (lists // 256).astype(BF16), (lists % 256).astype(BF16)
    wanted = dot(of_part, high, 1, 1) * 256.0 + dot(of_part, low, 1, 1)
    shape = (2 * parts, slots)
    row = iota(shape, 0) % (2 * Y_SIZE)
    wanted = jnp.where(row < Y_SIZE, wanted, rep.astype(F32))
    wanted = jnp.sum(jnp.where(iota(shape, 1) == rep, wanted, 0.0), axis=1, keepdims=True)
    places = iota((2 * parts, feats_ref.shape[0]), 1) == wanted.astype(jnp.int32)
    places = places.astype(BF16)
    feats_copy.wait()
    rows = dot(places, feats_ref[...]).astype(BF16)
    lines = send_ref.shape[0] // depth
    shape = (depth * lines, 2 * parts)
    out, into = iota(shape, 0), iota(shape, 1)
    line, z = out % lines, out // lines
    packed = jnp.zeros(send_ref.shape, F32)
    for group in range(rows.shape[1] // LANES):
        first = group * (Y_SIZE + 1)
        wanted = jnp.where(
            jnp.logical_and(line >= first, line <= first + Y_SIZE),
            z * (2 * Y_SIZE) + line - first,
            -1,
        )
        lanes = slice(group * LANES, (group + 1) * LANES)
        packed += dot((into == wanted).astype(BF16), rows[:, lanes])
    send_ref[...] = packed.astype(BF16)


def plane_kernel(arrived_ref, send_ref):
    _, chunk, width = send_ref.shape
    depth = chunk // 2
    total = arrived_ref.shape[0]
    lines = total // depth
    shape = (Y_SIZE * chunk, total)
    out, into = iota(shape, 0), iota(shape, 1)
    z, kind, y = out % depth, out // depth % 2, out // chunk
    first = z * lines + jnp.where(kind == 0, y, Y_SIZE)
    arrived = arrived_ref[...]
    for group in range(width // LANES):
        moved = move(into == first + group * (Y_SIZE + 1), arrived)
        lanes = slice(group * LANES, (group + 1) * LANES)
        for y_to in range(Y_SIZE):
            for x_to in range(X_SIZE):
                send_ref[y_to * X_SIZE + x_to, :, lanes] = moved[y_to * chunk : (y_to + 1) * chunk]


def own_kernel(
    core_ref, dst_ref, src_ref, count_ref, tiles_ref, feats_ref, seeds_ref, w_self_ref, bias_ref,
    mats_ref, sums_ref, own_adj_ref, adj_ref,
):
    rows = feats_ref.shape[0]
    seeds = seeds_ref.shape[1]
    own_blocks = rows // BLK
    table = adj_ref.shape[1]
    place_tiles(dst_ref, src_ref, count_ref, tiles_ref, own_adj_ref, 0, own_blocks)
    place_tiles(
        dst_ref, src_ref, count_ref, tiles_ref, adj_ref, own_blocks, own_blocks + table // BLK
    )
    picks = (iota((rows, seeds), 0) == seeds_ref[...]).astype(BF16)
    feats = feats_ref[...]
    mats_ref[2 * seeds + adj_ref.shape[1] :, :seeds] = dot(feats, picks, 0, 0).astype(BF16)
    chosen = dot(picks, feats, 0, 0).astype(BF16)
    sums_ref[:seeds] = dot(chosen, w_self_ref[...]) + bias_ref[...].astype(F32)
    sums_ref[seeds:] = dot(own_adj_ref[...], feats)
    adj = adj_ref[...]
    half = table // 2
    depth = half // PLANE // 2
    shape = (half, table)
    line, source = iota(shape, 0), iota(shape, 1)
    z, kind = line % depth, line // depth % 2
    x, y = line // (2 * depth) % X_SIZE, line // (2 * depth * X_SIZE)
    start = kind * half + (z * Y_SIZE + y) * SLOTS + x * CORES
    for far, core in enumerate((core_ref[0], 1 - core_ref[0])):
        order = (source == start + core).astype(BF16)
        mats_ref[far * seeds : (far + 1) * seeds, :half] = dot(adj, order, 1, 1).astype(BF16)
        first = 2 * seeds + far * half
        mats_ref[first : first + half, :seeds] = dot(order, adj, 1, 1).astype(BF16)


def middle_kernel(
    core_ref, near_ref, far_ref, mats_ref, sums_ref, w_neigh_ref, cot_ref,
    out_ref, d_pre_ref, d_agg_ref, keep_ref, send_ref,
):
    width = w_neigh_ref.shape[0]
    half = near_ref.shape[0]
    seeds = cot_ref.shape[0]
    near_back, far_back, chosen_t = (2 * seeds + step * half for step in range(3))
    aggregate = (
        sums_ref[seeds:]
        + dot(mats_ref[:seeds, :half], near_ref[...])
        + dot(mats_ref[seeds : 2 * seeds, :half], far_ref[...])
    ).astype(BF16)
    preact = sums_ref[:seeds] + dot(aggregate, w_neigh_ref[...])
    gate = jax.nn.sigmoid(preact)
    out_ref[...] = (preact * gate).astype(BF16)
    d_pre = (cot_ref[...].astype(F32) * gate * (1.0 + preact * (1.0 - gate))).astype(BF16)
    d_pre_ref[...] = d_pre
    d_agg = dot(d_pre, w_neigh_ref[...], 1, 1).astype(BF16)
    d_agg_ref[...] = d_agg
    first = dot(mats_ref[chosen_t:, :seeds], d_pre).astype(BF16)
    second = dot(aggregate, d_pre, 0, 0).astype(BF16)
    is_first = core_ref[0] == 0
    keep_ref[:width] = jnp.where(is_first, first, second)
    send_ref[:width] = jnp.where(is_first, second, first)
    keep_ref[width : width + half] = dot(mats_ref[near_back:far_back, :seeds], d_agg).astype(BF16)
    send_ref[width : width + half] = dot(mats_ref[far_back:chosen_t, :seeds], d_agg).astype(BF16)
    bias = two_rows(jnp.sum(d_pre.astype(F32), 0, keepdims=True), keep_ref.shape[0] - width - half)
    keep_ref[width + half :] = bias
    send_ref[width + half :] = bias


def pair_sum_kernel(keep_ref, other_ref, send_ref, bias_ref):
    chunks, lines, width = send_ref.shape
    total = keep_ref[...].astype(F32) + other_ref[...].astype(F32)
    weight = width // chunks
    table = lines - weight
    bias_ref[...] = jnp.sum(total[width + chunks * table :], 0, keepdims=True)
    total = total.astype(BF16)
    for chunk in range(chunks):
        send_ref[chunk, :weight] = total[chunk * weight : (chunk + 1) * weight]
        send_ref[chunk, weight:] = total[width + chunk * table : width + (chunk + 1) * table]


def plane_sum_kernel(arrived_ref, bias_ref, send_ref):
    chunks, lines, width = arrived_ref.shape
    depth, block, _ = send_ref.shape
    weight = width // chunks
    each = weight // depth
    tail = weight + 2 * depth
    rows = []
    rest = None
    for y in range(Y_SIZE):
        some = arrived_ref[y * X_SIZE].astype(F32)
        for x in range(1, X_SIZE):
            some = some + arrived_ref[y * X_SIZE + x].astype(F32)
        rows.append(some[weight : weight + depth])
        rest = some if rest is None else rest + some
    bias = jnp.zeros((depth, width), F32) + bias_ref[...]
    rows += [rest[weight + depth : tail], rest[:weight], bias]
    rows = jnp.concatenate(rows, 0).astype(BF16)
    shape = (depth * block, rows.shape[0])
    out, into = iota(shape, 0), iota(shape, 1)
    line, z = out % block, out // block
    first = (Y_SIZE + 1) * depth
    of_weight = jnp.logical_and(line > Y_SIZE, line <= Y_SIZE + each)
    wanted = jnp.where(
        of_weight,
        first + z * each + line - Y_SIZE - 1,
        jnp.where(line <= Y_SIZE, line * depth, first + weight) + z,
    )
    send_ref[...] = move(into == wanted, rows).reshape(depth, block, width)


def weight_kernel(scale, arrived_ref, send_ref, bias_ref):
    depth, block, width = arrived_ref.shape
    total = jnp.sum(arrived_ref[...].astype(F32), 0) * scale
    each = block - Y_SIZE - 2
    row = iota((block, LANES), 0)
    done = jnp.zeros((block, LANES), F32)
    for group in range(width // LANES):
        for line in range(each):
            some = total[Y_SIZE + 1 + line : Y_SIZE + 2 + line, group * LANES : (group + 1) * LANES]
            done = jnp.where(row == group * each + line, some, done)
    done = done.astype(BF16)
    for z in range(depth):
        send_ref[z] = done
    bias_ref[...] = total[block - 1 :]


def gather_kernel(arrived_ref, whole_ref):
    weight, width = whole_ref.shape
    depth, block, _ = arrived_ref.shape
    groups = width // LANES
    each = weight // depth
    arrived = arrived_ref[...].reshape(depth * block, LANES)
    shape = (weight, depth * block)
    out, into = iota(shape, 0), iota(shape, 1)
    z, line = out // each, out % each
    for group in range(groups):
        rows = move(into == z * block + group * each + line, arrived)
        whole_ref[:, group * LANES : (group + 1) * LANES] = rows


def spread_kernel(whole_ref, bias_ref, send_ref):
    chunks, lines, _ = send_ref.shape
    bias = two_rows(bias_ref[...], lines - whole_ref.shape[0]).astype(F32)
    message = jnp.concatenate([whole_ref[...].astype(F32), bias], 0).astype(BF16)
    for chunk in range(chunks):
        send_ref[chunk] = message


def own_back_kernel(
    dst_ref, src_ref, count_ref, tiles_ref, seeds_ref, d_pre_ref, d_agg_ref, w_self_ref,
    own_ref, adj_ref,
):
    rows = own_ref.shape[0]
    seeds = seeds_ref.shape[1]
    place_tiles(dst_ref, src_ref, count_ref, tiles_ref, adj_ref, 0, rows // BLK)
    picks = (iota((rows, seeds), 0) == seeds_ref[...]).astype(BF16)
    seeded = dot(picks, d_pre_ref[...]).astype(BF16)
    own_ref[...] = dot(seeded, w_self_ref[...], 1, 1) + dot(adj_ref[...], d_agg_ref[...], 0, 0)


def scatter_kernel(rep_ref, lists_ref, arrived_ref, own_ref, keep_ref, *send_refs_and_total):
    *send_refs, total_ref = send_refs_and_total
    rows, width = own_ref.shape
    rep = rep_ref[0]
    places = boundary_places(rep, lists_ref, rows, summed_by_z(lists_ref.shape[1]))
    back = arrived_ref[...].reshape(places.shape[1], width)
    total_ref[...] = own_ref[...] + dot(places, back)
    share = rows // (X_SIZE * CORES)
    for step, ref in enumerate([keep_ref, *send_refs]):
        for core in range(CORES):
            place = jnp.bitwise_xor(rep, step * CORES + core)
            some = total_ref[pl.ds(pl.multiple_of(place * share, 32), share), :]
            ref[core * share : (core + 1) * share] = some.astype(ref.dtype)


def row_sum_kernel(keep_ref, *refs):
    *arrived_refs, own_ref, send_ref = refs
    share = own_ref.shape[0]
    total = keep_ref[...]
    for ref in arrived_refs:
        total = total + ref[...].astype(F32)
    own_ref[...] = total[:share]
    send_ref[...] = total[share:].astype(BF16)


def join_kernel(arrived_ref, rows_ref, send_ref, bias_ref):
    chunks, _, width = arrived_ref.shape
    weight = width // chunks
    bias = jnp.zeros(bias_ref.shape, F32)
    for chunk in range(chunks):
        arrived = arrived_ref[chunk].astype(F32)
        send_ref[chunk * weight : (chunk + 1) * weight] = arrived[:weight].astype(BF16)
        bias = bias + jnp.sum(arrived[weight:], 0, keepdims=True)
    send_ref[width:] = rows_ref[...]
    bias_ref[...] = bias


def finish_kernel(core_ref, near_ref, own_ref, far_ref, first_ref, second_ref, rows_ref):
    width = first_ref.shape[0]
    near, far = near_ref[:width], far_ref[:width]
    is_first = core_ref[0] == 0
    first_ref[...] = jnp.where(is_first, near, far)
    second_ref[...] = jnp.where(is_first, far, near)
    rows_ref[...] = own_ref[...] + far_ref[width:].astype(F32)


def body(
    feats,
    halo_index,
    seed_ids,
    tiles,
    tile_dst,
    tile_src,
    tile_count,
    w_self,
    w_neigh,
    bias,
    cotangent,
):
    depth = lax.axis_size("z")
    parts = depth * Y_SIZE
    reps = X_SIZE * CORES
    rows, width = feats.shape
    seeds = cotangent.shape[0]
    half = parts * SLOTS
    core_id = lax.axis_index("core").astype(jnp.int32)
    x_id = lax.axis_index("x").astype(jnp.int32)
    core = core_id.reshape(1)
    rep = (x_id * CORES + core_id).reshape(1)
    lists = halo_index[0].T
    seed_row = seed_ids.reshape(1, seeds)
    tile_scalars = (tile_dst, tile_src, tile_count)
    scale = float(seeds * parts * reps) ** (-0.5)

    window = 20_000_000_000

    def swap(values, axis):
        return lax.all_to_all(values, axis, split_axis=0, concat_axis=0, tiled=True)

    def pair(values):
        return lax.ppermute(values, "core", [(0, 1), (1, 0)])

    lines = -(-(Y_SIZE + 1) * (width // LANES) // 8) * 8
    (send,) = call(
        send_kernel, "pick_boundary", [((depth * lines, LANES), BF16)], [rep], [],
        hbm=[lists, feats], scratch=fetched([lists, feats]), flops=4 * parts * rows * width,
        limit=FULL_VMEM_BYTES,
    )
    by_depth = swap(send.reshape(depth, lines, LANES), "z").reshape(depth * lines, LANES)
    mats, sums = call(
        own_kernel, "own_rows",
        [
            ((2 * (seeds + half) + width, max(seeds, half)), BF16),
            ((2 * seeds, width), F32),
        ],
        [core, *tile_scalars],
        [tiles, feats, seed_row, w_self, bias.reshape(1, width)],
        scratch=[pltpu.VMEM((seeds, rows), BF16), pltpu.VMEM((seeds, 2 * half), BF16)],
        flops=2 * seeds * (3 * rows * width + width * width + 8 * half * half),
    )

    (plane,) = call(
        plane_kernel, "spread_plane", [((PLANE, 2 * depth, width), BF16)], [], [by_depth],
        flops=8 * parts * parts * width, after=[sums],
    )
    near = swap(plane, ("y", "x")).reshape(half, width)
    far = pair(near)

    out, d_pre, d_agg, keep, pair_send = call(
        middle_kernel, "forward_backward",
        [
            ((seeds, width), BF16),
            ((seeds, width), BF16),
            ((seeds, width), BF16),
            ((width + half + 16, width), BF16),
            ((width + half + 16, width), BF16),
        ],
        [core],
        [
            near, far, mats, sums, w_neigh, cotangent,
        ],
        flops=2 * seeds * width * (4 * half + 4 * width),
    )

    pair_arrived = pair(pair_send)
    (own,) = call(
        own_back_kernel, "own_rows_back", [((rows, width), F32)],
        [*tile_scalars], [tiles, seed_row, d_pre, d_agg, w_self],
        scratch=[pltpu.VMEM((seeds, rows), BF16)],
        flops=2 * seeds * width * 3 * rows,
    )
    plane_send, pair_bias = call(
        pair_sum_kernel, "sum_pair",
        [((PLANE, width // PLANE + 2 * depth, width), BF16), ((1, width), F32)],
        [], [keep, pair_arrived], after=[own],
    )
    plane_arrived = swap(plane_send, ("y", "x"))
    (depth_send,) = call(
        plane_sum_kernel, "sum_plane",
        [((depth, 2 * Y_SIZE, width), BF16)],
        [], [plane_arrived, pair_bias],
    )
    depth_arrived = swap(depth_send, "z")
    weight_send, plane_bias = call(
        functools.partial(weight_kernel, scale), "sum_weights",
        [((depth, 2 * Y_SIZE, LANES), BF16), ((1, width), F32)],
        [], [depth_arrived],
    )
    weight_depth = swap(weight_send, "z")
    share = rows // reps
    row_keep, *row_sends = call(
        scatter_kernel, "return_rows",
        [((CORES * share, width), F32)] + [((CORES * share, width), BF16)] * (X_SIZE - 1),
        [rep], [lists, depth_arrived, own],
        scratch=[pltpu.VMEM((rows, width), F32)],
        flops=4 * parts * rows * width, after=[weight_send],
    )
    row_arrived = [
        lax.ppermute(row_sends[step - 1], "x", [(x, x ^ step) for x in range(X_SIZE)])
        for step in (2, 1, 3)
    ]
    (weight_rows,) = call(
        gather_kernel, "gather_weights", [((width // PLANE, width), BF16)],
        [], [weight_depth], flops=window, after=[row_keep],
    )
    row_own, row_send = call(
        row_sum_kernel, "sum_rows", [((share, width), F32), ((share, width), BF16)],
        [], [row_keep, *row_arrived], flops=window,
    )
    (weight_plane,) = call(
        spread_kernel, "spread_weights", [((PLANE, width // PLANE + 8, width), BF16)],
        [], [weight_rows, plane_bias],
    )
    weight_near = swap(weight_plane, ("y", "x"))
    last_send, grad_bias = call(
        join_kernel, "join", [((width + share, width), BF16), ((1, width), F32)],
        [], [weight_near, row_send],
    )
    grad_self, grad_neigh, input_grad = call(
        finish_kernel, "finish",
        [((width, width), BF16), ((width, width), BF16), ((share, width), F32)],
        [core], [last_send, row_own, pair(last_send)],
    )
    grad_bias = grad_bias.reshape(width)
    return (out, input_grad, grad_self, grad_neigh, grad_bias)


def solution(mesh):
    parts = mesh.shape["dom"]
    physical = Mesh(
        mesh.devices.reshape(parts // Y_SIZE, Y_SIZE, X_SIZE, CORES), ("z", "y", "x", "core")
    )
    dom = ("z", "y")
    every = ("z", "y", "x", "core")
    placed = (
        P(dom, None),
        P(dom, None, None),
        P(every),
        P(every, None, None),
        P(every, None),
        P(every, None),
        P(every),
        P(),
        P(),
        P(),
        P(every, None),
    )
    return jax.shard_map(
        body,
        mesh=physical,
        in_specs=placed,
        out_specs=(P(every, None), P(every, None), P(), P(), P()),
        check_vma=False,
    )
```

```python
import functools
import math

import jax
import jax.numpy as jnp
from jax import lax
from jax.experimental import pallas as pl
from jax.experimental.pallas import tpu as pltpu
from jax.sharding import Mesh
from jax.sharding import PartitionSpec as P

BLK = 128
LANES = 128
SLOTS = 8
X_SIZE = 4
CORES = 2
Y_SIZE = 4
PLANE = Y_SIZE * X_SIZE
BF16 = jnp.bfloat16
F32 = jnp.float32
VMEM_BYTES = 24 * 1024 * 1024


def dot(a, b, contract_a=1, contract_b=0):
    return lax.dot_general(
        a, b, (((contract_a,), (contract_b,)), ((), ())), preferred_element_type=F32
    )


def move(matrix, rows):
    return dot(matrix.astype(BF16), rows).astype(BF16)


def iota(shape, dim):
    return lax.broadcasted_iota(jnp.int32, shape, dim)


def two_rows(wide, rows):
    high = wide.astype(BF16).astype(F32)
    row = iota((rows, wide.shape[1]), 0)
    return jnp.where(row == 0, high, jnp.where(row == 1, wide - high, 0.0)).astype(BF16)


def call(kernel, name, outs, scalars, arrays, scratch=(), flops=0, after=(), hbm=(), hbm_outs=()):
    if after:
        inner, at = kernel, len(scalars) + len(arrays) + len(hbm)
        kernel = lambda *refs: inner(*refs[:at], *refs[at + len(after) :])
    shapes = tuple(jax.ShapeDtypeStruct(shape, dtype) for shape, dtype in outs)
    shapes += tuple(pltpu.HBM(shape, dtype) for shape, dtype in hbm_outs)
    size = sum(math.prod(a.shape) * a.dtype.itemsize for a in (*arrays, *hbm, *shapes))
    return pl.pallas_call(
        kernel,
        out_shape=shapes,
        in_specs=[pl.BlockSpec(memory_space=pltpu.SMEM)] * len(scalars)
        + [pl.BlockSpec(memory_space=pltpu.VMEM)] * len(arrays)
        + [pl.BlockSpec(memory_space=pltpu.HBM)] * len(hbm)
        + [pl.BlockSpec(memory_space=pl.ANY)] * len(after),
        out_specs=tuple([pl.BlockSpec(memory_space=pltpu.VMEM)] * len(outs))
        + tuple([pl.BlockSpec(memory_space=pltpu.HBM)] * len(hbm_outs)),
        scratch_shapes=list(scratch),
        compiler_params=pltpu.CompilerParams(vmem_limit_bytes=VMEM_BYTES),
        cost_estimate=pl.CostEstimate(flops=flops, bytes_accessed=size, transcendentals=0),
        name=name,
    )(*scalars, *arrays, *(pltpu.with_memory_space_constraint(a, pltpu.HBM) for a in hbm), *after)


def fetched(arrays):
    return [pltpu.VMEM(a.shape, a.dtype) for a in arrays] + [
        pltpu.SemaphoreType.DMA((len(arrays),))
    ]


def fetch(from_refs, to_refs, sems):
    copies = [
        pltpu.make_async_copy(source, to, sems.at[at])
        for at, (source, to) in enumerate(zip(from_refs, to_refs))
    ]
    for copy in copies:
        copy.start()
    return copies


def place_tiles(dst_ref, src_ref, count_ref, tiles_ref, adj_ref, first, last):
    adj_ref[...] = jnp.zeros_like(adj_ref)

    def step(slot, carry):
        block = src_ref[0, slot]

        @pl.when(jnp.logical_and(block >= first, block < last))
        def _():
            row = pl.multiple_of(dst_ref[0, slot] * BLK, BLK)
            col = pl.multiple_of((block - first) * BLK, BLK)
            adj_ref[pl.ds(row, BLK), pl.ds(col, BLK)] = tiles_ref[slot]

        return carry

    lax.fori_loop(0, count_ref[0], step, 0)


def boundary_places(rep, lists_ref, rows, order):
    slots, parts = lists_ref.shape
    lists = lists_ref[...].astype(F32)
    wanted = jnp.sum(
        jnp.where(iota((slots, parts), 0) == rep, lists, 0.0), axis=0, keepdims=True
    ).astype(jnp.int32)
    place = iota((rows, parts), 0)
    places = jnp.concatenate([(place == wanted).astype(BF16), (place == rep).astype(BF16)], 1)
    return dot(places, order.astype(BF16), 1, 1).astype(BF16)


def summed_by_z(parts):
    shape = (2 * parts, 2 * parts)
    out, into = iota(shape, 0), iota(shape, 1)
    line, z = out % (2 * Y_SIZE), out // (2 * Y_SIZE)
    halo = jnp.logical_and(line < Y_SIZE, into == z * Y_SIZE + line)
    hub = jnp.logical_and(line == Y_SIZE, into == parts)
    return jnp.logical_or(halo, hub)


def send_kernel(rep_ref, lists_hbm, feats_hbm, send_ref, lists_ref, feats_ref, sems):
    lists_copy, feats_copy = fetch((lists_hbm, feats_hbm), (lists_ref, feats_ref), sems)
    slots, parts = lists_ref.shape
    depth = parts // Y_SIZE
    rep = rep_ref[0]
    shape = (2 * parts, parts)
    out, into = iota(shape, 0), iota(shape, 1)
    row, z = out % (2 * Y_SIZE), out // (2 * Y_SIZE)
    of_part = (into == z * Y_SIZE + row % Y_SIZE).astype(BF16)
    lists_copy.wait()
    lists = lists_ref[...]
    high, low = (lists // 256).astype(BF16), (lists % 256).astype(BF16)
    wanted = dot(of_part, high, 1, 1) * 256.0 + dot(of_part, low, 1, 1)
    shape = (2 * parts, slots)
    row = iota(shape, 0) % (2 * Y_SIZE)
    wanted = jnp.where(row < Y_SIZE, wanted, rep.astype(F32))
    wanted = jnp.sum(jnp.where(iota(shape, 1) == rep, wanted, 0.0), axis=1, keepdims=True)
    places = iota((2 * parts, feats_ref.shape[0]), 1) == wanted.astype(jnp.int32)
    places = places.astype(BF16)
    feats_copy.wait()
    rows = dot(places, feats_ref[...]).astype(BF16)
    lines = send_ref.shape[0] // depth
    shape = (depth * lines, 2 * parts)
    out, into = iota(shape, 0), iota(shape, 1)
    line, z = out % lines, out // lines
    packed = jnp.zeros(send_ref.shape, F32)
    for group in range(rows.shape[1] // LANES):
        first = group * (Y_SIZE + 1)
        wanted = jnp.where(
            jnp.logical_and(line >= first, line <= first + Y_SIZE),
            z * (2 * Y_SIZE) + line - first,
            -1,
        )
        lanes = slice(group * LANES, (group + 1) * LANES)
        packed += dot((into == wanted).astype(BF16), rows[:, lanes])
    send_ref[...] = packed.astype(BF16)


def plane_kernel(arrived_ref, send_ref):
    _, chunk, width = send_ref.shape
    depth = chunk // 2
    total = arrived_ref.shape[0]
    lines = total // depth
    shape = (Y_SIZE * chunk, total)
    out, into = iota(shape, 0), iota(shape, 1)
    z, kind, y = out % depth, out // depth % 2, out // chunk
    first = z * lines + jnp.where(kind == 0, y, Y_SIZE)
    arrived = arrived_ref[...]
    for group in range(width // LANES):
        moved = move(into == first + group * (Y_SIZE + 1), arrived)
        lanes = slice(group * LANES, (group + 1) * LANES)
        for y_to in range(Y_SIZE):
            for x_to in range(X_SIZE):
                send_ref[y_to * X_SIZE + x_to, :, lanes] = moved[y_to * chunk : (y_to + 1) * chunk]


def own_kernel(
    core_ref, count_ref, dst_hbm, src_hbm, tiles_hbm, feats_hbm, seeds_hbm, w_self_hbm,
    sums_ref, mats_hbm, dst_ref, src_ref, tiles_ref, feats_ref, seeds_ref, w_self_ref,
    sems, own_adj_ref, adj_ref, mats_ref, out_sem,
):
    *tile_copies, feats_copy, seeds_copy, w_self_copy = fetch(
        (dst_hbm, src_hbm, tiles_hbm, feats_hbm, seeds_hbm, w_self_hbm),
        (dst_ref, src_ref, tiles_ref, feats_ref, seeds_ref, w_self_ref),
        sems,
    )
    rows = feats_ref.shape[0]
    seeds = seeds_ref.shape[1]
    for copy in tile_copies:
        copy.wait()
    own_blocks = rows // BLK
    table = adj_ref.shape[1]
    place_tiles(dst_ref, src_ref, count_ref, tiles_ref, own_adj_ref, 0, own_blocks)
    place_tiles(
        dst_ref, src_ref, count_ref, tiles_ref, adj_ref, own_blocks, own_blocks + table // BLK
    )
    seeds_copy.wait()
    feats_copy.wait()
    picks = (iota((rows, seeds), 0) == seeds_ref[...]).astype(BF16)
    feats = feats_ref[...]
    mats_ref[2 * seeds + adj_ref.shape[1] :, :seeds] = dot(feats, picks, 0, 0).astype(BF16)
    chosen = dot(picks, feats, 0, 0).astype(BF16)
    w_self_copy.wait()
    sums_ref[:seeds] = dot(chosen, w_self_ref[...])
    sums_ref[seeds:] = dot(own_adj_ref[...], feats)
    adj = adj_ref[...]
    half = table // 2
    depth = half // PLANE // 2
    shape = (half, table)
    line, source = iota(shape, 0), iota(shape, 1)
    z, kind = line % depth, line // depth % 2
    x, y = line // (2 * depth) % X_SIZE, line // (2 * depth * X_SIZE)
    start = kind * half + (z * Y_SIZE + y) * SLOTS + x * CORES
    for far, core in enumerate((core_ref[0], 1 - core_ref[0])):
        order = (source == start + core).astype(BF16)
        mats_ref[far * seeds : (far + 1) * seeds, :half] = dot(adj, order, 1, 1).astype(BF16)
        first = 2 * seeds + far * half
        mats_ref[first : first + half, :seeds] = dot(order, adj, 1, 1).astype(BF16)
    back = pltpu.make_async_copy(mats_ref, mats_hbm, out_sem)
    back.start()
    back.wait()


def middle_kernel(
    core_ref, near_ref, far_ref, mats_ref, sums_ref, w_neigh_ref, cot_ref, bias_in_ref,
    out_ref, d_pre_ref, d_agg_ref, keep_ref, send_ref,
):
    width = w_neigh_ref.shape[0]
    half = near_ref.shape[0]
    seeds = cot_ref.shape[0]
    near_back, far_back, chosen_t = (2 * seeds + step * half for step in range(3))
    aggregate = (
        sums_ref[seeds:]
        + dot(mats_ref[:seeds, :half], near_ref[...])
        + dot(mats_ref[seeds : 2 * seeds, :half], far_ref[...])
    ).astype(BF16)
    preact = sums_ref[:seeds] + dot(aggregate, w_neigh_ref[...]) + bias_in_ref[...].astype(F32)
    gate = jax.nn.sigmoid(preact)
    out_ref[...] = (preact * gate).astype(BF16)
    d_pre = (cot_ref[...].astype(F32) * gate * (1.0 + preact * (1.0 - gate))).astype(BF16)
    d_pre_ref[...] = d_pre
    d_agg = dot(d_pre, w_neigh_ref[...], 1, 1).astype(BF16)
    d_agg_ref[...] = d_agg
    first = dot(mats_ref[chosen_t:, :seeds], d_pre).astype(BF16)
    second = dot(aggregate, d_pre, 0, 0).astype(BF16)
    is_first = core_ref[0] == 0
    keep_ref[:width] = jnp.where(is_first, first, second)
    send_ref[:width] = jnp.where(is_first, second, first)
    keep_ref[width : width + half] = dot(mats_ref[near_back:far_back, :seeds], d_agg).astype(BF16)
    send_ref[width : width + half] = dot(mats_ref[far_back:chosen_t, :seeds], d_agg).astype(BF16)
    bias = two_rows(jnp.sum(d_pre.astype(F32), 0, keepdims=True), keep_ref.shape[0] - width - half)
    keep_ref[width + half :] = bias
    send_ref[width + half :] = bias


def pair_sum_kernel(keep_ref, other_ref, send_ref, bias_ref):
    chunks, lines, width = send_ref.shape
    total = keep_ref[...].astype(F32) + other_ref[...].astype(F32)
    weight = width // chunks
    table = lines - weight
    bias_ref[...] = jnp.sum(total[width + chunks * table :], 0, keepdims=True)
    total = total.astype(BF16)
    for chunk in range(chunks):
        send_ref[chunk, :weight] = total[chunk * weight : (chunk + 1) * weight]
        send_ref[chunk, weight:] = total[width + chunk * table : width + (chunk + 1) * table]


def plane_sum_kernel(arrived_ref, bias_ref, send_ref):
    chunks, lines, width = arrived_ref.shape
    depth, block, _ = send_ref.shape
    weight = width // chunks
    each = weight // depth
    tail = weight + 2 * depth
    rows = []
    rest = None
    for y in range(Y_SIZE):
        some = arrived_ref[y * X_SIZE].astype(F32)
        for x in range(1, X_SIZE):
            some = some + arrived_ref[y * X_SIZE + x].astype(F32)
        rows.append(some[weight : weight + depth])
        rest = some if rest is None else rest + some
    bias = jnp.zeros((depth, width), F32) + bias_ref[...]
    rows += [rest[weight + depth : tail], rest[:weight], bias]
    rows = jnp.concatenate(rows, 0).astype(BF16)
    shape = (depth * block, rows.shape[0])
    out, into = iota(shape, 0), iota(shape, 1)
    line, z = out % block, out // block
    first = (Y_SIZE + 1) * depth
    of_weight = jnp.logical_and(line > Y_SIZE, line <= Y_SIZE + each)
    wanted = jnp.where(
        of_weight,
        first + z * each + line - Y_SIZE - 1,
        jnp.where(line <= Y_SIZE, line * depth, first + weight) + z,
    )
    send_ref[...] = move(into == wanted, rows).reshape(depth, block, width)


def weight_kernel(scale, arrived_ref, send_ref, bias_ref):
    depth, block, width = arrived_ref.shape
    total = jnp.sum(arrived_ref[...].astype(F32), 0) * scale
    each = block - Y_SIZE - 2
    row = iota((block, LANES), 0)
    done = jnp.zeros((block, LANES), F32)
    for group in range(width // LANES):
        for line in range(each):
            some = total[Y_SIZE + 1 + line : Y_SIZE + 2 + line, group * LANES : (group + 1) * LANES]
            done = jnp.where(row == group * each + line, some, done)
    done = done.astype(BF16)
    for z in range(depth):
        send_ref[z] = done
    bias_ref[...] = total[block - 1 :]


def gather_kernel(arrived_ref, whole_ref):
    weight, width = whole_ref.shape
    depth, block, _ = arrived_ref.shape
    groups = width // LANES
    each = weight // depth
    arrived = arrived_ref[...].reshape(depth * block, LANES)
    shape = (weight, depth * block)
    out, into = iota(shape, 0), iota(shape, 1)
    z, line = out // each, out % each
    for group in range(groups):
        rows = move(into == z * block + group * each + line, arrived)
        whole_ref[:, group * LANES : (group + 1) * LANES] = rows


def spread_kernel(whole_ref, bias_ref, send_ref):
    chunks, lines, _ = send_ref.shape
    bias = two_rows(bias_ref[...], lines - whole_ref.shape[0]).astype(F32)
    message = jnp.concatenate([whole_ref[...].astype(F32), bias], 0).astype(BF16)
    for chunk in range(chunks):
        send_ref[chunk] = message


def own_back_kernel(
    dst_ref, src_ref, count_ref, tiles_ref, seeds_ref, d_pre_ref, d_agg_ref, w_self_ref,
    own_ref, adj_ref,
):
    rows = own_ref.shape[0]
    seeds = seeds_ref.shape[1]
    place_tiles(dst_ref, src_ref, count_ref, tiles_ref, adj_ref, 0, rows // BLK)
    picks = (iota((rows, seeds), 0) == seeds_ref[...]).astype(BF16)
    seeded = dot(picks, d_pre_ref[...]).astype(BF16)
    own_ref[...] = dot(seeded, w_self_ref[...], 1, 1) + dot(adj_ref[...], d_agg_ref[...], 0, 0)


def scatter_kernel(rep_ref, lists_ref, arrived_ref, own_ref, keep_ref, *send_refs_and_total):
    *send_refs, total_ref = send_refs_and_total
    rows, width = own_ref.shape
    rep = rep_ref[0]
    places = boundary_places(rep, lists_ref, rows, summed_by_z(lists_ref.shape[1]))
    back = arrived_ref[...].reshape(places.shape[1], width)
    total_ref[...] = own_ref[...] + dot(places, back)
    share = rows // (X_SIZE * CORES)
    for step, ref in enumerate([keep_ref, *send_refs]):
        for core in range(CORES):
            place = jnp.bitwise_xor(rep, step * CORES + core)
            some = total_ref[pl.ds(pl.multiple_of(place * share, 32), share), :]
            ref[core * share : (core + 1) * share] = some.astype(ref.dtype)


def row_sum_kernel(keep_ref, *refs):
    *arrived_refs, own_ref, send_ref = refs
    share = own_ref.shape[0]
    total = keep_ref[...]
    for ref in arrived_refs:
        total = total + ref[...].astype(F32)
    own_ref[...] = total[:share]
    send_ref[...] = total[share:].astype(BF16)


def join_kernel(arrived_ref, rows_ref, send_ref, bias_ref):
    chunks, _, width = arrived_ref.shape
    weight = width // chunks
    bias = jnp.zeros(bias_ref.shape, F32)
    for chunk in range(chunks):
        arrived = arrived_ref[chunk].astype(F32)
        send_ref[chunk * weight : (chunk + 1) * weight] = arrived[:weight].astype(BF16)
        bias = bias + jnp.sum(arrived[weight:], 0, keepdims=True)
    send_ref[width:] = rows_ref[...]
    bias_ref[...] = bias


def finish_kernel(core_ref, near_ref, own_ref, far_ref, first_ref, second_ref, rows_ref):
    width = first_ref.shape[0]
    near, far = near_ref[:width], far_ref[:width]
    is_first = core_ref[0] == 0
    first_ref[...] = jnp.where(is_first, near, far)
    second_ref[...] = jnp.where(is_first, far, near)
    rows_ref[...] = own_ref[...] + far_ref[width:].astype(F32)


def body(
    feats,
    halo_index,
    seed_ids,
    tiles,
    tile_dst,
    tile_src,
    tile_count,
    w_self,
    w_neigh,
    bias,
    cotangent,
):
    depth = lax.axis_size("z")
    parts = depth * Y_SIZE
    reps = X_SIZE * CORES
    rows, width = feats.shape
    seeds = cotangent.shape[0]
    half = parts * SLOTS
    core_id = lax.axis_index("core").astype(jnp.int32)
    x_id = lax.axis_index("x").astype(jnp.int32)
    core = core_id.reshape(1)
    rep = (x_id * CORES + core_id).reshape(1)
    lists = halo_index[0].T
    seed_row = seed_ids.reshape(1, seeds)
    tile_scalars = (tile_dst, tile_src, tile_count)
    scale = float(seeds * parts * reps) ** (-0.5)

    window = 20_000_000_000

    def swap(values, axis):
        return lax.all_to_all(values, axis, split_axis=0, concat_axis=0, tiled=True)

    def pair(values):
        return lax.ppermute(values, "core", [(0, 1), (1, 0)])

    lines = -(-(Y_SIZE + 1) * (width // LANES) // 8) * 8
    (send,) = call(
        send_kernel, "pick_boundary", [((depth * lines, LANES), BF16)], [rep], [],
        hbm=[lists, feats], scratch=fetched([lists, feats]), flops=4 * parts * rows * width,
    )
    by_depth = swap(send.reshape(depth, lines, LANES), "z").reshape(depth * lines, LANES)
    mats_shape = (2 * (seeds + half) + width, max(seeds, half))
    own_args = [tile_dst, tile_src, tiles, feats, seed_row, w_self]
    sums, mats = call(
        own_kernel, "own_rows", [((2 * seeds, width), F32)], [core, tile_count], [],
        hbm=own_args,
        hbm_outs=[(mats_shape, BF16)],
        scratch=[pltpu.SMEM(a.shape, a.dtype) for a in (tile_dst, tile_src)]
        + fetched(own_args)[2:]
        + [
            pltpu.VMEM((seeds, rows), BF16),
            pltpu.VMEM((seeds, 2 * half), BF16),
            pltpu.VMEM(mats_shape, BF16),
            pltpu.SemaphoreType.DMA,
        ],
        flops=2 * seeds * (3 * rows * width + width * width + 8 * half * half),
    )
    (plane,) = call(
        plane_kernel, "spread_plane", [((PLANE, 2 * depth, width), BF16)], [], [by_depth],
        flops=8 * parts * parts * width, after=[sums],
    )
    near = swap(plane, ("y", "x")).reshape(half, width)
    far = pair(near)

    out, d_pre, d_agg, keep, pair_send = call(
        middle_kernel, "forward_backward",
        [
            ((seeds, width), BF16),
            ((seeds, width), BF16),
            ((seeds, width), BF16),
            ((width + half + 16, width), BF16),
            ((width + half + 16, width), BF16),
        ],
        [core],
        [
            near, far, mats, sums, w_neigh, cotangent, bias.reshape(1, width),
        ],
        flops=2 * seeds * width * (4 * half + 4 * width),
    )

    pair_arrived = pair(pair_send)
    (own,) = call(
        own_back_kernel, "own_rows_back", [((rows, width), F32)],
        [*tile_scalars], [tiles, seed_row, d_pre, d_agg, w_self],
        scratch=[pltpu.VMEM((seeds, rows), BF16)],
        flops=2 * seeds * width * 3 * rows,
    )
    plane_send, pair_bias = call(
        pair_sum_kernel, "sum_pair",
        [((PLANE, width // PLANE + 2 * depth, width), BF16), ((1, width), F32)],
        [], [keep, pair_arrived], after=[own],
    )
    plane_arrived = swap(plane_send, ("y", "x"))
    (depth_send,) = call(
        plane_sum_kernel, "sum_plane",
        [((depth, 2 * Y_SIZE, width), BF16)],
        [], [plane_arrived, pair_bias],
    )
    depth_arrived = swap(depth_send, "z")
    weight_send, plane_bias = call(
        functools.partial(weight_kernel, scale), "sum_weights",
        [((depth, 2 * Y_SIZE, LANES), BF16), ((1, width), F32)],
        [], [depth_arrived],
    )
    weight_depth = swap(weight_send, "z")
    share = rows // reps
    row_keep, *row_sends = call(
        scatter_kernel, "return_rows",
        [((CORES * share, width), F32)] + [((CORES * share, width), BF16)] * (X_SIZE - 1),
        [rep], [lists, depth_arrived, own],
        scratch=[pltpu.VMEM((rows, width), F32)],
        flops=4 * parts * rows * width, after=[weight_send],
    )
    row_arrived = [
        lax.ppermute(row_sends[step - 1], "x", [(x, x ^ step) for x in range(X_SIZE)])
        for step in (2, 1, 3)
    ]
    (weight_rows,) = call(
        gather_kernel, "gather_weights", [((width // PLANE, width), BF16)],
        [], [weight_depth], flops=window, after=[row_keep],
    )
    row_own, row_send = call(
        row_sum_kernel, "sum_rows", [((share, width), F32), ((share, width), BF16)],
        [], [row_keep, *row_arrived], flops=window,
    )
    (weight_plane,) = call(
        spread_kernel, "spread_weights", [((PLANE, width // PLANE + 8, width), BF16)],
        [], [weight_rows, plane_bias],
    )
    weight_near = swap(weight_plane, ("y", "x"))
    last_send, grad_bias = call(
        join_kernel, "join", [((width + share, width), BF16), ((1, width), F32)],
        [], [weight_near, row_send],
    )
    grad_self, grad_neigh, input_grad = call(
        finish_kernel, "finish",
        [((width, width), BF16), ((width, width), BF16), ((share, width), F32)],
        [core], [last_send, row_own, pair(last_send)],
    )
    grad_bias = grad_bias.reshape(width)
    return (out, input_grad, grad_self, grad_neigh, grad_bias)


def solution(mesh):
    parts = mesh.shape["dom"]
    physical = Mesh(
        mesh.devices.reshape(parts // Y_SIZE, Y_SIZE, X_SIZE, CORES), ("z", "y", "x", "core")
    )
    dom = ("z", "y")
    every = ("z", "y", "x", "core")
    placed = (
        P(dom, None),
        P(dom, None, None),
        P(every),
        P(every, None, None),
        P(every, None),
        P(every, None),
        P(every),
        P(),
        P(),
        P(),
        P(every, None),
    )
    return jax.shard_map(
        body,
        mesh=physical,
        in_specs=placed,
        out_specs=(P(every, None), P(every, None), P(), P(), P()),
        check_vma=False,
    )
```

```python
import functools
import math

import jax
import jax.numpy as jnp
from jax import lax
from jax.experimental import pallas as pl
from jax.experimental.pallas import tpu as pltpu
from jax.sharding import Mesh
from jax.sharding import PartitionSpec as P

BLK = 128
LANES = 128
SLOTS = 8
X_SIZE = 4
CORES = 2
Y_SIZE = 4
PLANE = Y_SIZE * X_SIZE
BF16 = jnp.bfloat16
F32 = jnp.float32
VMEM_BYTES = 24 * 1024 * 1024


def dot(a, b, contract_a=1, contract_b=0):
    return lax.dot_general(
        a, b, (((contract_a,), (contract_b,)), ((), ())), preferred_element_type=F32
    )


def move(matrix, rows):
    return dot(matrix.astype(BF16), rows).astype(BF16)


def iota(shape, dim):
    return lax.broadcasted_iota(jnp.int32, shape, dim)


def two_rows(wide, rows):
    high = wide.astype(BF16).astype(F32)
    row = iota((rows, wide.shape[1]), 0)
    return jnp.where(row == 0, high, jnp.where(row == 1, wide - high, 0.0)).astype(BF16)


def call(kernel, name, outs, scalars, arrays, scratch=(), flops=0, after=(), hbm=(), hbm_outs=()):
    if after:
        inner, at = kernel, len(scalars) + len(arrays) + len(hbm)
        kernel = lambda *refs: inner(*refs[:at], *refs[at + len(after) :])
    shapes = tuple(jax.ShapeDtypeStruct(shape, dtype) for shape, dtype in outs)
    shapes += tuple(pltpu.HBM(shape, dtype) for shape, dtype in hbm_outs)
    size = sum(math.prod(a.shape) * a.dtype.itemsize for a in (*arrays, *hbm, *shapes))
    return pl.pallas_call(
        kernel,
        out_shape=shapes,
        in_specs=[pl.BlockSpec(memory_space=pltpu.SMEM)] * len(scalars)
        + [pl.BlockSpec(memory_space=pltpu.VMEM)] * len(arrays)
        + [pl.BlockSpec(memory_space=pltpu.HBM)] * len(hbm)
        + [pl.BlockSpec(memory_space=pl.ANY)] * len(after),
        out_specs=tuple([pl.BlockSpec(memory_space=pltpu.VMEM)] * len(outs))
        + tuple([pl.BlockSpec(memory_space=pltpu.HBM)] * len(hbm_outs)),
        scratch_shapes=list(scratch),
        compiler_params=pltpu.CompilerParams(vmem_limit_bytes=VMEM_BYTES),
        cost_estimate=pl.CostEstimate(flops=flops, bytes_accessed=size, transcendentals=0),
        name=name,
    )(*scalars, *arrays, *(pltpu.with_memory_space_constraint(a, pltpu.HBM) for a in hbm), *after)


def fetched(arrays):
    return [pltpu.VMEM(a.shape, a.dtype) for a in arrays] + [
        pltpu.SemaphoreType.DMA((len(arrays),))
    ]


def fetch(from_refs, to_refs, sems):
    copies = [
        pltpu.make_async_copy(source, to, sems.at[at])
        for at, (source, to) in enumerate(zip(from_refs, to_refs))
    ]
    for copy in copies:
        copy.start()
    return copies


def place_tiles(dst_ref, src_ref, count_ref, tiles_ref, adj_ref, first, last):
    adj_ref[...] = jnp.zeros_like(adj_ref)

    def step(slot, carry):
        block = src_ref[0, slot]

        @pl.when(jnp.logical_and(block >= first, block < last))
        def _():
            row = pl.multiple_of(dst_ref[0, slot] * BLK, BLK)
            col = pl.multiple_of((block - first) * BLK, BLK)
            adj_ref[pl.ds(row, BLK), pl.ds(col, BLK)] = tiles_ref[slot]

        return carry

    lax.fori_loop(0, count_ref[0], step, 0)


def boundary_places(rep, lists_ref, rows, order):
    slots, parts = lists_ref.shape
    lists = lists_ref[...].astype(F32)
    wanted = jnp.sum(
        jnp.where(iota((slots, parts), 0) == rep, lists, 0.0), axis=0, keepdims=True
    ).astype(jnp.int32)
    place = iota((rows, parts), 0)
    places = jnp.concatenate([(place == wanted).astype(BF16), (place == rep).astype(BF16)], 1)
    return dot(places, order.astype(BF16), 1, 1).astype(BF16)


def summed_by_z(parts):
    shape = (2 * parts, 2 * parts)
    out, into = iota(shape, 0), iota(shape, 1)
    line, z = out % (2 * Y_SIZE), out // (2 * Y_SIZE)
    halo = jnp.logical_and(line < Y_SIZE, into == z * Y_SIZE + line)
    hub = jnp.logical_and(line == Y_SIZE, into == parts)
    return jnp.logical_or(halo, hub)


def send_kernel(rep_ref, lists_hbm, feats_hbm, send_ref, lists_ref, feats_ref, sems):
    lists_copy = pltpu.make_async_copy(lists_hbm, lists_ref, sems.at[0])
    lists_copy.start()
    count = sems.shape[0] - 1
    piece = feats_ref.shape[0] // count
    feats_copies = []
    for at in range(count):
        rows = pl.ds(at * piece, piece)
        copy = pltpu.make_async_copy(feats_hbm.at[rows], feats_ref.at[rows], sems.at[1 + at])
        copy.start()
        feats_copies.append(copy)
    slots, parts = lists_ref.shape
    depth = parts // Y_SIZE
    rep = rep_ref[0]
    shape = (2 * parts, parts)
    out, into = iota(shape, 0), iota(shape, 1)
    row, z = out % (2 * Y_SIZE), out // (2 * Y_SIZE)
    of_part = (into == z * Y_SIZE + row % Y_SIZE).astype(BF16)
    lists_copy.wait()
    lists = lists_ref[...]
    high, low = (lists // 256).astype(BF16), (lists % 256).astype(BF16)
    wanted = dot(of_part, high, 1, 1) * 256.0 + dot(of_part, low, 1, 1)
    shape = (2 * parts, slots)
    row = iota(shape, 0) % (2 * Y_SIZE)
    wanted = jnp.where(row < Y_SIZE, wanted, rep.astype(F32))
    wanted = jnp.sum(jnp.where(iota(shape, 1) == rep, wanted, 0.0), axis=1, keepdims=True)
    places = iota((2 * parts, feats_ref.shape[0]), 1) == wanted.astype(jnp.int32)
    places = places.astype(BF16)
    for copy in feats_copies:
        copy.wait()
    rows = dot(places, feats_ref[...]).astype(BF16)
    lines = send_ref.shape[0] // depth
    shape = (depth * lines, 2 * parts)
    out, into = iota(shape, 0), iota(shape, 1)
    line, z = out % lines, out // lines
    packed = jnp.zeros(send_ref.shape, F32)
    for group in range(rows.shape[1] // LANES):
        first = group * (Y_SIZE + 1)
        wanted = jnp.where(
            jnp.logical_and(line >= first, line <= first + Y_SIZE),
            z * (2 * Y_SIZE) + line - first,
            -1,
        )
        lanes = slice(group * LANES, (group + 1) * LANES)
        packed += dot((into == wanted).astype(BF16), rows[:, lanes])
    send_ref[...] = packed.astype(BF16)


def plane_kernel(arrived_ref, send_ref):
    _, chunk, width = send_ref.shape
    depth = chunk // 2
    total = arrived_ref.shape[0]
    lines = total // depth
    shape = (Y_SIZE * chunk, total)
    out, into = iota(shape, 0), iota(shape, 1)
    z, kind, y = out % depth, out // depth % 2, out // chunk
    first = z * lines + jnp.where(kind == 0, y, Y_SIZE)
    arrived = arrived_ref[...]
    for group in range(width // LANES):
        moved = move(into == first + group * (Y_SIZE + 1), arrived)
        lanes = slice(group * LANES, (group + 1) * LANES)
        for y_to in range(Y_SIZE):
            for x_to in range(X_SIZE):
                send_ref[y_to * X_SIZE + x_to, :, lanes] = moved[y_to * chunk : (y_to + 1) * chunk]


def own_kernel(
    core_ref, count_ref, dst_hbm, src_hbm, tiles_hbm, feats_hbm, seeds_hbm, w_self_hbm,
    sums_ref, mats_hbm, dst_ref, src_ref, tiles_ref, feats_ref, seeds_ref, w_self_ref,
    sems, own_adj_ref, adj_ref, mats_ref, out_sem,
):
    *tile_copies, feats_copy, seeds_copy, w_self_copy = fetch(
        (dst_hbm, src_hbm, tiles_hbm, feats_hbm, seeds_hbm, w_self_hbm),
        (dst_ref, src_ref, tiles_ref, feats_ref, seeds_ref, w_self_ref),
        sems,
    )
    rows = feats_ref.shape[0]
    seeds = seeds_ref.shape[1]
    for copy in tile_copies:
        copy.wait()
    own_blocks = rows // BLK
    table = adj_ref.shape[1]
    place_tiles(dst_ref, src_ref, count_ref, tiles_ref, own_adj_ref, 0, own_blocks)
    place_tiles(
        dst_ref, src_ref, count_ref, tiles_ref, adj_ref, own_blocks, own_blocks + table // BLK
    )
    seeds_copy.wait()
    feats_copy.wait()
    picks = (iota((rows, seeds), 0) == seeds_ref[...]).astype(BF16)
    feats = feats_ref[...]
    mats_ref[2 * seeds + adj_ref.shape[1] :, :seeds] = dot(feats, picks, 0, 0).astype(BF16)
    chosen = dot(picks, feats, 0, 0).astype(BF16)
    w_self_copy.wait()
    sums_ref[:seeds] = dot(chosen, w_self_ref[...])
    sums_ref[seeds:] = dot(own_adj_ref[...], feats)
    adj = adj_ref[...]
    half = table // 2
    depth = half // PLANE // 2
    shape = (half, table)
    line, source = iota(shape, 0), iota(shape, 1)
    z, kind = line % depth, line // depth % 2
    x, y = line // (2 * depth) % X_SIZE, line // (2 * depth * X_SIZE)
    start = kind * half + (z * Y_SIZE + y) * SLOTS + x * CORES
    for far, core in enumerate((core_ref[0], 1 - core_ref[0])):
        order = (source == start + core).astype(BF16)
        mats_ref[far * seeds : (far + 1) * seeds, :half] = dot(adj, order, 1, 1).astype(BF16)
        first = 2 * seeds + far * half
        mats_ref[first : first + half, :seeds] = dot(order, adj, 1, 1).astype(BF16)
    back = pltpu.make_async_copy(mats_ref, mats_hbm, out_sem)
    back.start()
    back.wait()


def middle_kernel(
    core_ref, near_ref, far_ref, mats_ref, sums_ref, w_neigh_ref, cot_ref, bias_in_ref,
    out_ref, d_pre_ref, d_agg_ref, keep_ref, send_ref,
):
    width = w_neigh_ref.shape[0]
    half = near_ref.shape[0]
    seeds = cot_ref.shape[0]
    near_back, far_back, chosen_t = (2 * seeds + step * half for step in range(3))
    aggregate = (
        sums_ref[seeds:]
        + dot(mats_ref[:seeds, :half], near_ref[...])
        + dot(mats_ref[seeds : 2 * seeds, :half], far_ref[...])
    ).astype(BF16)
    preact = sums_ref[:seeds] + dot(aggregate, w_neigh_ref[...]) + bias_in_ref[...].astype(F32)
    gate = jax.nn.sigmoid(preact)
    out_ref[...] = (preact * gate).astype(BF16)
    d_pre = (cot_ref[...].astype(F32) * gate * (1.0 + preact * (1.0 - gate))).astype(BF16)
    d_pre_ref[...] = d_pre
    d_agg = dot(d_pre, w_neigh_ref[...], 1, 1).astype(BF16)
    d_agg_ref[...] = d_agg
    first = dot(mats_ref[chosen_t:, :seeds], d_pre).astype(BF16)
    second = dot(aggregate, d_pre, 0, 0).astype(BF16)
    is_first = core_ref[0] == 0
    keep_ref[:width] = jnp.where(is_first, first, second)
    send_ref[:width] = jnp.where(is_first, second, first)
    keep_ref[width : width + half] = dot(mats_ref[near_back:far_back, :seeds], d_agg).astype(BF16)
    send_ref[width : width + half] = dot(mats_ref[far_back:chosen_t, :seeds], d_agg).astype(BF16)
    bias = two_rows(jnp.sum(d_pre.astype(F32), 0, keepdims=True), keep_ref.shape[0] - width - half)
    keep_ref[width + half :] = bias
    send_ref[width + half :] = bias


def pair_sum_kernel(keep_ref, other_ref, send_ref, bias_ref):
    chunks, lines, width = send_ref.shape
    total = keep_ref[...].astype(F32) + other_ref[...].astype(F32)
    weight = width // chunks
    table = lines - weight
    bias_ref[...] = jnp.sum(total[width + chunks * table :], 0, keepdims=True)
    total = total.astype(BF16)
    for chunk in range(chunks):
        send_ref[chunk, :weight] = total[chunk * weight : (chunk + 1) * weight]
        send_ref[chunk, weight:] = total[width + chunk * table : width + (chunk + 1) * table]


def plane_sum_kernel(arrived_ref, bias_ref, send_ref):
    chunks, lines, width = arrived_ref.shape
    depth, block, _ = send_ref.shape
    weight = width // chunks
    each = weight // depth
    tail = weight + 2 * depth
    rows = []
    rest = None
    for y in range(Y_SIZE):
        some = arrived_ref[y * X_SIZE].astype(F32)
        for x in range(1, X_SIZE):
            some = some + arrived_ref[y * X_SIZE + x].astype(F32)
        rows.append(some[weight : weight + depth])
        rest = some if rest is None else rest + some
    bias = jnp.zeros((depth, width), F32) + bias_ref[...]
    rows += [rest[weight + depth : tail], rest[:weight], bias]
    rows = jnp.concatenate(rows, 0).astype(BF16)
    shape = (depth * block, rows.shape[0])
    out, into = iota(shape, 0), iota(shape, 1)
    line, z = out % block, out // block
    first = (Y_SIZE + 1) * depth
    of_weight = jnp.logical_and(line > Y_SIZE, line <= Y_SIZE + each)
    wanted = jnp.where(
        of_weight,
        first + z * each + line - Y_SIZE - 1,
        jnp.where(line <= Y_SIZE, line * depth, first + weight) + z,
    )
    send_ref[...] = move(into == wanted, rows).reshape(depth, block, width)


def weight_kernel(scale, arrived_ref, send_ref, bias_ref):
    depth, block, width = arrived_ref.shape
    total = jnp.sum(arrived_ref[...].astype(F32), 0) * scale
    each = block - Y_SIZE - 2
    row = iota((block, LANES), 0)
    done = jnp.zeros((block, LANES), F32)
    for group in range(width // LANES):
        for line in range(each):
            some = total[Y_SIZE + 1 + line : Y_SIZE + 2 + line, group * LANES : (group + 1) * LANES]
            done = jnp.where(row == group * each + line, some, done)
    done = done.astype(BF16)
    for z in range(depth):
        send_ref[z] = done
    bias_ref[...] = total[block - 1 :]


def gather_kernel(arrived_ref, whole_ref):
    weight, width = whole_ref.shape
    depth, block, _ = arrived_ref.shape
    groups = width // LANES
    each = weight // depth
    arrived = arrived_ref[...].reshape(depth * block, LANES)
    shape = (weight, depth * block)
    out, into = iota(shape, 0), iota(shape, 1)
    z, line = out // each, out % each
    for group in range(groups):
        rows = move(into == z * block + group * each + line, arrived)
        whole_ref[:, group * LANES : (group + 1) * LANES] = rows


def spread_kernel(whole_ref, bias_ref, send_ref):
    chunks, lines, _ = send_ref.shape
    bias = two_rows(bias_ref[...], lines - whole_ref.shape[0]).astype(F32)
    message = jnp.concatenate([whole_ref[...].astype(F32), bias], 0).astype(BF16)
    for chunk in range(chunks):
        send_ref[chunk] = message


def own_back_kernel(
    dst_ref, src_ref, count_ref, tiles_ref, seeds_ref, d_pre_ref, d_agg_ref, w_self_ref,
    own_ref, adj_ref,
):
    rows = own_ref.shape[0]
    seeds = seeds_ref.shape[1]
    place_tiles(dst_ref, src_ref, count_ref, tiles_ref, adj_ref, 0, rows // BLK)
    picks = (iota((rows, seeds), 0) == seeds_ref[...]).astype(BF16)
    seeded = dot(picks, d_pre_ref[...]).astype(BF16)
    own_ref[...] = dot(seeded, w_self_ref[...], 1, 1) + dot(adj_ref[...], d_agg_ref[...], 0, 0)


def scatter_kernel(rep_ref, lists_ref, arrived_ref, own_ref, keep_ref, *send_refs_and_total):
    *send_refs, total_ref = send_refs_and_total
    rows, width = own_ref.shape
    rep = rep_ref[0]
    places = boundary_places(rep, lists_ref, rows, summed_by_z(lists_ref.shape[1]))
    back = arrived_ref[...].reshape(places.shape[1], width)
    total_ref[...] = own_ref[...] + dot(places, back)
    share = rows // (X_SIZE * CORES)
    for step, ref in enumerate([keep_ref, *send_refs]):
        for core in range(CORES):
            place = jnp.bitwise_xor(rep, step * CORES + core)
            some = total_ref[pl.ds(pl.multiple_of(place * share, 32), share), :]
            ref[core * share : (core + 1) * share] = some.astype(ref.dtype)


def row_sum_kernel(keep_ref, *refs):
    *arrived_refs, own_ref, send_ref = refs
    share = own_ref.shape[0]
    total = keep_ref[...]
    for ref in arrived_refs:
        total = total + ref[...].astype(F32)
    own_ref[...] = total[:share]
    send_ref[...] = total[share:].astype(BF16)


def join_kernel(arrived_ref, rows_ref, send_ref):
    chunks, _, width = arrived_ref.shape
    weight = width // chunks
    for chunk in range(chunks):
        send_ref[chunk * weight : (chunk + 1) * weight] = arrived_ref[chunk, :weight]
    send_ref[width:] = rows_ref[...]


def bias_kernel(arrived_ref, bias_ref):
    chunks, _, width = arrived_ref.shape
    weight = width // chunks
    bias = jnp.zeros(bias_ref.shape, F32)
    for chunk in range(chunks):
        arrived = arrived_ref[chunk].astype(F32)
        bias = bias + jnp.sum(arrived[weight:], 0, keepdims=True)
    bias_ref[...] = bias


def finish_kernel(core_ref, near_ref, own_ref, far_ref, rows_ref, first_hbm, second_hbm, sems):
    width = first_hbm.shape[0]
    weights = pl.ds(0, width)

    def copies(near_to, far_to):
        return (
            pltpu.make_async_copy(near_ref.at[weights], near_to, sems.at[0]),
            pltpu.make_async_copy(far_ref.at[weights], far_to, sems.at[1]),
        )

    @pl.when(core_ref[0] == 0)
    def _():
        for copy in copies(first_hbm, second_hbm):
            copy.start()

    @pl.when(core_ref[0] != 0)
    def _():
        for copy in copies(second_hbm, first_hbm):
            copy.start()

    rows_ref[...] = own_ref[...] + far_ref[width:].astype(F32)
    for copy in copies(first_hbm, second_hbm):
        copy.wait()


def body(
    feats,
    halo_index,
    seed_ids,
    tiles,
    tile_dst,
    tile_src,
    tile_count,
    w_self,
    w_neigh,
    bias,
    cotangent,
):
    depth = lax.axis_size("z")
    parts = depth * Y_SIZE
    reps = X_SIZE * CORES
    rows, width = feats.shape
    seeds = cotangent.shape[0]
    half = parts * SLOTS
    core_id = lax.axis_index("core").astype(jnp.int32)
    x_id = lax.axis_index("x").astype(jnp.int32)
    core = core_id.reshape(1)
    rep = (x_id * CORES + core_id).reshape(1)
    lists = halo_index[0].T
    seed_row = seed_ids.reshape(1, seeds)
    tile_scalars = (tile_dst, tile_src, tile_count)
    scale = float(seeds * parts * reps) ** (-0.5)

    window = 20_000_000_000

    def swap(values, axis):
        return lax.all_to_all(values, axis, split_axis=0, concat_axis=0, tiled=True)

    def pair(values):
        return lax.ppermute(values, "core", [(0, 1), (1, 0)])

    lines = -(-(Y_SIZE + 1) * (width // LANES) // 8) * 8
    (send,) = call(
        send_kernel, "pick_boundary", [((depth * lines, LANES), BF16)], [rep], [],
        hbm=[lists, feats], flops=4 * parts * rows * width,
        scratch=fetched([lists, feats])[:2] + [pltpu.SemaphoreType.DMA((1 + 4,))],
    )
    by_depth = swap(send.reshape(depth, lines, LANES), "z").reshape(depth * lines, LANES)
    mats_shape = (2 * (seeds + half) + width, max(seeds, half))
    own_args = [tile_dst, tile_src, tiles, feats, seed_row, w_self]
    sums, mats = call(
        own_kernel, "own_rows", [((2 * seeds, width), F32)], [core, tile_count], [],
        hbm=own_args,
        hbm_outs=[(mats_shape, BF16)],
        scratch=[pltpu.SMEM(a.shape, a.dtype) for a in (tile_dst, tile_src)]
        + fetched(own_args)[2:]
        + [
            pltpu.VMEM((seeds, rows), BF16),
            pltpu.VMEM((seeds, 2 * half), BF16),
            pltpu.VMEM(mats_shape, BF16),
            pltpu.SemaphoreType.DMA,
        ],
        flops=2 * seeds * (3 * rows * width + width * width + 8 * half * half),
    )
    (plane,) = call(
        plane_kernel, "spread_plane", [((PLANE, 2 * depth, width), BF16)], [], [by_depth],
        flops=8 * parts * parts * width, after=[sums],
    )
    near = swap(plane, ("y", "x")).reshape(half, width)
    far = pair(near)

    out, d_pre, d_agg, keep, pair_send = call(
        middle_kernel, "forward_backward",
        [
            ((seeds, width), BF16),
            ((seeds, width), BF16),
            ((seeds, width), BF16),
            ((width + half + 16, width), BF16),
            ((width + half + 16, width), BF16),
        ],
        [core],
        [
            near, far, mats, sums, w_neigh, cotangent, bias.reshape(1, width),
        ],
        flops=2 * seeds * width * (4 * half + 4 * width),
    )

    pair_arrived = pair(pair_send)
    (own,) = call(
        own_back_kernel, "own_rows_back", [((rows, width), F32)],
        [*tile_scalars], [tiles, seed_row, d_pre, d_agg, w_self],
        scratch=[pltpu.VMEM((seeds, rows), BF16)],
        flops=2 * seeds * width * 3 * rows,
    )
    plane_send, pair_bias = call(
        pair_sum_kernel, "sum_pair",
        [((PLANE, width // PLANE + 2 * depth, width), BF16), ((1, width), F32)],
        [], [keep, pair_arrived], after=[own],
    )
    plane_arrived = swap(plane_send, ("y", "x"))
    (depth_send,) = call(
        plane_sum_kernel, "sum_plane",
        [((depth, 2 * Y_SIZE, width), BF16)],
        [], [plane_arrived, pair_bias],
    )
    depth_arrived = swap(depth_send, "z")
    weight_send, plane_bias = call(
        functools.partial(weight_kernel, scale), "sum_weights",
        [((depth, 2 * Y_SIZE, LANES), BF16), ((1, width), F32)],
        [], [depth_arrived],
    )
    weight_depth = swap(weight_send, "z")
    share = rows // reps
    row_keep, *row_sends = call(
        scatter_kernel, "return_rows",
        [((CORES * share, width), F32)] + [((CORES * share, width), BF16)] * (X_SIZE - 1),
        [rep], [lists, depth_arrived, own],
        scratch=[pltpu.VMEM((rows, width), F32)],
        flops=4 * parts * rows * width, after=[weight_send],
    )
    row_arrived = [
        lax.ppermute(row_sends[step - 1], "x", [(x, x ^ step) for x in range(X_SIZE)])
        for step in (2, 1, 3)
    ]
    (weight_rows,) = call(
        gather_kernel, "gather_weights", [((width // PLANE, width), BF16)],
        [], [weight_depth], flops=window, after=[row_keep],
    )
    row_own, row_send = call(
        row_sum_kernel, "sum_rows", [((share, width), F32), ((share, width), BF16)],
        [], [row_keep, *row_arrived], flops=window,
    )
    (weight_plane,) = call(
        spread_kernel, "spread_weights", [((PLANE, width // PLANE + 8, width), BF16)],
        [], [weight_rows, plane_bias],
    )
    weight_near = swap(weight_plane, ("y", "x"))
    (last_send,) = call(
        join_kernel, "join", [((width + share, width), BF16)], [], [weight_near, row_send]
    )
    (grad_bias,) = call(
        bias_kernel, "sum_bias", [((1, width), F32)], [], [weight_near], after=[last_send]
    )
    input_grad, grad_self, grad_neigh = call(
        finish_kernel, "finish", [((share, width), F32)],
        [core], [last_send, row_own, pair(last_send)],
        hbm_outs=[((width, width), BF16), ((width, width), BF16)],
        scratch=[pltpu.SemaphoreType.DMA((2,))],
    )
    grad_bias = grad_bias.reshape(width)
    return (out, input_grad, grad_self, grad_neigh, grad_bias)


def solution(mesh):
    parts = mesh.shape["dom"]
    physical = Mesh(
        mesh.devices.reshape(parts // Y_SIZE, Y_SIZE, X_SIZE, CORES), ("z", "y", "x", "core")
    )
    dom = ("z", "y")
    every = ("z", "y", "x", "core")
    placed = (
        P(dom, None),
        P(dom, None, None),
        P(every),
        P(every, None, None),
        P(every, None),
        P(every, None),
        P(every),
        P(),
        P(),
        P(),
        P(every, None),
    )
    return jax.shard_map(
        body,
        mesh=physical,
        in_specs=placed,
        out_specs=(P(every, None), P(every, None), P(), P(), P()),
        check_vma=False,
    )
```

```python
import functools
import math

import jax
import jax.numpy as jnp
from jax import lax
from jax.experimental import pallas as pl
from jax.experimental.pallas import tpu as pltpu
from jax.sharding import Mesh
from jax.sharding import PartitionSpec as P

BLK = 128
LANES = 128
SLOTS = 8
X_SIZE = 4
CORES = 2
Y_SIZE = 4
PLANE = Y_SIZE * X_SIZE
BF16 = jnp.bfloat16
F32 = jnp.float32
VMEM_BYTES = 24 * 1024 * 1024


def dot(a, b, contract_a=1, contract_b=0):
    return lax.dot_general(
        a, b, (((contract_a,), (contract_b,)), ((), ())), preferred_element_type=F32
    )


def move(matrix, rows):
    return dot(matrix.astype(BF16), rows).astype(BF16)


def iota(shape, dim):
    return lax.broadcasted_iota(jnp.int32, shape, dim)


def two_rows(wide, rows):
    high = wide.astype(BF16).astype(F32)
    row = iota((rows, wide.shape[1]), 0)
    return jnp.where(row == 0, high, jnp.where(row == 1, wide - high, 0.0)).astype(BF16)


def call(kernel, name, outs, scalars, arrays, scratch=(), flops=0, after=(), hbm=(), hbm_outs=()):
    if after:
        inner, at = kernel, len(scalars) + len(arrays) + len(hbm)
        kernel = lambda *refs: inner(*refs[:at], *refs[at + len(after) :])
    shapes = tuple(jax.ShapeDtypeStruct(shape, dtype) for shape, dtype in outs)
    shapes += tuple(pltpu.HBM(shape, dtype) for shape, dtype in hbm_outs)
    size = sum(math.prod(a.shape) * a.dtype.itemsize for a in (*arrays, *hbm, *shapes))
    return pl.pallas_call(
        kernel,
        out_shape=shapes,
        in_specs=[pl.BlockSpec(memory_space=pltpu.SMEM)] * len(scalars)
        + [pl.BlockSpec(memory_space=pltpu.VMEM)] * len(arrays)
        + [pl.BlockSpec(memory_space=pltpu.HBM)] * len(hbm)
        + [pl.BlockSpec(memory_space=pl.ANY)] * len(after),
        out_specs=tuple([pl.BlockSpec(memory_space=pltpu.VMEM)] * len(outs))
        + tuple([pl.BlockSpec(memory_space=pltpu.HBM)] * len(hbm_outs)),
        scratch_shapes=list(scratch),
        compiler_params=pltpu.CompilerParams(vmem_limit_bytes=VMEM_BYTES),
        cost_estimate=pl.CostEstimate(flops=flops, bytes_accessed=size, transcendentals=0),
        name=name,
    )(*scalars, *arrays, *(pltpu.with_memory_space_constraint(a, pltpu.HBM) for a in hbm), *after)


def fetched(arrays):
    return [pltpu.VMEM(a.shape, a.dtype) for a in arrays] + [
        pltpu.SemaphoreType.DMA((len(arrays),))
    ]


def fetch(from_refs, to_refs, sems):
    copies = [
        pltpu.make_async_copy(source, to, sems.at[at])
        for at, (source, to) in enumerate(zip(from_refs, to_refs))
    ]
    for copy in copies:
        copy.start()
    return copies


def place_tiles(dst_ref, src_ref, count_ref, tiles_ref, adj_ref, first, last):
    adj_ref[...] = jnp.zeros_like(adj_ref)

    def step(slot, carry):
        block = src_ref[0, slot]

        @pl.when(jnp.logical_and(block >= first, block < last))
        def _():
            row = pl.multiple_of(dst_ref[0, slot] * BLK, BLK)
            col = pl.multiple_of((block - first) * BLK, BLK)
            adj_ref[pl.ds(row, BLK), pl.ds(col, BLK)] = tiles_ref[slot]

        return carry

    lax.fori_loop(0, count_ref[0], step, 0)


def boundary_places(rep, lists_ref, rows, order):
    slots, parts = lists_ref.shape
    lists = lists_ref[...].astype(F32)
    wanted = jnp.sum(
        jnp.where(iota((slots, parts), 0) == rep, lists, 0.0), axis=0, keepdims=True
    ).astype(jnp.int32)
    place = iota((rows, parts), 0)
    places = jnp.concatenate([(place == wanted).astype(BF16), (place == rep).astype(BF16)], 1)
    return dot(places, order.astype(BF16), 1, 1).astype(BF16)


def summed_by_z(parts):
    shape = (2 * parts, 2 * parts)
    out, into = iota(shape, 0), iota(shape, 1)
    line, z = out % (2 * Y_SIZE), out // (2 * Y_SIZE)
    halo = jnp.logical_and(line < Y_SIZE, into == z * Y_SIZE + line)
    hub = jnp.logical_and(line == Y_SIZE, into == parts)
    return jnp.logical_or(halo, hub)


def send_kernel(rep_ref, lists_hbm, feats_hbm, send_ref, lists_ref, feats_ref, sems):
    lists_copy, feats_copy = fetch((lists_hbm, feats_hbm), (lists_ref, feats_ref), sems)
    slots, parts = lists_ref.shape
    depth = parts // Y_SIZE
    rep = rep_ref[0]
    shape = (2 * parts, parts)
    out, into = iota(shape, 0), iota(shape, 1)
    row, z = out % (2 * Y_SIZE), out // (2 * Y_SIZE)
    of_part = (into == z * Y_SIZE + row % Y_SIZE).astype(BF16)
    lists_copy.wait()
    lists = lists_ref[...]
    high, low = (lists // 256).astype(BF16), (lists % 256).astype(BF16)
    wanted = dot(of_part, high, 1, 1) * 256.0 + dot(of_part, low, 1, 1)
    shape = (2 * parts, slots)
    row = iota(shape, 0) % (2 * Y_SIZE)
    wanted = jnp.where(row < Y_SIZE, wanted, rep.astype(F32))
    wanted = jnp.sum(jnp.where(iota(shape, 1) == rep, wanted, 0.0), axis=1, keepdims=True)
    places = iota((2 * parts, feats_ref.shape[0]), 1) == wanted.astype(jnp.int32)
    places = places.astype(BF16)
    feats_copy.wait()
    rows = dot(places, feats_ref[...]).astype(BF16)
    lines = send_ref.shape[0] // depth
    shape = (depth * lines, 2 * parts)
    out, into = iota(shape, 0), iota(shape, 1)
    line, z = out % lines, out // lines
    packed = jnp.zeros(send_ref.shape, F32)
    for group in range(rows.shape[1] // LANES):
        first = group * (Y_SIZE + 1)
        wanted = jnp.where(
            jnp.logical_and(line >= first, line <= first + Y_SIZE),
            z * (2 * Y_SIZE) + line - first,
            -1,
        )
        lanes = slice(group * LANES, (group + 1) * LANES)
        packed += dot((into == wanted).astype(BF16), rows[:, lanes])
    send_ref[...] = packed.astype(BF16)


def plane_kernel(arrived_ref, send_ref):
    _, chunk, width = send_ref.shape
    depth = chunk // 2
    total = arrived_ref.shape[0]
    lines = total // depth
    shape = (Y_SIZE * chunk, total)
    out, into = iota(shape, 0), iota(shape, 1)
    z, kind, y = out % depth, out // depth % 2, out // chunk
    first = z * lines + jnp.where(kind == 0, y, Y_SIZE)
    arrived = arrived_ref[...]
    for group in range(width // LANES):
        moved = move(into == first + group * (Y_SIZE + 1), arrived)
        lanes = slice(group * LANES, (group + 1) * LANES)
        for y_to in range(Y_SIZE):
            for x_to in range(X_SIZE):
                send_ref[y_to * X_SIZE + x_to, :, lanes] = moved[y_to * chunk : (y_to + 1) * chunk]


def own_kernel(
    core_ref, count_ref, dst_hbm, src_hbm, tiles_hbm, feats_hbm, seeds_hbm, w_self_hbm,
    sums_ref, mats_hbm, dst_ref, src_ref, tiles_ref, feats_ref, seeds_ref, w_self_ref,
    sems, own_adj_ref, adj_ref, mats_ref, out_sem,
):
    *tile_copies, feats_copy, seeds_copy, w_self_copy = fetch(
        (dst_hbm, src_hbm, tiles_hbm, feats_hbm, seeds_hbm, w_self_hbm),
        (dst_ref, src_ref, tiles_ref, feats_ref, seeds_ref, w_self_ref),
        sems,
    )
    rows = feats_ref.shape[0]
    seeds = seeds_ref.shape[1]
    for copy in tile_copies:
        copy.wait()
    own_blocks = rows // BLK
    table = adj_ref.shape[1]
    place_tiles(dst_ref, src_ref, count_ref, tiles_ref, own_adj_ref, 0, own_blocks)
    place_tiles(
        dst_ref, src_ref, count_ref, tiles_ref, adj_ref, own_blocks, own_blocks + table // BLK
    )
    seeds_copy.wait()
    feats_copy.wait()
    picks = (iota((rows, seeds), 0) == seeds_ref[...]).astype(BF16)
    feats = feats_ref[...]
    mats_ref[2 * seeds + adj_ref.shape[1] :, :seeds] = dot(feats, picks, 0, 0).astype(BF16)
    chosen = dot(picks, feats, 0, 0).astype(BF16)
    w_self_copy.wait()
    sums_ref[:seeds] = dot(chosen, w_self_ref[...])
    sums_ref[seeds:] = dot(own_adj_ref[...], feats)
    adj = adj_ref[...]
    half = table // 2
    depth = half // PLANE // 2
    shape = (half, table)
    line, source = iota(shape, 0), iota(shape, 1)
    z, kind = line % depth, line // depth % 2
    x, y = line // (2 * depth) % X_SIZE, line // (2 * depth * X_SIZE)
    start = kind * half + (z * Y_SIZE + y) * SLOTS + x * CORES
    for far, core in enumerate((core_ref[0], 1 - core_ref[0])):
        order = (source == start + core).astype(BF16)
        mats_ref[far * seeds : (far + 1) * seeds, :half] = dot(adj, order, 1, 1).astype(BF16)
        first = 2 * seeds + far * half
        mats_ref[first : first + half, :seeds] = dot(order, adj, 1, 1).astype(BF16)
    back = pltpu.make_async_copy(mats_ref, mats_hbm, out_sem)
    back.start()
    back.wait()


def middle_kernel(
    core_ref, near_ref, far_ref, mats_ref, sums_ref, w_neigh_ref, cot_ref, bias_in_ref,
    out_ref, d_pre_ref, d_agg_ref, keep_ref, send_ref,
):
    width = w_neigh_ref.shape[0]
    half = near_ref.shape[0]
    seeds = cot_ref.shape[0]
    near_back, far_back, chosen_t = (2 * seeds + step * half for step in range(3))
    aggregate = (
        sums_ref[seeds:]
        + dot(mats_ref[:seeds, :half], near_ref[...])
        + dot(mats_ref[seeds : 2 * seeds, :half], far_ref[...])
    ).astype(BF16)
    preact = sums_ref[:seeds] + dot(aggregate, w_neigh_ref[...]) + bias_in_ref[...].astype(F32)
    gate = jax.nn.sigmoid(preact)
    out_ref[...] = (preact * gate).astype(BF16)
    d_pre = (cot_ref[...].astype(F32) * gate * (1.0 + preact * (1.0 - gate))).astype(BF16)
    d_pre_ref[...] = d_pre
    d_agg = dot(d_pre, w_neigh_ref[...], 1, 1).astype(BF16)
    d_agg_ref[...] = d_agg
    first = dot(mats_ref[chosen_t:, :seeds], d_pre).astype(BF16)
    second = dot(aggregate, d_pre, 0, 0).astype(BF16)
    is_first = core_ref[0] == 0
    keep_ref[:width] = jnp.where(is_first, first, second)
    send_ref[:width] = jnp.where(is_first, second, first)
    keep_ref[width : width + half] = dot(mats_ref[near_back:far_back, :seeds], d_agg).astype(BF16)
    send_ref[width : width + half] = dot(mats_ref[far_back:chosen_t, :seeds], d_agg).astype(BF16)
    bias = two_rows(jnp.sum(d_pre.astype(F32), 0, keepdims=True), keep_ref.shape[0] - width - half)
    keep_ref[width + half :] = bias
    send_ref[width + half :] = bias


def pair_sum_kernel(keep_ref, other_ref, send_ref, bias_ref):
    chunks, lines, width = send_ref.shape
    total = keep_ref[...].astype(F32) + other_ref[...].astype(F32)
    weight = width // chunks
    table = lines - weight
    bias_ref[...] = jnp.sum(total[width + chunks * table :], 0, keepdims=True)
    total = total.astype(BF16)
    for chunk in range(chunks):
        send_ref[chunk, :weight] = total[chunk * weight : (chunk + 1) * weight]
        send_ref[chunk, weight:] = total[width + chunk * table : width + (chunk + 1) * table]


def plane_sum_kernel(arrived_ref, bias_ref, send_ref):
    chunks, lines, width = arrived_ref.shape
    depth, block, _ = send_ref.shape
    weight = width // chunks
    each = weight // depth
    tail = weight + 2 * depth
    rows = []
    rest = None
    for y in range(Y_SIZE):
        some = arrived_ref[y * X_SIZE].astype(F32)
        for x in range(1, X_SIZE):
            some = some + arrived_ref[y * X_SIZE + x].astype(F32)
        rows.append(some[weight : weight + depth])
        rest = some if rest is None else rest + some
    bias = jnp.zeros((depth, width), F32) + bias_ref[...]
    rows += [rest[weight + depth : tail], rest[:weight], bias]
    rows = jnp.concatenate(rows, 0).astype(BF16)
    shape = (depth * block, rows.shape[0])
    out, into = iota(shape, 0), iota(shape, 1)
    line, z = out % block, out // block
    first = (Y_SIZE + 1) * depth
    of_weight = jnp.logical_and(line > Y_SIZE, line <= Y_SIZE + each)
    wanted = jnp.where(
        of_weight,
        first + z * each + line - Y_SIZE - 1,
        jnp.where(line <= Y_SIZE, line * depth, first + weight) + z,
    )
    send_ref[...] = move(into == wanted, rows).reshape(depth, block, width)


def weight_kernel(scale, arrived_ref, send_ref, bias_ref):
    depth, block, width = arrived_ref.shape
    total = jnp.sum(arrived_ref[...].astype(F32), 0) * scale
    each = block - Y_SIZE - 2
    row = iota((block, LANES), 0)
    done = jnp.zeros((block, LANES), F32)
    for group in range(width // LANES):
        for line in range(each):
            some = total[Y_SIZE + 1 + line : Y_SIZE + 2 + line, group * LANES : (group + 1) * LANES]
            done = jnp.where(row == group * each + line, some, done)
    done = done.astype(BF16)
    for z in range(depth):
        send_ref[z] = done
    bias_ref[...] = total[block - 1 :]


def gather_kernel(arrived_ref, whole_ref):
    weight, width = whole_ref.shape
    depth, block, _ = arrived_ref.shape
    groups = width // LANES
    each = weight // depth
    arrived = arrived_ref[...].reshape(depth * block, LANES)
    shape = (weight, depth * block)
    out, into = iota(shape, 0), iota(shape, 1)
    z, line = out // each, out % each
    for group in range(groups):
        rows = move(into == z * block + group * each + line, arrived)
        whole_ref[:, group * LANES : (group + 1) * LANES] = rows


def spread_kernel(whole_ref, bias_ref, send_ref):
    chunks, lines, _ = send_ref.shape
    bias = two_rows(bias_ref[...], lines - whole_ref.shape[0]).astype(F32)
    message = jnp.concatenate([whole_ref[...].astype(F32), bias], 0).astype(BF16)
    for chunk in range(chunks):
        send_ref[chunk] = message


def own_back_kernel(
    dst_ref, src_ref, count_ref, tiles_ref, seeds_ref, d_pre_ref, d_agg_ref, w_self_ref,
    own_ref, adj_ref,
):
    rows = own_ref.shape[0]
    seeds = seeds_ref.shape[1]
    place_tiles(dst_ref, src_ref, count_ref, tiles_ref, adj_ref, 0, rows // BLK)
    picks = (iota((rows, seeds), 0) == seeds_ref[...]).astype(BF16)
    seeded = dot(picks, d_pre_ref[...]).astype(BF16)
    own_ref[...] = dot(seeded, w_self_ref[...], 1, 1) + dot(adj_ref[...], d_agg_ref[...], 0, 0)


def scatter_kernel(rep_ref, lists_ref, arrived_ref, own_ref, keep_ref, *send_refs_and_total):
    *send_refs, total_ref = send_refs_and_total
    rows, width = own_ref.shape
    rep = rep_ref[0]
    places = boundary_places(rep, lists_ref, rows, summed_by_z(lists_ref.shape[1]))
    back = arrived_ref[...].reshape(places.shape[1], width)
    total_ref[...] = own_ref[...] + dot(places, back)
    share = rows // (X_SIZE * CORES)
    for step, ref in enumerate([keep_ref, *send_refs]):
        for core in range(CORES):
            place = jnp.bitwise_xor(rep, step * CORES + core)
            some = total_ref[pl.ds(pl.multiple_of(place * share, 32), share), :]
            ref[core * share : (core + 1) * share] = some.astype(ref.dtype)


def row_sum_kernel(keep_ref, *refs):
    *arrived_refs, own_ref, send_ref = refs
    share = own_ref.shape[0]
    total = keep_ref[...]
    for ref in arrived_refs:
        total = total + ref[...].astype(F32)
    own_ref[...] = total[:share]
    send_ref[...] = total[share:].astype(BF16)


def join_kernel(arrived_ref, rows_ref, send_ref):
    chunks, _, width = arrived_ref.shape
    weight = width // chunks
    for chunk in range(chunks):
        send_ref[chunk * weight : (chunk + 1) * weight] = arrived_ref[chunk, :weight]
    send_ref[width:] = rows_ref[...]


def bias_kernel(arrived_ref, bias_ref):
    chunks, _, width = arrived_ref.shape
    weight = width // chunks
    bias = jnp.zeros(bias_ref.shape, F32)
    for chunk in range(chunks):
        arrived = arrived_ref[chunk].astype(F32)
        bias = bias + jnp.sum(arrived[weight:], 0, keepdims=True)
    bias_ref[...] = bias


def finish_kernel(core_ref, near_ref, own_ref, far_ref, first_ref, second_ref, rows_ref):
    width = first_ref.shape[0]
    near, far = near_ref[:width], far_ref[:width]
    is_first = core_ref[0] == 0
    first_ref[...] = jnp.where(is_first, near, far)
    second_ref[...] = jnp.where(is_first, far, near)
    rows_ref[...] = own_ref[...] + far_ref[width:].astype(F32)


def body(
    feats,
    halo_index,
    seed_ids,
    tiles,
    tile_dst,
    tile_src,
    tile_count,
    w_self,
    w_neigh,
    bias,
    cotangent,
):
    depth = lax.axis_size("z")
    parts = depth * Y_SIZE
    reps = X_SIZE * CORES
    rows, width = feats.shape
    seeds = cotangent.shape[0]
    half = parts * SLOTS
    core_id = lax.axis_index("core").astype(jnp.int32)
    x_id = lax.axis_index("x").astype(jnp.int32)
    core = core_id.reshape(1)
    rep = (x_id * CORES + core_id).reshape(1)
    lists = halo_index[0].T
    seed_row = seed_ids.reshape(1, seeds)
    tile_scalars = (tile_dst, tile_src, tile_count)
    scale = float(seeds * parts * reps) ** (-0.5)

    window = 20_000_000_000

    def swap(values, axis):
        return lax.all_to_all(values, axis, split_axis=0, concat_axis=0, tiled=True)

    def pair(values):
        return lax.ppermute(values, "core", [(0, 1), (1, 0)])

    lines = -(-(Y_SIZE + 1) * (width // LANES) // 8) * 8
    (send,) = call(
        send_kernel, "pick_boundary", [((depth * lines, LANES), BF16)], [rep], [],
        hbm=[lists, feats], scratch=fetched([lists, feats]), flops=4 * parts * rows * width,
    )
    by_depth = swap(send.reshape(depth, lines, LANES), "z").reshape(depth * lines, LANES)
    mats_shape = (2 * (seeds + half) + width, max(seeds, half))
    own_args = [tile_dst, tile_src, tiles, feats, seed_row, w_self]
    sums, mats = call(
        own_kernel, "own_rows", [((2 * seeds, width), F32)], [core, tile_count], [],
        hbm=own_args,
        hbm_outs=[(mats_shape, BF16)],
        scratch=[pltpu.SMEM(a.shape, a.dtype) for a in (tile_dst, tile_src)]
        + fetched(own_args)[2:]
        + [
            pltpu.VMEM((seeds, rows), BF16),
            pltpu.VMEM((seeds, 2 * half), BF16),
            pltpu.VMEM(mats_shape, BF16),
            pltpu.SemaphoreType.DMA,
        ],
        flops=2 * seeds * (3 * rows * width + width * width + 8 * half * half),
    )
    (plane,) = call(
        plane_kernel, "spread_plane", [((PLANE, 2 * depth, width), BF16)], [], [by_depth],
        flops=8 * parts * parts * width, after=[sums],
    )
    near = swap(plane, ("y", "x")).reshape(half, width)
    far = pair(near)

    out, d_pre, d_agg, keep, pair_send = call(
        middle_kernel, "forward_backward",
        [
            ((seeds, width), BF16),
            ((seeds, width), BF16),
            ((seeds, width), BF16),
            ((width + half + 16, width), BF16),
            ((width + half + 16, width), BF16),
        ],
        [core],
        [
            near, far, mats, sums, w_neigh, cotangent, bias.reshape(1, width),
        ],
        flops=2 * seeds * width * (4 * half + 4 * width),
    )

    pair_arrived = pair(pair_send)
    (own,) = call(
        own_back_kernel, "own_rows_back", [((rows, width), F32)],
        [*tile_scalars], [tiles, seed_row, d_pre, d_agg, w_self],
        scratch=[pltpu.VMEM((seeds, rows), BF16)],
        flops=2 * seeds * width * 3 * rows,
    )
    plane_send, pair_bias = call(
        pair_sum_kernel, "sum_pair",
        [((PLANE, width // PLANE + 2 * depth, width), BF16), ((1, width), F32)],
        [], [keep, pair_arrived], after=[own],
    )
    plane_arrived = swap(plane_send, ("y", "x"))
    (depth_send,) = call(
        plane_sum_kernel, "sum_plane",
        [((depth, 2 * Y_SIZE, width), BF16)],
        [], [plane_arrived, pair_bias],
    )
    depth_arrived = swap(depth_send, "z")
    weight_send, plane_bias = call(
        functools.partial(weight_kernel, scale), "sum_weights",
        [((depth, 2 * Y_SIZE, LANES), BF16), ((1, width), F32)],
        [], [depth_arrived],
    )
    weight_depth = swap(weight_send, "z")
    share = rows // reps
    row_keep, *row_sends = call(
        scatter_kernel, "return_rows",
        [((CORES * share, width), F32)] + [((CORES * share, width), BF16)] * (X_SIZE - 1),
        [rep], [lists, depth_arrived, own],
        scratch=[pltpu.VMEM((rows, width), F32)],
        flops=4 * parts * rows * width, after=[weight_send],
    )
    row_arrived = [
        lax.ppermute(row_sends[step - 1], "x", [(x, x ^ step) for x in range(X_SIZE)])
        for step in (2, 1, 3)
    ]
    (weight_rows,) = call(
        gather_kernel, "gather_weights", [((width // PLANE, width), BF16)],
        [], [weight_depth], flops=window, after=[row_keep],
    )
    row_own, row_send = call(
        row_sum_kernel, "sum_rows", [((share, width), F32), ((share, width), BF16)],
        [], [row_keep, *row_arrived], flops=window,
    )
    (weight_plane,) = call(
        spread_kernel, "spread_weights", [((PLANE, width // PLANE + 8, width), BF16)],
        [], [weight_rows, plane_bias],
    )
    weight_near = swap(weight_plane, ("y", "x"))
    (last_send,) = call(
        join_kernel, "join", [((width + share, width), BF16)], [], [weight_near, row_send]
    )
    (grad_bias,) = call(
        bias_kernel, "sum_bias", [((1, width), F32)], [], [weight_near], after=[last_send]
    )
    grad_self, grad_neigh, input_grad = call(
        finish_kernel, "finish",
        [((width, width), BF16), ((width, width), BF16), ((share, width), F32)],
        [core], [last_send, row_own, pair(last_send)],
    )
    grad_bias = grad_bias.reshape(width)
    return (out, input_grad, grad_self, grad_neigh, grad_bias)


def solution(mesh):
    parts = mesh.shape["dom"]
    physical = Mesh(
        mesh.devices.reshape(parts // Y_SIZE, Y_SIZE, X_SIZE, CORES), ("z", "y", "x", "core")
    )
    dom = ("z", "y")
    every = ("z", "y", "x", "core")
    placed = (
        P(dom, None),
        P(dom, None, None),
        P(every),
        P(every, None, None),
        P(every, None),
        P(every, None),
        P(every),
        P(),
        P(),
        P(),
        P(every, None),
    )
    return jax.shard_map(
        body,
        mesh=physical,
        in_specs=placed,
        out_specs=(P(every, None), P(every, None), P(), P(), P()),
        check_vma=False,
    )
```

```python
import functools
import math

import jax
import jax.numpy as jnp
from jax import lax
from jax.experimental import pallas as pl
from jax.experimental.pallas import tpu as pltpu
from jax.sharding import Mesh
from jax.sharding import PartitionSpec as P

BLK = 128
LANES = 128
SLOTS = 8
X_SIZE = 4
CORES = 2
Y_SIZE = 4
PLANE = Y_SIZE * X_SIZE
BF16 = jnp.bfloat16
F32 = jnp.float32
VMEM_BYTES = 24 * 1024 * 1024


def dot(a, b, contract_a=1, contract_b=0):
    return lax.dot_general(
        a, b, (((contract_a,), (contract_b,)), ((), ())), preferred_element_type=F32
    )


def move(matrix, rows):
    return dot(matrix.astype(BF16), rows).astype(BF16)


def iota(shape, dim):
    return lax.broadcasted_iota(jnp.int32, shape, dim)


def two_rows(wide, rows):
    high = wide.astype(BF16).astype(F32)
    row = iota((rows, wide.shape[1]), 0)
    return jnp.where(row == 0, high, jnp.where(row == 1, wide - high, 0.0)).astype(BF16)


def call(kernel, name, outs, scalars, arrays, scratch=(), flops=0, after=(), hbm=(), hbm_outs=()):
    if after:
        inner, at = kernel, len(scalars) + len(arrays) + len(hbm)
        kernel = lambda *refs: inner(*refs[:at], *refs[at + len(after) :])
    shapes = tuple(jax.ShapeDtypeStruct(shape, dtype) for shape, dtype in outs)
    shapes += tuple(pltpu.HBM(shape, dtype) for shape, dtype in hbm_outs)
    size = sum(math.prod(a.shape) * a.dtype.itemsize for a in (*arrays, *hbm, *shapes))
    return pl.pallas_call(
        kernel,
        out_shape=shapes,
        in_specs=[pl.BlockSpec(memory_space=pltpu.SMEM)] * len(scalars)
        + [pl.BlockSpec(memory_space=pltpu.VMEM)] * len(arrays)
        + [pl.BlockSpec(memory_space=pltpu.HBM)] * len(hbm)
        + [pl.BlockSpec(memory_space=pl.ANY)] * len(after),
        out_specs=tuple([pl.BlockSpec(memory_space=pltpu.VMEM)] * len(outs))
        + tuple([pl.BlockSpec(memory_space=pltpu.HBM)] * len(hbm_outs)),
        scratch_shapes=list(scratch),
        compiler_params=pltpu.CompilerParams(vmem_limit_bytes=VMEM_BYTES),
        cost_estimate=pl.CostEstimate(flops=flops, bytes_accessed=size, transcendentals=0),
        name=name,
    )(*scalars, *arrays, *(pltpu.with_memory_space_constraint(a, pltpu.HBM) for a in hbm), *after)


def fetched(arrays):
    return [pltpu.VMEM(a.shape, a.dtype) for a in arrays] + [
        pltpu.SemaphoreType.DMA((len(arrays),))
    ]


def fetch(from_refs, to_refs, sems):
    copies = [
        pltpu.make_async_copy(source, to, sems.at[at])
        for at, (source, to) in enumerate(zip(from_refs, to_refs))
    ]
    for copy in copies:
        copy.start()
    return copies


def place_tiles(dst_ref, src_ref, count_ref, tiles_ref, adj_ref, first, last):
    adj_ref[...] = jnp.zeros_like(adj_ref)

    def step(slot, carry):
        block = src_ref[0, slot]

        @pl.when(jnp.logical_and(block >= first, block < last))
        def _():
            row = pl.multiple_of(dst_ref[0, slot] * BLK, BLK)
            col = pl.multiple_of((block - first) * BLK, BLK)
            adj_ref[pl.ds(row, BLK), pl.ds(col, BLK)] = tiles_ref[slot]

        return carry

    lax.fori_loop(0, count_ref[0], step, 0)


def boundary_places(rep, lists_ref, rows, order):
    slots, parts = lists_ref.shape
    lists = lists_ref[...].astype(F32)
    wanted = jnp.sum(
        jnp.where(iota((slots, parts), 0) == rep, lists, 0.0), axis=0, keepdims=True
    ).astype(jnp.int32)
    place = iota((rows, parts), 0)
    places = jnp.concatenate([(place == wanted).astype(BF16), (place == rep).astype(BF16)], 1)
    return dot(places, order.astype(BF16), 1, 1).astype(BF16)


def summed_by_z(parts):
    shape = (2 * parts, 2 * parts)
    out, into = iota(shape, 0), iota(shape, 1)
    line, z = out % (2 * Y_SIZE), out // (2 * Y_SIZE)
    halo = jnp.logical_and(line < Y_SIZE, into == z * Y_SIZE + line)
    hub = jnp.logical_and(line == Y_SIZE, into == parts)
    return jnp.logical_or(halo, hub)


def send_kernel(rep_ref, lists_hbm, feats_hbm, send_ref, lists_ref, feats_ref, sems):
    lists_copy, feats_copy = fetch((lists_hbm, feats_hbm), (lists_ref, feats_ref), sems)
    slots, parts = lists_ref.shape
    depth = parts // Y_SIZE
    rep = rep_ref[0]
    shape = (2 * parts, parts)
    out, into = iota(shape, 0), iota(shape, 1)
    row, z = out % (2 * Y_SIZE), out // (2 * Y_SIZE)
    of_part = (into == z * Y_SIZE + row % Y_SIZE).astype(BF16)
    lists_copy.wait()
    lists = lists_ref[...]
    high, low = (lists // 256).astype(BF16), (lists % 256).astype(BF16)
    wanted = dot(of_part, high, 1, 1) * 256.0 + dot(of_part, low, 1, 1)
    shape = (2 * parts, slots)
    row = iota(shape, 0) % (2 * Y_SIZE)
    wanted = jnp.where(row < Y_SIZE, wanted, rep.astype(F32))
    wanted = jnp.sum(jnp.where(iota(shape, 1) == rep, wanted, 0.0), axis=1, keepdims=True)
    places = iota((2 * parts, feats_ref.shape[0]), 1) == wanted.astype(jnp.int32)
    places = places.astype(BF16)
    feats_copy.wait()
    rows = dot(places, feats_ref[...]).astype(BF16)
    lines = send_ref.shape[0] // depth
    shape = (depth * lines, 2 * parts)
    out, into = iota(shape, 0), iota(shape, 1)
    line, z = out % lines, out // lines
    packed = jnp.zeros(send_ref.shape, F32)
    for group in range(rows.shape[1] // LANES):
        first = group * (Y_SIZE + 1)
        wanted = jnp.where(
            jnp.logical_and(line >= first, line <= first + Y_SIZE),
            z * (2 * Y_SIZE) + line - first,
            -1,
        )
        lanes = slice(group * LANES, (group + 1) * LANES)
        packed += dot((into == wanted).astype(BF16), rows[:, lanes])
    send_ref[...] = packed.astype(BF16)


def plane_kernel(arrived_ref, send_ref):
    _, chunk, width = send_ref.shape
    depth = chunk // 2
    total = arrived_ref.shape[0]
    lines = total // depth
    shape = (Y_SIZE * chunk, total)
    out, into = iota(shape, 0), iota(shape, 1)
    z, kind, y = out % depth, out // depth % 2, out // chunk
    first = z * lines + jnp.where(kind == 0, y, Y_SIZE)
    arrived = arrived_ref[...]
    for group in range(width // LANES):
        moved = move(into == first + group * (Y_SIZE + 1), arrived)
        lanes = slice(group * LANES, (group + 1) * LANES)
        for y_to in range(Y_SIZE):
            for x_to in range(X_SIZE):
                send_ref[y_to * X_SIZE + x_to, :, lanes] = moved[y_to * chunk : (y_to + 1) * chunk]


def own_kernel(
    core_ref, count_ref, dst_hbm, src_hbm, tiles_hbm, feats_hbm, seeds_hbm, w_self_hbm,
    sums_ref, mats_hbm, dst_ref, src_ref, tiles_ref, feats_ref, seeds_ref, w_self_ref,
    sems, own_adj_ref, adj_ref, mats_ref, out_sems,
):
    *tile_copies, feats_copy, seeds_copy, w_self_copy = fetch(
        (dst_hbm, src_hbm, tiles_hbm, feats_hbm, seeds_hbm, w_self_hbm),
        (dst_ref, src_ref, tiles_ref, feats_ref, seeds_ref, w_self_ref),
        sems,
    )
    rows = feats_ref.shape[0]
    seeds = seeds_ref.shape[1]
    for copy in tile_copies:
        copy.wait()
    own_blocks = rows // BLK
    table = adj_ref.shape[1]
    place_tiles(dst_ref, src_ref, count_ref, tiles_ref, own_adj_ref, 0, own_blocks)
    place_tiles(
        dst_ref, src_ref, count_ref, tiles_ref, adj_ref, own_blocks, own_blocks + table // BLK
    )
    adj = adj_ref[...]
    half = table // 2
    depth = half // PLANE // 2
    shape = (half, table)
    line, source = iota(shape, 0), iota(shape, 1)
    z, kind = line % depth, line // depth % 2
    x, y = line // (2 * depth) % X_SIZE, line // (2 * depth * X_SIZE)
    start = kind * half + (z * Y_SIZE + y) * SLOTS + x * CORES
    for far, core in enumerate((core_ref[0], 1 - core_ref[0])):
        order = (source == start + core).astype(BF16)
        mats_ref[far * seeds : (far + 1) * seeds, :half] = dot(adj, order, 1, 1).astype(BF16)
        first = 2 * seeds + far * half
        mats_ref[first : first + half, :seeds] = dot(order, adj, 1, 1).astype(BF16)
    ready = pl.ds(0, 2 * (seeds + half))
    early = pltpu.make_async_copy(mats_ref.at[ready], mats_hbm.at[ready], out_sems.at[0])
    early.start()
    seeds_copy.wait()
    feats_copy.wait()
    picks = (iota((rows, seeds), 0) == seeds_ref[...]).astype(BF16)
    feats = feats_ref[...]
    mats_ref[2 * (seeds + half) :, :seeds] = dot(feats, picks, 0, 0).astype(BF16)
    rest = pl.ds(2 * (seeds + half), mats_ref.shape[0] - 2 * (seeds + half))
    late = pltpu.make_async_copy(mats_ref.at[rest], mats_hbm.at[rest], out_sems.at[1])
    late.start()
    chosen = dot(picks, feats, 0, 0).astype(BF16)
    w_self_copy.wait()
    sums_ref[:seeds] = dot(chosen, w_self_ref[...])
    sums_ref[seeds:] = dot(own_adj_ref[...], feats)
    early.wait()
    late.wait()


def near_kernel(near_ref, mats_ref, sums_ref, part_ref):
    seeds, half = part_ref.shape[0], near_ref.shape[0]
    part_ref[...] = sums_ref[seeds:] + dot(mats_ref[:seeds, :half], near_ref[...])


def middle_kernel(
    core_ref, part_ref, far_ref, mats_ref, sums_ref, w_neigh_ref, cot_ref, bias_in_ref,
    out_ref, d_pre_ref, d_agg_ref, keep_ref, send_ref,
):
    width = w_neigh_ref.shape[0]
    half = far_ref.shape[0]
    seeds = cot_ref.shape[0]
    near_back, far_back, chosen_t = (2 * seeds + step * half for step in range(3))
    aggregate = (
        part_ref[...] + dot(mats_ref[seeds : 2 * seeds, :half], far_ref[...])
    ).astype(BF16)
    preact = sums_ref[:seeds] + dot(aggregate, w_neigh_ref[...]) + bias_in_ref[...].astype(F32)
    gate = jax.nn.sigmoid(preact)
    out_ref[...] = (preact * gate).astype(BF16)
    d_pre = (cot_ref[...].astype(F32) * gate * (1.0 + preact * (1.0 - gate))).astype(BF16)
    d_pre_ref[...] = d_pre
    d_agg = dot(d_pre, w_neigh_ref[...], 1, 1).astype(BF16)
    d_agg_ref[...] = d_agg
    first = dot(mats_ref[chosen_t:, :seeds], d_pre).astype(BF16)
    second = dot(aggregate, d_pre, 0, 0).astype(BF16)
    is_first = core_ref[0] == 0
    keep_ref[:width] = jnp.where(is_first, first, second)
    send_ref[:width] = jnp.where(is_first, second, first)
    keep_ref[width : width + half] = dot(mats_ref[near_back:far_back, :seeds], d_agg).astype(BF16)
    send_ref[width : width + half] = dot(mats_ref[far_back:chosen_t, :seeds], d_agg).astype(BF16)
    bias = two_rows(jnp.sum(d_pre.astype(F32), 0, keepdims=True), keep_ref.shape[0] - width - half)
    keep_ref[width + half :] = bias
    send_ref[width + half :] = bias


def pair_sum_kernel(keep_ref, other_ref, send_ref, bias_ref):
    chunks, lines, width = send_ref.shape
    total = keep_ref[...].astype(F32) + other_ref[...].astype(F32)
    weight = width // chunks
    table = lines - weight
    bias_ref[...] = jnp.sum(total[width + chunks * table :], 0, keepdims=True)
    total = total.astype(BF16)
    for chunk in range(chunks):
        send_ref[chunk, :weight] = total[chunk * weight : (chunk + 1) * weight]
        send_ref[chunk, weight:] = total[width + chunk * table : width + (chunk + 1) * table]


def plane_sum_kernel(arrived_ref, bias_ref, send_ref):
    chunks, lines, width = arrived_ref.shape
    depth, block, _ = send_ref.shape
    weight = width // chunks
    each = weight // depth
    tail = weight + 2 * depth
    rows = []
    rest = None
    for y in range(Y_SIZE):
        some = arrived_ref[y * X_SIZE].astype(F32)
        for x in range(1, X_SIZE):
            some = some + arrived_ref[y * X_SIZE + x].astype(F32)
        rows.append(some[weight : weight + depth])
        rest = some if rest is None else rest + some
    bias = jnp.zeros((depth, width), F32) + bias_ref[...]
    rows += [rest[weight + depth : tail], rest[:weight], bias]
    rows = jnp.concatenate(rows, 0).astype(BF16)
    shape = (depth * block, rows.shape[0])
    out, into = iota(shape, 0), iota(shape, 1)
    line, z = out % block, out // block
    first = (Y_SIZE + 1) * depth
    of_weight = jnp.logical_and(line > Y_SIZE, line <= Y_SIZE + each)
    wanted = jnp.where(
        of_weight,
        first + z * each + line - Y_SIZE - 1,
        jnp.where(line <= Y_SIZE, line * depth, first + weight) + z,
    )
    send_ref[...] = move(into == wanted, rows).reshape(depth, block, width)


def weight_kernel(scale, arrived_ref, send_ref, bias_ref):
    depth, block, width = arrived_ref.shape
    total = jnp.sum(arrived_ref[...].astype(F32), 0) * scale
    each = block - Y_SIZE - 2
    row = iota((block, LANES), 0)
    done = jnp.zeros((block, LANES), F32)
    for group in range(width // LANES):
        for line in range(each):
            some = total[Y_SIZE + 1 + line : Y_SIZE + 2 + line, group * LANES : (group + 1) * LANES]
            done = jnp.where(row == group * each + line, some, done)
    done = done.astype(BF16)
    for z in range(depth):
        send_ref[z] = done
    bias_ref[...] = total[block - 1 :]


def gather_kernel(arrived_ref, whole_ref):
    weight, width = whole_ref.shape
    depth, block, _ = arrived_ref.shape
    groups = width // LANES
    each = weight // depth
    arrived = arrived_ref[...].reshape(depth * block, LANES)
    shape = (weight, depth * block)
    out, into = iota(shape, 0), iota(shape, 1)
    z, line = out // each, out % each
    for group in range(groups):
        rows = move(into == z * block + group * each + line, arrived)
        whole_ref[:, group * LANES : (group + 1) * LANES] = rows


def spread_kernel(whole_ref, bias_ref, send_ref):
    chunks, lines, _ = send_ref.shape
    bias = two_rows(bias_ref[...], lines - whole_ref.shape[0]).astype(F32)
    message = jnp.concatenate([whole_ref[...].astype(F32), bias], 0).astype(BF16)
    for chunk in range(chunks):
        send_ref[chunk] = message


def own_back_kernel(
    dst_ref, src_ref, count_ref, tiles_ref, seeds_ref, d_pre_ref, d_agg_ref, w_self_ref,
    own_ref, adj_ref,
):
    rows = own_ref.shape[0]
    seeds = seeds_ref.shape[1]
    place_tiles(dst_ref, src_ref, count_ref, tiles_ref, adj_ref, 0, rows // BLK)
    picks = (iota((rows, seeds), 0) == seeds_ref[...]).astype(BF16)
    seeded = dot(picks, d_pre_ref[...]).astype(BF16)
    own_ref[...] = dot(seeded, w_self_ref[...], 1, 1) + dot(adj_ref[...], d_agg_ref[...], 0, 0)


def scatter_kernel(rep_ref, lists_ref, arrived_ref, own_ref, keep_ref, *send_refs_and_total):
    *send_refs, total_ref = send_refs_and_total
    rows, width = own_ref.shape
    rep = rep_ref[0]
    places = boundary_places(rep, lists_ref, rows, summed_by_z(lists_ref.shape[1]))
    back = arrived_ref[...].reshape(places.shape[1], width)
    total_ref[...] = own_ref[...] + dot(places, back)
    share = rows // (X_SIZE * CORES)
    for step, ref in enumerate([keep_ref, *send_refs]):
        for core in range(CORES):
            place = jnp.bitwise_xor(rep, step * CORES + core)
            some = total_ref[pl.ds(pl.multiple_of(place * share, 32), share), :]
            ref[core * share : (core + 1) * share] = some.astype(ref.dtype)


def row_sum_kernel(keep_ref, *refs):
    *arrived_refs, own_ref, send_ref = refs
    share = own_ref.shape[0]
    total = keep_ref[...]
    for ref in arrived_refs:
        total = total + ref[...].astype(F32)
    own_ref[...] = total[:share]
    send_ref[...] = total[share:].astype(BF16)


def join_kernel(arrived_ref, rows_ref, send_ref):
    chunks, _, width = arrived_ref.shape
    weight = width // chunks
    for chunk in range(chunks):
        send_ref[chunk * weight : (chunk + 1) * weight] = arrived_ref[chunk, :weight]
    send_ref[width:] = rows_ref[...]


def bias_kernel(arrived_ref, bias_ref):
    chunks, _, width = arrived_ref.shape
    weight = width // chunks
    bias = jnp.zeros(bias_ref.shape, F32)
    for chunk in range(chunks):
        arrived = arrived_ref[chunk].astype(F32)
        bias = bias + jnp.sum(arrived[weight:], 0, keepdims=True)
    bias_ref[...] = bias


def finish_kernel(core_ref, near_ref, own_ref, far_ref, first_ref, second_ref, rows_ref):
    width = first_ref.shape[0]
    near, far = near_ref[:width], far_ref[:width]
    is_first = core_ref[0] == 0
    first_ref[...] = jnp.where(is_first, near, far)
    second_ref[...] = jnp.where(is_first, far, near)
    rows_ref[...] = own_ref[...] + far_ref[width:].astype(F32)


def body(
    feats,
    halo_index,
    seed_ids,
    tiles,
    tile_dst,
    tile_src,
    tile_count,
    w_self,
    w_neigh,
    bias,
    cotangent,
):
    depth = lax.axis_size("z")
    parts = depth * Y_SIZE
    reps = X_SIZE * CORES
    rows, width = feats.shape
    seeds = cotangent.shape[0]
    half = parts * SLOTS
    core_id = lax.axis_index("core").astype(jnp.int32)
    x_id = lax.axis_index("x").astype(jnp.int32)
    core = core_id.reshape(1)
    rep = (x_id * CORES + core_id).reshape(1)
    lists = halo_index[0].T
    seed_row = seed_ids.reshape(1, seeds)
    tile_scalars = (tile_dst, tile_src, tile_count)
    scale = float(seeds * parts * reps) ** (-0.5)

    window = 20_000_000_000

    def swap(values, axis):
        return lax.all_to_all(values, axis, split_axis=0, concat_axis=0, tiled=True)

    def pair(values):
        return lax.ppermute(values, "core", [(0, 1), (1, 0)])

    lines = -(-(Y_SIZE + 1) * (width // LANES) // 8) * 8
    (send,) = call(
        send_kernel, "pick_boundary", [((depth * lines, LANES), BF16)], [rep], [],
        hbm=[lists, feats], scratch=fetched([lists, feats]), flops=4 * parts * rows * width,
    )
    by_depth = swap(send.reshape(depth, lines, LANES), "z").reshape(depth * lines, LANES)
    mats_shape = (2 * (seeds + half) + width, max(seeds, half))
    own_args = [tile_dst, tile_src, tiles, feats, seed_row, w_self]
    sums, mats = call(
        own_kernel, "own_rows", [((2 * seeds, width), F32)], [core, tile_count], [],
        hbm=own_args,
        hbm_outs=[(mats_shape, BF16)],
        scratch=[pltpu.SMEM(a.shape, a.dtype) for a in (tile_dst, tile_src)]
        + fetched(own_args)[2:]
        + [
            pltpu.VMEM((seeds, rows), BF16),
            pltpu.VMEM((seeds, 2 * half), BF16),
            pltpu.VMEM(mats_shape, BF16),
            pltpu.SemaphoreType.DMA((2,)),
        ],
        flops=2 * seeds * (3 * rows * width + width * width + 8 * half * half),
    )
    (plane,) = call(
        plane_kernel, "spread_plane", [((PLANE, 2 * depth, width), BF16)], [], [by_depth],
        flops=8 * parts * parts * width, after=[sums],
    )
    near = swap(plane, ("y", "x")).reshape(half, width)
    far = pair(near)

    (part,) = call(
        near_kernel, "near_rows", [((seeds, width), F32)], [], [near, mats, sums],
        flops=2 * seeds * width * half,
    )
    out, d_pre, d_agg, keep, pair_send = call(
        middle_kernel, "forward_backward",
        [
            ((seeds, width), BF16),
            ((seeds, width), BF16),
            ((seeds, width), BF16),
            ((width + half + 16, width), BF16),
            ((width + half + 16, width), BF16),
        ],
        [core],
        [
            part, far, mats, sums, w_neigh, cotangent, bias.reshape(1, width),
        ],
        flops=2 * seeds * width * (4 * half + 4 * width),
    )

    pair_arrived = pair(pair_send)
    (own,) = call(
        own_back_kernel, "own_rows_back", [((rows, width), F32)],
        [*tile_scalars], [tiles, seed_row, d_pre, d_agg, w_self],
        scratch=[pltpu.VMEM((seeds, rows), BF16)],
        flops=2 * seeds * width * 3 * rows,
    )
    plane_send, pair_bias = call(
        pair_sum_kernel, "sum_pair",
        [((PLANE, width // PLANE + 2 * depth, width), BF16), ((1, width), F32)],
        [], [keep, pair_arrived], after=[own],
    )
    plane_arrived = swap(plane_send, ("y", "x"))
    (depth_send,) = call(
        plane_sum_kernel, "sum_plane",
        [((depth, 2 * Y_SIZE, width), BF16)],
        [], [plane_arrived, pair_bias],
    )
    depth_arrived = swap(depth_send, "z")
    weight_send, plane_bias = call(
        functools.partial(weight_kernel, scale), "sum_weights",
        [((depth, 2 * Y_SIZE, LANES), BF16), ((1, width), F32)],
        [], [depth_arrived],
    )
    weight_depth = swap(weight_send, "z")
    share = rows // reps
    row_keep, *row_sends = call(
        scatter_kernel, "return_rows",
        [((CORES * share, width), F32)] + [((CORES * share, width), BF16)] * (X_SIZE - 1),
        [rep], [lists, depth_arrived, own],
        scratch=[pltpu.VMEM((rows, width), F32)],
        flops=4 * parts * rows * width, after=[weight_send],
    )
    row_arrived = [
        lax.ppermute(row_sends[step - 1], "x", [(x, x ^ step) for x in range(X_SIZE)])
        for step in (2, 1, 3)
    ]
    (weight_rows,) = call(
        gather_kernel, "gather_weights", [((width // PLANE, width), BF16)],
        [], [weight_depth], flops=window, after=[row_keep],
    )
    row_own, row_send = call(
        row_sum_kernel, "sum_rows", [((share, width), F32), ((share, width), BF16)],
        [], [row_keep, *row_arrived], flops=window,
    )
    (weight_plane,) = call(
        spread_kernel, "spread_weights", [((PLANE, width // PLANE + 8, width), BF16)],
        [], [weight_rows, plane_bias],
    )
    weight_near = swap(weight_plane, ("y", "x"))
    (last_send,) = call(
        join_kernel, "join", [((width + share, width), BF16)], [], [weight_near, row_send]
    )
    (grad_bias,) = call(
        bias_kernel, "sum_bias", [((1, width), F32)], [], [weight_near], after=[last_send]
    )
    grad_self, grad_neigh, input_grad = call(
        finish_kernel, "finish",
        [((width, width), BF16), ((width, width), BF16), ((share, width), F32)],
        [core], [last_send, row_own, pair(last_send)],
    )
    grad_bias = grad_bias.reshape(width)
    return (out, input_grad, grad_self, grad_neigh, grad_bias)


def solution(mesh):
    parts = mesh.shape["dom"]
    physical = Mesh(
        mesh.devices.reshape(parts // Y_SIZE, Y_SIZE, X_SIZE, CORES), ("z", "y", "x", "core")
    )
    dom = ("z", "y")
    every = ("z", "y", "x", "core")
    placed = (
        P(dom, None),
        P(dom, None, None),
        P(every),
        P(every, None, None),
        P(every, None),
        P(every, None),
        P(every),
        P(),
        P(),
        P(),
        P(every, None),
    )
    return jax.shard_map(
        body,
        mesh=physical,
        in_specs=placed,
        out_specs=(P(every, None), P(every, None), P(), P(), P()),
        check_vma=False,
    )
```

```python
import functools
import math

import jax
import jax.numpy as jnp
from jax import lax
from jax.experimental import pallas as pl
from jax.experimental.pallas import tpu as pltpu
from jax.sharding import Mesh
from jax.sharding import PartitionSpec as P

BLK = 128
LANES = 128
SLOTS = 8
X_SIZE = 4
CORES = 2
Y_SIZE = 4
PLANE = Y_SIZE * X_SIZE
BF16 = jnp.bfloat16
F32 = jnp.float32
VMEM_BYTES = 24 * 1024 * 1024


def dot(a, b, contract_a=1, contract_b=0):
    return lax.dot_general(
        a, b, (((contract_a,), (contract_b,)), ((), ())), preferred_element_type=F32
    )


def move(matrix, rows):
    return dot(matrix.astype(BF16), rows).astype(BF16)


def iota(shape, dim):
    return lax.broadcasted_iota(jnp.int32, shape, dim)


def two_rows(wide, rows):
    high = wide.astype(BF16).astype(F32)
    row = iota((rows, wide.shape[1]), 0)
    return jnp.where(row == 0, high, jnp.where(row == 1, wide - high, 0.0)).astype(BF16)


def call(kernel, name, outs, scalars, arrays, scratch=(), flops=0, after=(), hbm=(), hbm_outs=()):
    if after:
        inner, at = kernel, len(scalars) + len(arrays) + len(hbm)
        kernel = lambda *refs: inner(*refs[:at], *refs[at + len(after) :])
    shapes = tuple(jax.ShapeDtypeStruct(shape, dtype) for shape, dtype in outs)
    shapes += tuple(pltpu.HBM(shape, dtype) for shape, dtype in hbm_outs)
    size = sum(math.prod(a.shape) * a.dtype.itemsize for a in (*arrays, *hbm, *shapes))
    return pl.pallas_call(
        kernel,
        out_shape=shapes,
        in_specs=[pl.BlockSpec(memory_space=pltpu.SMEM)] * len(scalars)
        + [pl.BlockSpec(memory_space=pltpu.VMEM)] * len(arrays)
        + [pl.BlockSpec(memory_space=pltpu.HBM)] * len(hbm)
        + [pl.BlockSpec(memory_space=pl.ANY)] * len(after),
        out_specs=tuple([pl.BlockSpec(memory_space=pltpu.VMEM)] * len(outs))
        + tuple([pl.BlockSpec(memory_space=pltpu.HBM)] * len(hbm_outs)),
        scratch_shapes=list(scratch),
        compiler_params=pltpu.CompilerParams(vmem_limit_bytes=VMEM_BYTES),
        cost_estimate=pl.CostEstimate(flops=flops, bytes_accessed=size, transcendentals=0),
        name=name,
    )(*scalars, *arrays, *(pltpu.with_memory_space_constraint(a, pltpu.HBM) for a in hbm), *after)


def fetched(arrays):
    return [pltpu.VMEM(a.shape, a.dtype) for a in arrays] + [
        pltpu.SemaphoreType.DMA((len(arrays),))
    ]


def fetch(from_refs, to_refs, sems):
    copies = [
        pltpu.make_async_copy(source, to, sems.at[at])
        for at, (source, to) in enumerate(zip(from_refs, to_refs))
    ]
    for copy in copies:
        copy.start()
    return copies


def place_tiles(dst_ref, src_ref, count_ref, tiles_ref, adj_ref, first, last):
    adj_ref[...] = jnp.zeros_like(adj_ref)

    def step(slot, carry):
        block = src_ref[0, slot]

        @pl.when(jnp.logical_and(block >= first, block < last))
        def _():
            row = pl.multiple_of(dst_ref[0, slot] * BLK, BLK)
            col = pl.multiple_of((block - first) * BLK, BLK)
            adj_ref[pl.ds(row, BLK), pl.ds(col, BLK)] = tiles_ref[slot]

        return carry

    lax.fori_loop(0, count_ref[0], step, 0)


def boundary_places(rep, lists_ref, rows, order):
    slots, parts = lists_ref.shape
    lists = lists_ref[...].astype(F32)
    wanted = jnp.sum(
        jnp.where(iota((slots, parts), 0) == rep, lists, 0.0), axis=0, keepdims=True
    ).astype(jnp.int32)
    place = iota((rows, parts), 0)
    places = jnp.concatenate([(place == wanted).astype(BF16), (place == rep).astype(BF16)], 1)
    return dot(places, order.astype(BF16), 1, 1).astype(BF16)


def summed_by_z(parts):
    shape = (2 * parts, 2 * parts)
    out, into = iota(shape, 0), iota(shape, 1)
    line, z = out % (2 * Y_SIZE), out // (2 * Y_SIZE)
    halo = jnp.logical_and(line < Y_SIZE, into == z * Y_SIZE + line)
    hub = jnp.logical_and(line == Y_SIZE, into == parts)
    return jnp.logical_or(halo, hub)


def send_kernel(rep_ref, lists_hbm, feats_hbm, send_ref, lists_ref, feats_ref, sems):
    lists_copy, feats_copy = fetch((lists_hbm, feats_hbm), (lists_ref, feats_ref), sems)
    slots, parts = lists_ref.shape
    depth = parts // Y_SIZE
    rep = rep_ref[0]
    shape = (2 * parts, parts)
    out, into = iota(shape, 0), iota(shape, 1)
    row, z = out % (2 * Y_SIZE), out // (2 * Y_SIZE)
    of_part = (into == z * Y_SIZE + row % Y_SIZE).astype(BF16)
    lists_copy.wait()
    lists = lists_ref[...]
    high, low = (lists // 256).astype(BF16), (lists % 256).astype(BF16)
    wanted = dot(of_part, high, 1, 1) * 256.0 + dot(of_part, low, 1, 1)
    shape = (2 * parts, slots)
    row = iota(shape, 0) % (2 * Y_SIZE)
    wanted = jnp.where(row < Y_SIZE, wanted, rep.astype(F32))
    wanted = jnp.sum(jnp.where(iota(shape, 1) == rep, wanted, 0.0), axis=1, keepdims=True)
    places = iota((2 * parts, feats_ref.shape[0]), 1) == wanted.astype(jnp.int32)
    places = places.astype(BF16)
    feats_copy.wait()
    rows = dot(places, feats_ref[...]).astype(BF16)
    lines = send_ref.shape[0] // depth
    shape = (depth * lines, 2 * parts)
    out, into = iota(shape, 0), iota(shape, 1)
    line, z = out % lines, out // lines
    packed = jnp.zeros(send_ref.shape, F32)
    for group in range(rows.shape[1] // LANES):
        first = group * (Y_SIZE + 1)
        wanted = jnp.where(
            jnp.logical_and(line >= first, line <= first + Y_SIZE),
            z * (2 * Y_SIZE) + line - first,
            -1,
        )
        lanes = slice(group * LANES, (group + 1) * LANES)
        packed += dot((into == wanted).astype(BF16), rows[:, lanes])
    send_ref[...] = packed.astype(BF16)


def plane_kernel(arrived_ref, send_ref):
    _, chunk, width = send_ref.shape
    depth = chunk // 2
    total = arrived_ref.shape[0]
    lines = total // depth
    shape = (Y_SIZE * chunk, total)
    out, into = iota(shape, 0), iota(shape, 1)
    z, kind, y = out % depth, out // depth % 2, out // chunk
    first = z * lines + jnp.where(kind == 0, y, Y_SIZE)
    arrived = arrived_ref[...]
    for group in range(width // LANES):
        moved = move(into == first + group * (Y_SIZE + 1), arrived)
        lanes = slice(group * LANES, (group + 1) * LANES)
        for y_to in range(Y_SIZE):
            for x_to in range(X_SIZE):
                send_ref[y_to * X_SIZE + x_to, :, lanes] = moved[y_to * chunk : (y_to + 1) * chunk]


def own_kernel(
    core_ref, count_ref, dst_hbm, src_hbm, tiles_hbm, feats_hbm, seeds_hbm, w_self_hbm,
    sums_ref, mats_hbm, dst_ref, src_ref, tiles_ref, feats_ref, seeds_ref, w_self_ref,
    sems, own_adj_ref, adj_ref, mats_ref, out_sems,
):
    *tile_copies, feats_copy, seeds_copy, w_self_copy = fetch(
        (dst_hbm, src_hbm, tiles_hbm, feats_hbm, seeds_hbm, w_self_hbm),
        (dst_ref, src_ref, tiles_ref, feats_ref, seeds_ref, w_self_ref),
        sems,
    )
    rows = feats_ref.shape[0]
    seeds = seeds_ref.shape[1]
    for copy in tile_copies:
        copy.wait()
    own_blocks = rows // BLK
    table = adj_ref.shape[1]
    place_tiles(dst_ref, src_ref, count_ref, tiles_ref, own_adj_ref, 0, own_blocks)
    place_tiles(
        dst_ref, src_ref, count_ref, tiles_ref, adj_ref, own_blocks, own_blocks + table // BLK
    )
    adj = adj_ref[...]
    half = table // 2
    depth = half // PLANE // 2
    shape = (half, table)
    line, source = iota(shape, 0), iota(shape, 1)
    z, kind = line % depth, line // depth % 2
    x, y = line // (2 * depth) % X_SIZE, line // (2 * depth * X_SIZE)
    start = kind * half + (z * Y_SIZE + y) * SLOTS + x * CORES
    for far, core in enumerate((core_ref[0], 1 - core_ref[0])):
        order = (source == start + core).astype(BF16)
        mats_ref[far * seeds : (far + 1) * seeds, :half] = dot(adj, order, 1, 1).astype(BF16)
        first = 2 * seeds + far * half
        mats_ref[first : first + half, :seeds] = dot(order, adj, 1, 1).astype(BF16)
    ready = pl.ds(0, 2 * (seeds + half))
    early = pltpu.make_async_copy(mats_ref.at[ready], mats_hbm.at[ready], out_sems.at[0])
    early.start()
    seeds_copy.wait()
    feats_copy.wait()
    picks = (iota((rows, seeds), 0) == seeds_ref[...]).astype(BF16)
    feats = feats_ref[...]
    mats_ref[2 * (seeds + half) :, :seeds] = dot(feats, picks, 0, 0).astype(BF16)
    rest = pl.ds(2 * (seeds + half), mats_ref.shape[0] - 2 * (seeds + half))
    late = pltpu.make_async_copy(mats_ref.at[rest], mats_hbm.at[rest], out_sems.at[1])
    late.start()
    chosen = dot(picks, feats, 0, 0).astype(BF16)
    w_self_copy.wait()
    sums_ref[:seeds] = dot(chosen, w_self_ref[...])
    sums_ref[seeds:] = dot(own_adj_ref[...], feats)
    early.wait()
    late.wait()


def near_kernel(near_ref, mats_ref, sums_ref, part_ref):
    seeds, half = part_ref.shape[0], near_ref.shape[0]
    part_ref[...] = sums_ref[seeds:] + dot(mats_ref[:seeds, :half], near_ref[...])


def middle_kernel(
    core_ref, part_ref, far_ref, mats_ref, sums_ref, w_neigh_ref, cot_ref, bias_in_ref,
    out_ref, d_pre_ref, d_agg_ref, keep_ref, send_ref,
):
    width = w_neigh_ref.shape[0]
    half = far_ref.shape[0]
    seeds = cot_ref.shape[0]
    near_back, far_back, chosen_t = (2 * seeds + step * half for step in range(3))
    aggregate = (
        part_ref[...] + dot(mats_ref[seeds : 2 * seeds, :half], far_ref[...])
    ).astype(BF16)
    preact = sums_ref[:seeds] + dot(aggregate, w_neigh_ref[...]) + bias_in_ref[...].astype(F32)
    gate = jax.nn.sigmoid(preact)
    out_ref[...] = (preact * gate).astype(BF16)
    d_pre = (cot_ref[...].astype(F32) * gate * (1.0 + preact * (1.0 - gate))).astype(BF16)
    d_pre_ref[...] = d_pre
    d_agg = dot(d_pre, w_neigh_ref[...], 1, 1).astype(BF16)
    d_agg_ref[...] = d_agg
    first = dot(mats_ref[chosen_t:, :seeds], d_pre).astype(BF16)
    second = dot(aggregate, d_pre, 0, 0).astype(BF16)
    is_first = core_ref[0] == 0
    keep_ref[:width] = jnp.where(is_first, first, second)
    send_ref[:width] = jnp.where(is_first, second, first)
    keep_ref[width : width + half] = dot(mats_ref[near_back:far_back, :seeds], d_agg).astype(BF16)
    send_ref[width : width + half] = dot(mats_ref[far_back:chosen_t, :seeds], d_agg).astype(BF16)
    bias = two_rows(jnp.sum(d_pre.astype(F32), 0, keepdims=True), keep_ref.shape[0] - width - half)
    keep_ref[width + half :] = bias
    send_ref[width + half :] = bias


def pair_sum_kernel(keep_ref, other_ref, send_ref, bias_ref):
    chunks, lines, width = send_ref.shape
    total = keep_ref[...].astype(F32) + other_ref[...].astype(F32)
    weight = width // chunks
    table = lines - weight
    bias_ref[...] = jnp.sum(total[width + chunks * table :], 0, keepdims=True)
    total = total.astype(BF16)
    for chunk in range(chunks):
        send_ref[chunk, :weight] = total[chunk * weight : (chunk + 1) * weight]
        send_ref[chunk, weight:] = total[width + chunk * table : width + (chunk + 1) * table]


def plane_sum_kernel(arrived_ref, bias_ref, send_ref):
    chunks, lines, width = arrived_ref.shape
    depth, block, _ = send_ref.shape
    weight = width // chunks
    each = weight // depth
    tail = weight + 2 * depth
    rows = []
    rest = None
    for y in range(Y_SIZE):
        some = arrived_ref[y * X_SIZE].astype(F32)
        for x in range(1, X_SIZE):
            some = some + arrived_ref[y * X_SIZE + x].astype(F32)
        rows.append(some[weight : weight + depth])
        rest = some if rest is None else rest + some
    bias = jnp.zeros((depth, width), F32) + bias_ref[...]
    rows += [rest[weight + depth : tail], rest[:weight], bias]
    rows = jnp.concatenate(rows, 0).astype(BF16)
    shape = (depth * block, rows.shape[0])
    out, into = iota(shape, 0), iota(shape, 1)
    line, z = out % block, out // block
    first = (Y_SIZE + 1) * depth
    of_weight = jnp.logical_and(line > Y_SIZE, line <= Y_SIZE + each)
    wanted = jnp.where(
        of_weight,
        first + z * each + line - Y_SIZE - 1,
        jnp.where(line <= Y_SIZE, line * depth, first + weight) + z,
    )
    send_ref[...] = move(into == wanted, rows).reshape(depth, block, width)


def weight_kernel(scale, arrived_ref, send_ref, bias_ref):
    depth, block, width = arrived_ref.shape
    total = jnp.sum(arrived_ref[...].astype(F32), 0) * scale
    each = block - Y_SIZE - 2
    row = iota((block, LANES), 0)
    done = jnp.zeros((block, LANES), F32)
    for group in range(width // LANES):
        for line in range(each):
            some = total[Y_SIZE + 1 + line : Y_SIZE + 2 + line, group * LANES : (group + 1) * LANES]
            done = jnp.where(row == group * each + line, some, done)
    done = done.astype(BF16)
    for z in range(depth):
        send_ref[z] = done
    bias_ref[...] = total[block - 1 :]


def gather_kernel(arrived_ref, whole_ref):
    weight, width = whole_ref.shape
    depth, block, _ = arrived_ref.shape
    groups = width // LANES
    each = weight // depth
    arrived = arrived_ref[...].reshape(depth * block, LANES)
    shape = (weight, depth * block)
    out, into = iota(shape, 0), iota(shape, 1)
    z, line = out // each, out % each
    for group in range(groups):
        rows = move(into == z * block + group * each + line, arrived)
        whole_ref[:, group * LANES : (group + 1) * LANES] = rows


def spread_kernel(whole_ref, bias_ref, send_ref):
    chunks, lines, _ = send_ref.shape
    bias = two_rows(bias_ref[...], lines - whole_ref.shape[0]).astype(F32)
    message = jnp.concatenate([whole_ref[...].astype(F32), bias], 0).astype(BF16)
    for chunk in range(chunks):
        send_ref[chunk] = message


def own_back_kernel(
    dst_ref, src_ref, count_ref, tiles_ref, seeds_ref, d_pre_ref, d_agg_ref, w_self_ref,
    own_ref, adj_ref,
):
    rows = own_ref.shape[0]
    seeds = seeds_ref.shape[1]
    place_tiles(dst_ref, src_ref, count_ref, tiles_ref, adj_ref, 0, rows // BLK)
    picks = (iota((rows, seeds), 0) == seeds_ref[...]).astype(BF16)
    seeded = dot(picks, d_pre_ref[...]).astype(BF16)
    own_ref[...] = dot(seeded, w_self_ref[...], 1, 1) + dot(adj_ref[...], d_agg_ref[...], 0, 0)


def scatter_kernel(rep_ref, lists_ref, arrived_ref, own_ref, keep_ref, *send_refs_and_total):
    *send_refs, total_ref = send_refs_and_total
    rows, width = own_ref.shape
    rep = rep_ref[0]
    places = boundary_places(rep, lists_ref, rows, summed_by_z(lists_ref.shape[1]))
    back = arrived_ref[...].reshape(places.shape[1], width)
    total_ref[...] = own_ref[...] + dot(places, back)
    share = rows // (X_SIZE * CORES)
    for step, ref in enumerate([keep_ref, *send_refs]):
        for core in range(CORES):
            place = jnp.bitwise_xor(rep, step * CORES + core)
            some = total_ref[pl.ds(pl.multiple_of(place * share, 32), share), :]
            ref[core * share : (core + 1) * share] = some.astype(ref.dtype)


def row_sum_kernel(keep_ref, *refs):
    *arrived_refs, own_ref, send_ref = refs
    share = own_ref.shape[0]
    total = keep_ref[...]
    for ref in arrived_refs:
        total = total + ref[...].astype(F32)
    own_ref[...] = total[:share]
    send_ref[...] = total[share:].astype(BF16)


def join_kernel(arrived_ref, send_ref):
    chunks, _, width = arrived_ref.shape
    weight = width // chunks
    for chunk in range(chunks):
        send_ref[chunk * weight : (chunk + 1) * weight] = arrived_ref[chunk, :weight]


def bias_kernel(arrived_ref, bias_ref):
    chunks, _, width = arrived_ref.shape
    weight = width // chunks
    bias = jnp.zeros(bias_ref.shape, F32)
    for chunk in range(chunks):
        arrived = arrived_ref[chunk].astype(F32)
        bias = bias + jnp.sum(arrived[weight:], 0, keepdims=True)
    bias_ref[...] = bias


def finish_kernel(core_ref, near_ref, own_ref, far_ref, row_far_ref, first_ref, second_ref, rows_ref):
    width = first_ref.shape[0]
    near, far = near_ref[:width], far_ref[:width]
    is_first = core_ref[0] == 0
    first_ref[...] = jnp.where(is_first, near, far)
    second_ref[...] = jnp.where(is_first, far, near)
    rows_ref[...] = own_ref[...] + row_far_ref[...].astype(F32)


def body(
    feats,
    halo_index,
    seed_ids,
    tiles,
    tile_dst,
    tile_src,
    tile_count,
    w_self,
    w_neigh,
    bias,
    cotangent,
):
    depth = lax.axis_size("z")
    parts = depth * Y_SIZE
    reps = X_SIZE * CORES
    rows, width = feats.shape
    seeds = cotangent.shape[0]
    half = parts * SLOTS
    core_id = lax.axis_index("core").astype(jnp.int32)
    x_id = lax.axis_index("x").astype(jnp.int32)
    core = core_id.reshape(1)
    rep = (x_id * CORES + core_id).reshape(1)
    lists = halo_index[0].T
    seed_row = seed_ids.reshape(1, seeds)
    tile_scalars = (tile_dst, tile_src, tile_count)
    scale = float(seeds * parts * reps) ** (-0.5)

    window = 20_000_000_000

    def swap(values, axis):
        return lax.all_to_all(values, axis, split_axis=0, concat_axis=0, tiled=True)

    def pair(values):
        return lax.ppermute(values, "core", [(0, 1), (1, 0)])

    lines = -(-(Y_SIZE + 1) * (width // LANES) // 8) * 8
    (send,) = call(
        send_kernel, "pick_boundary", [((depth * lines, LANES), BF16)], [rep], [],
        hbm=[lists, feats], scratch=fetched([lists, feats]), flops=4 * parts * rows * width,
    )
    by_depth = swap(send.reshape(depth, lines, LANES), "z").reshape(depth * lines, LANES)
    mats_shape = (2 * (seeds + half) + width, max(seeds, half))
    own_args = [tile_dst, tile_src, tiles, feats, seed_row, w_self]
    sums, mats = call(
        own_kernel, "own_rows", [((2 * seeds, width), F32)], [core, tile_count], [],
        hbm=own_args,
        hbm_outs=[(mats_shape, BF16)],
        scratch=[pltpu.SMEM(a.shape, a.dtype) for a in (tile_dst, tile_src)]
        + fetched(own_args)[2:]
        + [
            pltpu.VMEM((seeds, rows), BF16),
            pltpu.VMEM((seeds, 2 * half), BF16),
            pltpu.VMEM(mats_shape, BF16),
            pltpu.SemaphoreType.DMA((2,)),
        ],
        flops=2 * seeds * (3 * rows * width + width * width + 8 * half * half),
    )
    (plane,) = call(
        plane_kernel, "spread_plane", [((PLANE, 2 * depth, width), BF16)], [], [by_depth],
        flops=8 * parts * parts * width, after=[sums],
    )
    near = swap(plane, ("y", "x")).reshape(half, width)
    far = pair(near)

    (part,) = call(
        near_kernel, "near_rows", [((seeds, width), F32)], [], [near, mats, sums],
        flops=2 * seeds * width * half,
    )
    out, d_pre, d_agg, keep, pair_send = call(
        middle_kernel, "forward_backward",
        [
            ((seeds, width), BF16),
            ((seeds, width), BF16),
            ((seeds, width), BF16),
            ((width + half + 16, width), BF16),
            ((width + half + 16, width), BF16),
        ],
        [core],
        [
            part, far, mats, sums, w_neigh, cotangent, bias.reshape(1, width),
        ],
        flops=2 * seeds * width * (4 * half + 4 * width),
    )

    pair_arrived = pair(pair_send)
    (own,) = call(
        own_back_kernel, "own_rows_back", [((rows, width), F32)],
        [*tile_scalars], [tiles, seed_row, d_pre, d_agg, w_self],
        scratch=[pltpu.VMEM((seeds, rows), BF16)],
        flops=2 * seeds * width * 3 * rows,
    )
    plane_send, pair_bias = call(
        pair_sum_kernel, "sum_pair",
        [((PLANE, width // PLANE + 2 * depth, width), BF16), ((1, width), F32)],
        [], [keep, pair_arrived], after=[own],
    )
    plane_arrived = swap(plane_send, ("y", "x"))
    (depth_send,) = call(
        plane_sum_kernel, "sum_plane",
        [((depth, 2 * Y_SIZE, width), BF16)],
        [], [plane_arrived, pair_bias],
    )
    depth_arrived = swap(depth_send, "z")
    weight_send, plane_bias = call(
        functools.partial(weight_kernel, scale), "sum_weights",
        [((depth, 2 * Y_SIZE, LANES), BF16), ((1, width), F32)],
        [], [depth_arrived],
    )
    weight_depth = swap(weight_send, "z")
    share = rows // reps
    row_keep, *row_sends = call(
        scatter_kernel, "return_rows",
        [((CORES * share, width), F32)] + [((CORES * share, width), BF16)] * (X_SIZE - 1),
        [rep], [lists, depth_arrived, own],
        scratch=[pltpu.VMEM((rows, width), F32)],
        flops=4 * parts * rows * width, after=[weight_send],
    )
    row_arrived = [
        lax.ppermute(row_sends[step - 1], "x", [(x, x ^ step) for x in range(X_SIZE)])
        for step in (2, 1, 3)
    ]
    (weight_rows,) = call(
        gather_kernel, "gather_weights", [((width // PLANE, width), BF16)],
        [], [weight_depth], flops=window, after=[row_keep],
    )
    row_own, row_send = call(
        row_sum_kernel, "sum_rows", [((share, width), F32), ((share, width), BF16)],
        [], [row_keep, *row_arrived], flops=window,
    )
    (weight_plane,) = call(
        spread_kernel, "spread_weights", [((PLANE, width // PLANE + 8, width), BF16)],
        [], [weight_rows, plane_bias],
    )
    weight_near = swap(weight_plane, ("y", "x"))
    row_far = pair(row_send)
    (last_send,) = call(
        join_kernel, "join", [((width, width), BF16)], [], [weight_near], after=[row_far]
    )
    (grad_bias,) = call(
        bias_kernel, "sum_bias", [((1, width), F32)], [], [weight_near], after=[last_send]
    )
    grad_self, grad_neigh, input_grad = call(
        finish_kernel, "finish",
        [((width, width), BF16), ((width, width), BF16), ((share, width), F32)],
        [core], [last_send, row_own, pair(last_send), row_far],
    )
    grad_bias = grad_bias.reshape(width)
    return (out, input_grad, grad_self, grad_neigh, grad_bias)


def solution(mesh):
    parts = mesh.shape["dom"]
    physical = Mesh(
        mesh.devices.reshape(parts // Y_SIZE, Y_SIZE, X_SIZE, CORES), ("z", "y", "x", "core")
    )
    dom = ("z", "y")
    every = ("z", "y", "x", "core")
    placed = (
        P(dom, None),
        P(dom, None, None),
        P(every),
        P(every, None, None),
        P(every, None),
        P(every, None),
        P(every),
        P(),
        P(),
        P(),
        P(every, None),
    )
    return jax.shard_map(
        body,
        mesh=physical,
        in_specs=placed,
        out_specs=(P(every, None), P(every, None), P(), P(), P()),
        check_vma=False,
    )
```
